512 devices in a mesh: leaf: 128 (over y, z, core), col: 4 (over x).
Axes of the slice: x: 4, y: 4, z: 16, core: 2. Of those that a mesh axis runs over, the one named last changes fastest.
Arguments:
- leaf_rhs: float32 [114688, 512], P('leaf', 'col'), may hold values from -6 to 6
- leaf_inverse: float32 [896, 128, 128], P('leaf'), may hold values from -0.5 to 0.5
- leaf_blocks: float32 [2688, 128, 128], P('leaf'), may hold values from -0.1875 to 0.1875
- leaf_pattern: int32 [128, 21], P('leaf'), may hold values 0 or 1
- leaf_coupling: float32 [65536, 512], P('leaf'), may hold values from -0.0625 to 0.0625
- sep_rhs: float32 [22016, 512], P('leaf', 'col'), may hold values from -6 to 6
- sep_inverse: float32 [22016, 512], P('leaf', 'col'), may hold values from -0.25 to 0.25
- sep_coupling: float32 [21504, 512], P('leaf', 'col'), may hold values from -0.09375 to 0.09375
Outputs:
- leaf_solution: float32 [114688, 512], P('leaf', 'col')
- sep_solution: float32 [22016, 512], P('leaf', 'col')
The draws below stay inside these ranges and needn't reach their ends.
Inputs may be any that keep to these rules, and one draw needn't show every extreme that they name: `leaf_pattern`: 1 where a factor block below the diagonal is nonzero, 0 where it is zero.
All inputs are finite; a program needn't handle non-finite values.
Results may differ from the reference program's by a relative error of at most 0.00011.
Values sent between devices are 32-bit elements; how exact they have to be, the bound alone decides.
No kernel may reach another device: no remote copies, remote signals or barrier semaphores. Data moves between devices by JAX's collectives and lax.ppermute only.
A program may use at most 64 MiB of HBM per device.

```python
import jax
import jax.numpy as jnp
from jax import lax

BLK = 128
NB = 7
SEP = 512
NRHS = 512
LR = 896
NPAIR = 21
LEVELS = 4
SR = 172
VC = 168
N_LEAF = 128


def plant(entries, own_key, low, top_value):
    longest = entries.shape.index(max(entries.shape))
    spots = []
    for shift in (0, 1):
        where = [jax.random.randint(jax.random.fold_in(own_key, axis), (), 0, length) for axis, length in enumerate(entries.shape)]
        where[longest] = (where[longest] + shift) % entries.shape[longest]
        spots.append(tuple(where))
    return entries.at[spots[0]].set(low).at[spots[1]].set(top_value)


def shard_levels(key, shape, pieces, least, largest):
    level = 1.0
    for position, blocks in pieces:
        draws = jax.random.uniform(jax.random.fold_in(jax.random.fold_in(key, 6), position), (blocks,), jnp.float32, least / len(pieces), largest / len(pieces))
        level = level * jnp.repeat(jnp.exp(draws), shape[position] // blocks).reshape((-1,) + (1,) * (len(shape) - 1 - position))
    return level


def gaussian(own_key, dims, scale, most, cuts=(), kind=jnp.bfloat16):
    values = scale * jax.random.normal(own_key, dims, jnp.float32)
    if cuts:
        values = values * shard_levels(own_key, dims, cuts, -0.22, 0.18)
    return jnp.clip(values, -most, most).astype(kind)


def setup_inputs(seed: int = 0) -> dict:
    seeds = jax.random.split(jax.random.key(seed), 9)
    leaf_rhs = gaussian(seeds[0], (N_LEAF * LR, NRHS), 1.0, 6.0, ((0, 128), (1, 4)), jnp.float32)
    leaf_inverse = gaussian(seeds[1], (N_LEAF * NB, BLK, BLK), BLK ** -0.5, 0.5, ((0, 128),), jnp.float32)
    leaf_blocks = gaussian(seeds[2], (N_LEAF * NPAIR, BLK, BLK), (BLK * NB) ** -0.5, 0.1875, ((0, 128),), jnp.float32)
    leaf_pattern = plant((jax.random.randint(seeds[3], (N_LEAF, NPAIR), 0, 2) < 1).astype(jnp.int32), jax.random.fold_in(seeds[3], 1), 0, 1)
    leaf_coupling = gaussian(seeds[4], (N_LEAF * LEVELS * BLK, SEP), (64 * BLK) ** -0.5, 0.0625, ((0, 128),), jnp.float32)
    sep_rhs = gaussian(seeds[5], (N_LEAF * SR, NRHS), 1.0, 6.0, ((0, 128), (1, 4)), jnp.float32)
    sep_inverse = gaussian(seeds[6], (N_LEAF * SR, SEP), SEP ** -0.5, 0.25, ((0, 128), (1, 4)), jnp.float32)
    sep_coupling = gaussian(seeds[7], (N_LEAF * VC, SEP), (8 * SEP) ** -0.5, 0.09375, ((0, 128), (1, 4)), jnp.float32)
    return {"leaf_rhs": leaf_rhs, "leaf_inverse": leaf_inverse, "leaf_blocks": leaf_blocks, "leaf_pattern": leaf_pattern, "leaf_coupling": leaf_coupling, "sep_rhs": sep_rhs, "sep_inverse": sep_inverse, "sep_coupling": sep_coupling}


HIGH = lax.Precision.HIGHEST


def group_sizes(leaf_count):
    result = []
    for level_index in range(1, 5):
        group_span = 4 ** level_index
        if group_span // 4 < leaf_count:
            result.append(min(group_span, leaf_count))
    return result


def grouped(piece, group_size, leaf_count):
    return piece.reshape(leaf_count // group_size, group_size * piece.shape[1], piece.shape[2])


def reference(leaf_rhs, leaf_inverse, leaf_blocks, leaf_pattern, leaf_coupling, sep_rhs, sep_inverse, sep_coupling):
    leaf_count = N_LEAF
    block_count = NB
    block_rows = BLK
    sep_rows = SEP
    columns = NRHS
    rhs_blocks = leaf_rhs.reshape(leaf_count, block_count, block_rows, columns)
    inverse = leaf_inverse.reshape(leaf_count, block_count, block_rows, block_rows)
    weighted = leaf_blocks.reshape(leaf_count, -1, block_rows, block_rows) * leaf_pattern.astype(jnp.float32)[:, :, None, None]
    column_starts = []
    running = 0
    for column_index in range(block_count):
        column_starts.append(running)
        running = running + block_count - 1 - column_index
    pending = [rhs_blocks[:, i] for i in range(block_count)]
    forward = []
    for column_index in range(block_count):
        solved = jnp.einsum('nab,nbc->nac', inverse[:, column_index], pending[column_index], precision=HIGH)
        forward.append(solved)
        for later_index in range(column_index + 1, block_count):
            pair_index = column_starts[column_index] + later_index - column_index - 1
            pending[later_index] = pending[later_index] - jnp.einsum('nab,nbc->nac', weighted[:, pair_index], solved, precision=HIGH)
    sizes_list = group_sizes(leaf_count)
    level_total = len(sizes_list)
    row_counts = [sep_rows // size_item for size_item in sizes_list]
    offsets = []
    running = 0
    for row_count in row_counts:
        offsets.append(running)
        running = running + row_count
    sep_right = sep_rhs.reshape(leaf_count, -1, columns)
    sep_inv = sep_inverse.reshape(leaf_count, -1, sep_rows)
    sep_cpl = sep_coupling.reshape(leaf_count, -1, sep_rows)
    couple = leaf_coupling.reshape(leaf_count, level_total, block_rows, sep_rows)
    last_block = forward[-1]
    forward_levels = []
    for level_index in range(level_total):
        group_size = sizes_list[level_index]
        row_count = row_counts[level_index]
        row_offset = offsets[level_index]
        leaf_term = jnp.einsum('nks,nkc->nsc', couple[:, level_index], last_block, precision=HIGH)
        leaf_term = leaf_term.reshape(leaf_count // group_size, group_size, sep_rows, columns).sum(1)
        summed = grouped(sep_right[:, row_offset:row_offset + row_count], group_size, leaf_count) - leaf_term
        if level_index > 0:
            child_size = sizes_list[level_index - 1]
            child_count = row_counts[level_index - 1]
            child_offset = offsets[level_index - 1]
            child_matrix = grouped(sep_cpl[:, child_offset:child_offset + child_count], child_size, leaf_count)
            child_term = jnp.einsum('nrs,nrc->nsc', child_matrix, forward_levels[-1], precision=HIGH)
            summed = summed - child_term.reshape(leaf_count // group_size, group_size // child_size, sep_rows, columns).sum(1)
        diag_matrix = grouped(sep_inv[:, row_offset:row_offset + row_count], group_size, leaf_count)
        forward_levels.append(jnp.einsum('nsr,nrc->nsc', diag_matrix, summed, precision=HIGH))
    back_levels = [None] * level_total
    for level_index in reversed(range(level_total)):
        group_size = sizes_list[level_index]
        row_count = row_counts[level_index]
        row_offset = offsets[level_index]
        target = forward_levels[level_index]
        if level_index < level_total - 1:
            parent_size = sizes_list[level_index + 1]
            child_matrix = grouped(sep_cpl[:, row_offset:row_offset + row_count], group_size, leaf_count)
            parent_rep = jnp.repeat(back_levels[level_index + 1], parent_size // group_size, axis=0)
            target = target - jnp.einsum('nrs,nsc->nrc', child_matrix, parent_rep, precision=HIGH)
        diag_matrix = grouped(sep_inv[:, row_offset:row_offset + row_count], group_size, leaf_count)
        back_levels[level_index] = jnp.einsum('nsr,nsc->nrc', diag_matrix, target, precision=HIGH)
    correction = jnp.zeros((leaf_count, block_rows, columns), jnp.float32)
    for level_index in range(level_total):
        spread = jnp.repeat(back_levels[level_index], sizes_list[level_index], axis=0)
        correction = correction + jnp.einsum('nks,nsc->nkc', couple[:, level_index], spread, precision=HIGH)
    pending = list(forward)
    pending[-1] = pending[-1] - correction
    backward = [None] * block_count
    for column_index in reversed(range(block_count)):
        target = pending[column_index]
        for later_index in range(column_index + 1, block_count):
            pair_index = column_starts[column_index] + later_index - column_index - 1
            target = target - jnp.einsum('nab,nac->nbc', weighted[:, pair_index], backward[later_index], precision=HIGH)
        backward[column_index] = jnp.einsum('nab,nac->nbc', inverse[:, column_index], target, precision=HIGH)
    leaf_solution = jnp.stack(backward, axis=1).reshape(leaf_count * block_count * block_rows, columns)
    sep_pieces = [back_levels[i].reshape(leaf_count, row_counts[i], columns) for i in range(level_total)]
    sep_solution = jnp.concatenate(sep_pieces, axis=1).reshape(-1, columns)
    return leaf_solution, sep_solution
```

```python
import functools

import jax
import jax.numpy as jnp
from jax import lax
from jax.experimental import pallas as pl
from jax.experimental.pallas import tpu as pltpu
from jax.sharding import PartitionSpec as P

F32 = jnp.float32
BF16 = jnp.bfloat16
NN = (((1,), (0,)), ((), ()))
NT = (((1,), (1,)), ((), ()))
TN = (((0,), (0,)), ((), ()))
LEVELS = 4
CORE, Z1, Z2, Z4, Z8, Y1, Y2 = range(7)


def halves(value):
    high = value.astype(BF16)
    low = (value - high.astype(F32)).astype(BF16)
    return high, low


def mm(left, right, dims):
    left_high, left_low = halves(left)
    right_high, right_low = halves(right)
    dot = functools.partial(lax.dot_general, dimension_numbers=dims, preferred_element_type=F32)
    return dot(left_high, right_high) + (dot(left_high, right_low) + dot(left_low, right_high))


def exact(left, right, dims):
    return lax.dot_general(left, right, dims, precision=lax.Precision.HIGHEST, preferred_element_type=F32)


def swap(value, axis, mask):
    return lax.ppermute(value, axis, [(i, i ^ mask) for i in range(lax.axis_size(axis))])


def across(value, bit):
    return swap(value, "leaf", 1 << bit)


def grow(value, bit):
    return jnp.concatenate([value, across(value, bit)], axis=1)


def pair_starts(blocks):
    starts, running = [], 0
    for column in range(blocks):
        starts.append(running)
        running += blocks - 1 - column
    return starts


def placement(rows, offset, count, start, width):
    row = lax.broadcasted_iota(jnp.int32, (rows, width), 0)
    column = lax.broadcasted_iota(jnp.int32, (rows, width), 1)
    inside = (row >= offset) & (row < offset + count)
    return jnp.where(inside & (row - offset == column - start), 1.0, 0.0).astype(F32)


def forward_kernel(sizes, where, pattern, rhs, inverse, blocks, coupling, sep_rhs, y_out, t_out):
    count, size = inverse.shape[0], inverse.shape[1]
    starts = pair_starts(count)
    pending = [rhs[i * size : (i + 1) * size, :] for i in range(count)]
    for column in range(count):
        solved = mm(inverse[column], pending[column], NN)
        y_out[column * size : (column + 1) * size, :] = solved
        for later in range(column + 1, count):
            pair = starts[column] + later - column - 1
            weight = pattern[0, pair].astype(F32)
            pending[later] = pending[later] - weight * mm(blocks[pair], solved, NN)
    last = y_out[(count - 1) * size :, :]
    right = sep_rhs[...]
    width = coupling.shape[1]
    offset = 0
    for level, rows in enumerate(sizes):
        spread = placement(right.shape[0], offset, rows, where[level], width)
        offset += rows
        t_out[:, level * width : (level + 1) * width] = exact(right, spread, TN) - mm(
            last, coupling[level * size : (level + 1) * size, :], TN
        )


def backward_kernel(sizes, where, pattern, y, x, inverse, blocks, coupling, out, sep_out):
    count, size = inverse.shape[0], inverse.shape[1]
    starts = pair_starts(count)
    width = coupling.shape[1]
    place = where[LEVELS]
    quarter = x.shape[0]
    xs = jnp.concatenate([x[jnp.bitwise_xor(place, q)] for q in range(quarter)], axis=0)
    correction = jnp.zeros((size, y.shape[1]), F32)
    pieces = jnp.zeros((sep_out.shape[0], y.shape[1]), F32)
    offset = 0
    for level, rows in enumerate(sizes):
        part = xs[:, level * width : (level + 1) * width]
        correction = correction + mm(coupling[level * size : (level + 1) * size, :], part, NT)
        spread = placement(sep_out.shape[0], offset, rows, where[level], width)
        pieces = pieces + exact(spread, part, NT)
        offset += rows
    sep_out[...] = pieces
    pending = [y[i * size : (i + 1) * size, :] for i in range(count)]
    pending[-1] = pending[-1] - correction
    for column in reversed(range(count)):
        solved = mm(inverse[column], pending[column], TN)
        out[column * size : (column + 1) * size, :] = solved
        for earlier in reversed(range(column)):
            pair = starts[earlier] + column - earlier - 1
            weight = pattern[0, pair].astype(F32)
            pending[earlier] = pending[earlier] - weight * mm(blocks[pair], solved, TN)


def spans(plane, count):
    return [pl.ds(pl.multiple_of(jnp.bitwise_xor(plane, r) * 128, 128), 128) for r in range(count)]


def times_rows(value, spots, mats):
    result = []
    for half in mats:
        total = None
        for spot, block in zip(spots, half):
            term = mm(value[:, spot], block[0], NT)
            total = term if total is None else total + term
        result.append(total)
    return result


def times_matrix(value, mats, r):
    total = None
    for piece, half in zip(value, mats):
        term = mm(piece, half[r][0], NN)
        total = term if total is None else total + term
    return total


def split(refs, count):
    per = 2 * count
    return [[refs[i * per + h * count : i * per + (h + 1) * count] for h in range(2)] for i in range(len(refs) // per)]


def level_kernel(count, plane, right, base, *refs):
    mats, (z_out, v_out) = refs[:-2], refs[-2:]
    diagonal, below = split(mats, count)
    spots = spans(plane[0], count)
    z = times_rows(right, spots, diagonal)
    z_out[...] = jnp.concatenate(z, axis=1)
    for r, spot in enumerate(spots):
        v_out[:, spot] = base[:, spot] - times_matrix(z, below, r)


def top_kernel(count, plane, right, z1, z2, z3, *refs):
    mats, x_out = refs[:-1], refs[-1]
    d4, d3, c3, d2, c2, d1, c1 = split(mats, count)
    width = right.shape[1]
    spots = spans(plane[0], count)
    z = times_rows(right, spots, d4)
    level = 3
    order = [(z3, d3, c3), (z2, d2, c2), (z1, d1, c1)]
    diagonal = d4
    while True:
        places = [pl.ds(pl.multiple_of(level * width + jnp.bitwise_xor(plane[0], r) * 128, 128), 128) for r in range(count)]
        for r, place in enumerate(places):
            x_out[:, place] = times_matrix(z, diagonal, r)
        if not order:
            break
        held, diagonal, below = order.pop(0)
        moved = times_rows(x_out, places, below)
        half = held.shape[1] // 2
        z = [held[:, :half] - moved[0], held[:, half:] - moved[1]]
        level -= 1


SMEM = pl.BlockSpec(memory_space=pltpu.SMEM)
VMEM = pl.BlockSpec(memory_space=pltpu.VMEM)


def params():
    return pltpu.CompilerParams(vmem_limit_bytes=40 * 1024 * 1024)


def mat_specs(gathered, index):
    rows = gathered[0].shape[1]
    spec = pl.BlockSpec((1, rows, 128), lambda step: (index, 0, 0))
    return [spec] * len(gathered), list(gathered)


def with_mats(kernel, plane, small, mats, outs):
    specs, arrays = [], []
    for gathered, index in mats:
        more, given = mat_specs(gathered, index)
        specs += more
        arrays += given
    whole = [pl.BlockSpec(v.shape, lambda step: (0, 0)) for v in small]
    return pl.pallas_call(
        kernel,
        grid=(1,),
        out_shape=[jax.ShapeDtypeStruct(s, F32) for s in outs],
        in_specs=[SMEM] + whole + specs,
        out_specs=[pl.BlockSpec(s, lambda step: (0, 0)) for s in outs],
        compiler_params=params(),
    )(plane, *small, *arrays)


def over_col(value):
    return [value] + [swap(value, "col", r) for r in range(1, lax.axis_size("col"))]


def gathered(value):
    mine = over_col(value)
    return mine + [across(v, CORE) for v in mine]


def shards(leaf_rhs, leaf_inverse, leaf_blocks, leaf_pattern, leaf_coupling, sep_rhs, sep_inverse, sep_coupling):
    position = lax.axis_index("leaf")
    planes = lax.axis_size("col")
    columns = leaf_rhs.shape[1]
    width = leaf_coupling.shape[1]
    groups = [4, 16, 64, 128]
    sizes = [width // g for g in groups]
    offsets = [sum(sizes[:i]) for i in range(LEVELS)]
    where = jnp.stack([position % g * r for g, r in zip(groups, sizes)] + [position % 4]).astype(jnp.int32)
    plane = lax.axis_index("col").astype(jnp.int32)[None]

    def rows(array, level):
        return array[offsets[level] : offsets[level] + sizes[level]][None]

    def both(level):
        return jnp.concatenate([rows(sep_inverse, level), rows(sep_coupling, level)], 0)

    first = gathered(grow(both(0), Z1))
    far = grow(rows(sep_inverse, 3), Y2)
    far = grow(jnp.concatenate([far, both(2)], 0), Y1)
    far = grow(far, Z8)
    far = grow(jnp.concatenate([far, both(1)], 0), Z4)
    far = gathered(grow(grow(far, Z2), Z1))

    padded = jnp.pad(sep_rhs, ((0, 4), (0, 0)))
    y, t = pl.pallas_call(
        functools.partial(forward_kernel, sizes),
        out_shape=[
            jax.ShapeDtypeStruct(leaf_rhs.shape, F32),
            jax.ShapeDtypeStruct((columns, LEVELS * width), F32),
        ],
        in_specs=[SMEM, SMEM] + [VMEM] * 5,
        out_specs=[VMEM, VMEM],
        compiler_params=params(),
    )(where, leaf_pattern, leaf_rhs, leaf_inverse, leaf_blocks, leaf_coupling, padded)

    near = [[g * 4 + m for m in range(4)] for g in range(lax.axis_size("leaf") // 4)]
    t = lax.all_to_all(t, "leaf", 0, 0, axis_index_groups=near, tiled=True)
    t = t.reshape(4, columns // 4, LEVELS * width).sum(0)
    t1, t2, t3, t4 = [t[:, i * width : (i + 1) * width] for i in range(LEVELS)]

    def total(value, bits):
        for bit in bits:
            value = value + across(value, bit)
        return value

    shape = t1.shape
    upper = total(jnp.concatenate([t3, t4], 1), (Z2, Z4))
    t3, t4 = upper[:, :width], upper[:, width:]
    t4 = total(t4, (Z8, Y1))
    level = functools.partial(level_kernel, planes)
    z1, v = with_mats(level, plane, [t1, t2], [(first, 0), (first, 1)], [shape] * 2)
    v = total(v, (Z2, Z4))
    z2, v = with_mats(level, plane, [v, t3], [(far, 3), (far, 4)], [shape] * 2)
    v = total(v, (Z8, Y1))
    z3, v = with_mats(level, plane, [v, t4], [(far, 1), (far, 2)], [shape] * 2)
    v = total(v, (Y2,))
    (x,) = with_mats(
        functools.partial(top_kernel, planes),
        plane,
        [v, z1, z2, z3],
        [(far, 0), (far, 1), (far, 2), (far, 3), (far, 4), (first, 0), (first, 1)],
        [(shape[0], LEVELS * width)],
    )
    x = grow(x[None, None], Z1)[0]
    other = across(x, CORE)
    x = jnp.stack([x[0], other[0], x[1], other[1]], 0)

    return pl.pallas_call(
        functools.partial(backward_kernel, sizes),
        out_shape=[jax.ShapeDtypeStruct(leaf_rhs.shape, F32), jax.ShapeDtypeStruct(padded.shape, F32)],
        in_specs=[SMEM, SMEM] + [VMEM] * 5,
        out_specs=[VMEM, VMEM],
        compiler_params=params(),
    )(where, leaf_pattern, y, x, leaf_inverse, leaf_blocks, leaf_coupling)


def program(*arrays):
    leaf, sep = shards(*arrays)
    return leaf, sep[: arrays[5].shape[0]]


def solution(mesh):
    return jax.shard_map(
        program,
        mesh=mesh,
        in_specs=(
            P("leaf", "col"),
            P("leaf", None, None),
            P("leaf", None, None),
            P("leaf", None),
            P("leaf", None),
            P("leaf", "col"),
            P("leaf", "col"),
            P("leaf", "col"),
        ),
        out_specs=(P("leaf", "col"), P("leaf", "col")),
        check_vma=False,
    )
```

```python
import functools

import jax
import jax.numpy as jnp
from jax import lax
from jax.experimental import pallas as pl
from jax.experimental.pallas import tpu as pltpu
from jax.sharding import PartitionSpec as P

F32 = jnp.float32
BF16 = jnp.bfloat16
NN = (((1,), (0,)), ((), ()))
NT = (((1,), (1,)), ((), ()))
TN = (((0,), (0,)), ((), ()))
LEVELS = 4
Z1, Z2, Z4, Z8, Y1, Y2 = range(1, 7)
CORE_MASK = 1


def halves(value):
    high = value.astype(BF16)
    low = (value - high.astype(F32)).astype(BF16)
    return high, low


def mm(left, right, dims):
    left_high, left_low = halves(left)
    right_high, right_low = halves(right)
    dot = functools.partial(lax.dot_general, dimension_numbers=dims, preferred_element_type=F32)
    return dot(left_high, right_high) + (dot(left_high, right_low) + dot(left_low, right_high))


def exact(left, right, dims):
    return lax.dot_general(left, right, dims, precision=lax.Precision.HIGHEST, preferred_element_type=F32)


def swap(value, axis, mask):
    return lax.ppermute(value, axis, [(i, i ^ mask) for i in range(lax.axis_size(axis))])


def across(value, mask):
    return swap(value, "leaf", mask)


def grow(value, mask):
    return jnp.concatenate([value, across(value, mask)], axis=1)


def pair_starts(blocks):
    starts, running = [], 0
    for column in range(blocks):
        starts.append(running)
        running += blocks - 1 - column
    return starts


def placement(rows, offset, count, start, width):
    row = lax.broadcasted_iota(jnp.int32, (rows, width), 0)
    column = lax.broadcasted_iota(jnp.int32, (rows, width), 1)
    inside = (row >= offset) & (row < offset + count)
    return jnp.where(inside & (row - offset == column - start), 1.0, 0.0).astype(F32)


def forward_kernel(sizes, where, pattern, rhs, inverse, blocks, coupling, sep_rhs, y_out, t_out):
    count, size = inverse.shape[0], inverse.shape[1]
    starts = pair_starts(count)
    pending = [rhs[i * size : (i + 1) * size, :] for i in range(count)]
    for column in range(count):
        solved = mm(inverse[column], pending[column], NN)
        y_out[column * size : (column + 1) * size, :] = solved
        for later in range(column + 1, count):
            pair = starts[column] + later - column - 1
            weight = pattern[0, pair].astype(F32)
            pending[later] = pending[later] - weight * mm(blocks[pair], solved, NN)
    last = y_out[(count - 1) * size :, :]
    right = sep_rhs[...]
    width = coupling.shape[1]
    offset = 0
    for level, rows in enumerate(sizes):
        spread = placement(right.shape[0], offset, rows, where[level], width)
        offset += rows
        t_out[:, level * width : (level + 1) * width] = exact(right, spread, TN) - mm(
            last, coupling[level * size : (level + 1) * size, :], TN
        )


def backward_kernel(sizes, where, pattern, y, x, inverse, blocks, coupling, out, sep_out):
    count, size = inverse.shape[0], inverse.shape[1]
    starts = pair_starts(count)
    width = coupling.shape[1]
    place = where[LEVELS]
    quarter = x.shape[0]
    xs = jnp.concatenate([x[jnp.bitwise_xor(place, q)] for q in range(quarter)], axis=0)
    correction = jnp.zeros((size, y.shape[1]), F32)
    pieces = jnp.zeros((sep_out.shape[0], y.shape[1]), F32)
    offset = 0
    for level, rows in enumerate(sizes):
        part = xs[:, level * width : (level + 1) * width]
        correction = correction + mm(coupling[level * size : (level + 1) * size, :], part, NT)
        spread = placement(sep_out.shape[0], offset, rows, where[level], width)
        pieces = pieces + exact(spread, part, NT)
        offset += rows
    sep_out[...] = pieces
    pending = [y[i * size : (i + 1) * size, :] for i in range(count)]
    pending[-1] = pending[-1] - correction
    for column in reversed(range(count)):
        solved = mm(inverse[column], pending[column], TN)
        out[column * size : (column + 1) * size, :] = solved
        for earlier in reversed(range(column)):
            pair = starts[earlier] + column - earlier - 1
            weight = pattern[0, pair].astype(F32)
            pending[earlier] = pending[earlier] - weight * mm(blocks[pair], solved, TN)


def times_rows(value, mats, index):
    result = []
    for half in mats:
        total = None
        for r in range(half.shape[0]):
            term = mm(value[:, r * 128 : (r + 1) * 128], half[r, index], NT)
            total = term if total is None else total + term
        result.append(total)
    return result


def times_matrix(value, mats, index, r):
    total = None
    for piece, half in zip(value, mats):
        term = mm(piece, half[r, index], NN)
        total = term if total is None else total + term
    return total


def level_kernel(index, right, base, mine, other, z_out, v_out):
    mats = (mine, other)
    z = times_rows(right, mats, index)
    z_out[...] = jnp.concatenate(z, axis=1)
    for r in range(mine.shape[0]):
        spot = slice(r * 128, (r + 1) * 128)
        v_out[:, spot] = base[:, spot] - times_matrix(z, mats, index + 1, r)


def top_kernel(right, z1, z2, z3, m1, o1, m2, o2, m3, o3, x_out):
    width = right.shape[1]
    top = (m3, o3)
    z = times_rows(right, top, 0)
    order = [(z3, top, 1), (z2, (m2, o2), 0), (z1, (m1, o1), 0)]
    mats, index = top, 0
    level = 3
    while True:
        for r in range(mats[0].shape[0]):
            start = level * width + r * 128
            x_out[:, start : start + 128] = times_matrix(z, mats, index, r)
        if not order:
            break
        held, mats, index = order.pop(0)
        moved = times_rows(x_out[:, level * width : (level + 1) * width], mats, index + 1)
        half = held.shape[1] // 2
        z = [held[:, :half] - moved[0], held[:, half:] - moved[1]]
        level -= 1


SMEM = pl.BlockSpec(memory_space=pltpu.SMEM)
VMEM = pl.BlockSpec(memory_space=pltpu.VMEM)


def params():
    return pltpu.CompilerParams(vmem_limit_bytes=40 * 1024 * 1024)


def call(kernel, outs, *arrays):
    return pl.pallas_call(
        kernel,
        out_shape=[jax.ShapeDtypeStruct(s, F32) for s in outs],
        in_specs=[SMEM if v.dtype == jnp.int32 else VMEM for v in arrays],
        out_specs=[VMEM] * len(outs),
        compiler_params=params(),
    )(*arrays)


def shards(leaf_rhs, leaf_inverse, leaf_blocks, leaf_pattern, leaf_coupling, sep_rhs, sep_inverse, sep_coupling):
    position = lax.axis_index("leaf")
    columns = leaf_rhs.shape[1]
    width = leaf_coupling.shape[1]
    leaves = lax.axis_size("leaf")
    groups = [4, 16, 64, 128]
    sizes = [width // g for g in groups]
    offsets = [sum(sizes[:i]) for i in range(LEVELS)]
    where = jnp.stack([position % g * r for g, r in zip(groups, sizes)] + [position % 4]).astype(jnp.int32)

    def rows(array, level):
        return array[offsets[level] : offsets[level] + sizes[level]]

    def both(level):
        return jnp.stack([rows(sep_inverse, level), rows(sep_coupling, level)])

    count = leaves // 4
    far = jnp.concatenate([rows(sep_inverse, 2), rows(sep_coupling, 2), rows(sep_inverse, 3)], 0)
    far = jnp.broadcast_to(far[None], (count, *far.shape))
    apart = [[m + 4 * k for k in range(count)] for m in range(4)]
    far = lax.all_to_all(far, "leaf", 0, 0, axis_index_groups=apart, tiled=True)

    first = grow(both(0), 1 << Z1)
    second = grow(both(1), 1 << Z4)
    padded = jnp.pad(sep_rhs, ((0, 4), (0, 0)))
    where, first, second = lax.optimization_barrier((where, first, second))
    y, t = call(
        functools.partial(forward_kernel, sizes),
        [leaf_rhs.shape, (columns, LEVELS * width)],
        where, leaf_pattern, leaf_rhs, leaf_inverse, leaf_blocks, leaf_coupling, padded,
    )
    first = lax.all_gather(first, "col", axis=0)
    near = [[g * 4 + m for m in range(4)] for g in range(leaves // 4)]
    second = grow(second, 1 << Z2)
    far, second, t = lax.optimization_barrier((far, second, t))
    t = lax.all_to_all(t, "leaf", 0, 0, axis_index_groups=near, tiled=True)
    t = t.reshape(4, columns // 4, LEVELS * width).sum(0)
    upper = t[:, 2 * width :]
    upper = upper + across(upper, 1 << Z2)
    first, upper = lax.optimization_barrier((first, upper))
    upper = upper + across(upper, 1 << Z4)
    first = (first, across(first, CORE_MASK))
    second = lax.all_gather(grow(second, 1 << Z1), "col", axis=0)
    own = lax.dynamic_slice_in_dim(far, position // 64 * 16, 16, 0)
    third = [
        far[:, 2 * sizes[2] :].reshape(-1, 128),
        own[:, : sizes[2]].reshape(-1, 128),
        own[:, sizes[2] : 2 * sizes[2]].reshape(-1, 128),
    ]
    third = lax.all_gather(grow(jnp.stack(third), 1 << Z1), "col", axis=0)

    t1, t2 = t[:, :width], t[:, width : 2 * width]
    t3, t4 = upper[:, :width], upper[:, width:]

    def total(value, *masks):
        for mask in masks:
            value = value + across(value, mask)
        return value

    shape = t1.shape
    halves_z, wrap_z, wrap_y = 1 << Z4, (1 << Z8) | (1 << Z4) | (1 << Z2), (1 << Y2) | (1 << Y1)
    t4 = total(t4, wrap_z, 1 << Y1)
    z1, v = call(functools.partial(level_kernel, 0), [shape] * 2, t1, t2, *first)
    v = total(v, 1 << Z2)
    v, second = lax.optimization_barrier((v, second))
    second = (second, across(second, CORE_MASK))
    v = total(v, halves_z)
    z2, v = call(functools.partial(level_kernel, 0), [shape] * 2, v, t3, *second)
    v, third = lax.optimization_barrier((v, third))
    third = (third, across(third, CORE_MASK))
    v = total(v, wrap_z, 1 << Y1)
    z3, v = call(functools.partial(level_kernel, 1), [shape] * 2, v, t4, *third)
    v = total(v, wrap_y)
    (x,) = call(top_kernel, [(shape[0], LEVELS * width)], v, z1, z2, z3, *first, *second, *third)
    x = jnp.stack([x, across(x, 1 << Z1)])
    other = across(x, CORE_MASK)
    x = jnp.stack([x[0], other[0], x[1], other[1]], 0)
    return call(
        functools.partial(backward_kernel, sizes),
        [leaf_rhs.shape, padded.shape],
        where, leaf_pattern, y, x, leaf_inverse, leaf_blocks, leaf_coupling,
    )


def program(*arrays):
    leaf, sep = shards(*arrays)
    return leaf, sep[: arrays[5].shape[0]]


def solution(mesh):
    return jax.shard_map(
        program,
        mesh=mesh,
        in_specs=(
            P("leaf", "col"),
            P("leaf", None, None),
            P("leaf", None, None),
            P("leaf", None),
            P("leaf", None),
            P("leaf", "col"),
            P("leaf", "col"),
            P("leaf", "col"),
        ),
        out_specs=(P("leaf", "col"), P("leaf", "col")),
        check_vma=False,
    )
```

```python
import functools

import jax
import jax.numpy as jnp
from jax import lax
from jax.experimental import pallas as pl
from jax.experimental.pallas import tpu as pltpu
from jax.sharding import PartitionSpec as P

F32 = jnp.float32
BF16 = jnp.bfloat16
NN = (((1,), (0,)), ((), ()))
NT = (((1,), (1,)), ((), ()))
TN = (((0,), (0,)), ((), ()))
LEVELS = 4
Z1, Z2, Z4, Z8, Y1, Y2 = range(1, 7)
CORE_MASK = 1


def halves(value):
    high = value.astype(BF16)
    low = (value - high.astype(F32)).astype(BF16)
    return high, low


def mm(left, right, dims):
    left_high, left_low = halves(left)
    right_high, right_low = halves(right)
    dot = functools.partial(lax.dot_general, dimension_numbers=dims, preferred_element_type=F32)
    return dot(left_high, right_high) + (dot(left_high, right_low) + dot(left_low, right_high))


def exact(left, right, dims):
    return lax.dot_general(left, right, dims, precision=lax.Precision.HIGHEST, preferred_element_type=F32)


def swap(value, axis, mask):
    return lax.ppermute(value, axis, [(i, i ^ mask) for i in range(lax.axis_size(axis))])


def across(value, mask):
    return swap(value, "leaf", mask)


def grow(value, mask):
    return jnp.concatenate([value, across(value, mask)], axis=1)


def pair_starts(blocks):
    starts, running = [], 0
    for column in range(blocks):
        starts.append(running)
        running += blocks - 1 - column
    return starts


def placement(rows, offset, count, start, width):
    row = lax.broadcasted_iota(jnp.int32, (rows, width), 0)
    column = lax.broadcasted_iota(jnp.int32, (rows, width), 1)
    inside = (row >= offset) & (row < offset + count)
    return jnp.where(inside & (row - offset == column - start), 1.0, 0.0).astype(F32)


def forward_kernel(sizes, where, pattern, rhs, inverse, blocks, coupling, sep_rhs, y_out, t_out):
    count, size = inverse.shape[0], inverse.shape[1]
    starts = pair_starts(count)
    pending = [rhs[i * size : (i + 1) * size, :] for i in range(count)]
    for column in range(count):
        solved = mm(inverse[column], pending[column], NN)
        y_out[column * size : (column + 1) * size, :] = solved
        for later in range(column + 1, count):
            pair = starts[column] + later - column - 1
            weight = pattern[0, pair].astype(F32)
            pending[later] = pending[later] - weight * mm(blocks[pair], solved, NN)
    last = y_out[(count - 1) * size :, :]
    right = sep_rhs[...]
    width = coupling.shape[1]
    offset = 0
    for level, rows in enumerate(sizes):
        spread = placement(right.shape[0], offset, rows, where[level], width)
        offset += rows
        t_out[:, level * width : (level + 1) * width] = exact(right, spread, TN) - mm(
            last, coupling[level * size : (level + 1) * size, :], TN
        )


def backward_kernel(sizes, where, pattern, y, x, inverse, blocks, coupling, out, sep_out):
    count, size = inverse.shape[0], inverse.shape[1]
    starts = pair_starts(count)
    width = coupling.shape[1]
    place = where[LEVELS]
    quarter = x.shape[0]
    xs = jnp.concatenate([x[jnp.bitwise_xor(place, q)] for q in range(quarter)], axis=0)
    correction = jnp.zeros((size, y.shape[1]), F32)
    pieces = jnp.zeros((sep_out.shape[0], y.shape[1]), F32)
    offset = 0
    for level, rows in enumerate(sizes):
        part = xs[:, level * width : (level + 1) * width]
        correction = correction + mm(coupling[level * size : (level + 1) * size, :], part, NT)
        spread = placement(sep_out.shape[0], offset, rows, where[level], width)
        pieces = pieces + exact(spread, part, NT)
        offset += rows
    sep_out[...] = pieces
    pending = [y[i * size : (i + 1) * size, :] for i in range(count)]
    pending[-1] = pending[-1] - correction
    for column in reversed(range(count)):
        solved = mm(inverse[column], pending[column], TN)
        out[column * size : (column + 1) * size, :] = solved
        for earlier in reversed(range(column)):
            pair = starts[earlier] + column - earlier - 1
            weight = pattern[0, pair].astype(F32)
            pending[earlier] = pending[earlier] - weight * mm(blocks[pair], solved, TN)


def spots(start, plane, count):
    return [pl.ds(pl.multiple_of(start + (plane ^ r) * 128, 128), 128) for r in range(count)]


def times_rows(value, places, mats, index):
    result = []
    for half in mats:
        total = None
        for r, place in enumerate(places):
            term = mm(value[:, place], half[r, index], NT)
            total = term if total is None else total + term
        result.append(total)
    return result


def times_matrix(value, mats, index, r):
    total = None
    for piece, half in zip(value, mats):
        term = mm(piece, half[r, index], NN)
        total = term if total is None else total + term
    return total


def level_kernel(index, plane, right, base, mine, other, z_out, v_out):
    mats = (mine, other)
    places = spots(0, plane[0], mine.shape[0])
    z = times_rows(right, places, mats, index)
    z_out[...] = jnp.concatenate(z, axis=1)
    for r, place in enumerate(places):
        v_out[:, place] = base[:, place] - times_matrix(z, mats, index + 1, r)


def top_kernel(plane, right, z1, z2, z3, m1, o1, m2, o2, m3, o3, x_out):
    width = right.shape[1]
    count = m3.shape[0]
    top = (m3, o3)
    z = times_rows(right, spots(0, 0, count), top, 0)
    order = [(z3, top, 1, 0), (z2, (m2, o2), 0, plane[0]), (z1, (m1, o1), 0, plane[0])]
    mats, index, turn = top, 0, 0
    level = 3
    while True:
        for r, place in enumerate(spots(level * width, turn, count)):
            x_out[:, place] = times_matrix(z, mats, index, r)
        if not order:
            break
        held, mats, index, turn = order.pop(0)
        moved = times_rows(x_out, spots(level * width, turn, count), mats, index + 1)
        half = held.shape[1] // 2
        z = [held[:, :half] - moved[0], held[:, half:] - moved[1]]
        level -= 1


SMEM = pl.BlockSpec(memory_space=pltpu.SMEM)
VMEM = pl.BlockSpec(memory_space=pltpu.VMEM)


def params():
    return pltpu.CompilerParams(vmem_limit_bytes=40 * 1024 * 1024)


def call(kernel, outs, *arrays):
    return pl.pallas_call(
        kernel,
        out_shape=[jax.ShapeDtypeStruct(s, F32) for s in outs],
        in_specs=[SMEM if v.dtype == jnp.int32 else VMEM for v in arrays],
        out_specs=[VMEM] * len(outs),
        compiler_params=params(),
    )(*arrays)


def shards(leaf_rhs, leaf_inverse, leaf_blocks, leaf_pattern, leaf_coupling, sep_rhs, sep_inverse, sep_coupling):
    position = lax.axis_index("leaf")
    columns = leaf_rhs.shape[1]
    width = leaf_coupling.shape[1]
    leaves = lax.axis_size("leaf")
    groups = [4, 16, 64, 128]
    sizes = [width // g for g in groups]
    offsets = [sum(sizes[:i]) for i in range(LEVELS)]
    where = jnp.stack([position % g * r for g, r in zip(groups, sizes)] + [position % 4]).astype(jnp.int32)

    plane = lax.axis_index("col").astype(jnp.int32)[None]

    def rows(array, level):
        return array[offsets[level] : offsets[level] + sizes[level]]

    def both(level):
        return jnp.stack([rows(sep_inverse, level), rows(sep_coupling, level)])

    def planes(value):
        return jnp.stack([value] + [swap(value, "col", r) for r in range(1, lax.axis_size("col"))])

    tie = lax.optimization_barrier
    halves_z, wrap_z, wrap_y = 1 << Z4, (1 << Z8) | (1 << Z4) | (1 << Z2), (1 << Y2) | (1 << Y1)

    padded = jnp.pad(sep_rhs, ((0, 4), (0, 0)))
    first, second = both(0), both(1)
    far = jnp.concatenate([rows(sep_inverse, 2), rows(sep_coupling, 2), rows(sep_inverse, 3)], 0)
    first = grow(first, 1 << Z1)
    y, t = call(
        functools.partial(forward_kernel, sizes),
        [leaf_rhs.shape, (columns, LEVELS * width)],
        where, leaf_pattern, leaf_rhs, leaf_inverse, leaf_blocks, leaf_coupling, padded,
    )
    t, first, second, far = tie((t, first, second, far))

    near = [[g * 4 + m for m in range(4)] for g in range(leaves // 4)]
    t = lax.all_to_all(t, "leaf", 0, 0, axis_index_groups=near, tiled=True)
    first = planes(first)
    second = grow(second, halves_z)
    t, first, second, far = tie((t, first, second, far))

    count = leaves // 4
    far = jnp.broadcast_to(far[None], (count, *far.shape))
    apart = [[m + 4 * k for k in range(count)] for m in range(4)]
    far = lax.all_to_all(far, "leaf", 0, 0, axis_index_groups=apart, tiled=True)
    t = t.reshape(4, columns // 4, LEVELS * width).sum(0)
    t1, t2, upper = t[:, :width], t[:, width : 2 * width], t[:, 2 * width :]
    first = (first, across(first, CORE_MASK))
    second = grow(second, 1 << Z2)
    upper_z2 = across(upper, 1 << Z2)
    shape = t1.shape
    z1, v = call(functools.partial(level_kernel, 0), [shape] * 2, plane, t1, t2, *first)
    v, second, upper, upper_z2 = tie((v, second, upper, upper_z2))

    upper = upper + upper_z2
    second = grow(second, 1 << Z1)
    upper_z4 = across(upper, halves_z)
    v = v + across(v, 1 << Z2)
    v, second, far = tie((v, second, far))

    own = lax.dynamic_slice_in_dim(far, position // 64 * 16, 16, 0)
    third = jnp.stack([
        far[:, 2 * sizes[2] :].reshape(-1, 128),
        own[:, : sizes[2]].reshape(-1, 128),
        own[:, sizes[2] : 2 * sizes[2]].reshape(-1, 128),
    ])
    second = planes(second)
    third = grow(third, 1 << Z1)
    v = v + across(v, halves_z)
    v, second, third, upper, upper_z4 = tie((v, second, third, upper, upper_z4))

    third = lax.all_gather(third, "col", axis=0)
    second = (second, across(second, CORE_MASK))
    upper = upper + upper_z4
    t3, t4 = upper[:, :width], upper[:, width:]
    t4_far = across(t4, wrap_z)
    z2, v = call(functools.partial(level_kernel, 0), [shape] * 2, plane, v, t3, *second)
    v, t4, t4_far = tie((v, t4, t4_far))

    t4 = t4 + t4_far
    t4_y = across(t4, 1 << Y1)
    v = v + across(v, wrap_z)
    v, t4, t4_y, third = tie((v, t4, t4_y, third))
    third = (third, across(third, CORE_MASK))
    v = v + across(v, 1 << Y1)
    z3, v = call(functools.partial(level_kernel, 1), [shape] * 2, plane * 0, v, t4 + t4_y, *third)
    v = v + across(v, wrap_y)
    (x,) = call(top_kernel, [(shape[0], LEVELS * width)], plane, v, z1, z2, z3, *first, *second, *third)
    x = jnp.stack([x, across(x, 1 << Z1)])
    other = across(x, CORE_MASK)
    x = jnp.stack([x[0], other[0], x[1], other[1]], 0)
    return call(
        functools.partial(backward_kernel, sizes),
        [leaf_rhs.shape, padded.shape],
        where, leaf_pattern, y, x, leaf_inverse, leaf_blocks, leaf_coupling,
    )


def program(*arrays):
    leaf, sep = shards(*arrays)
    return leaf, sep[: arrays[5].shape[0]]


def solution(mesh):
    return jax.shard_map(
        program,
        mesh=mesh,
        in_specs=(
            P("leaf", "col"),
            P("leaf", None, None),
            P("leaf", None, None),
            P("leaf", None),
            P("leaf", None),
            P("leaf", "col"),
            P("leaf", "col"),
            P("leaf", "col"),
        ),
        out_specs=(P("leaf", "col"), P("leaf", "col")),
        check_vma=False,
    )
```

```python
import functools

import jax
import jax.numpy as jnp
from jax import lax
from jax.experimental import pallas as pl
from jax.experimental.pallas import tpu as pltpu
from jax.sharding import PartitionSpec as P

F32 = jnp.float32
BF16 = jnp.bfloat16
NN = (((1,), (0,)), ((), ()))
NT = (((1,), (1,)), ((), ()))
TN = (((0,), (0,)), ((), ()))
LEVELS = 4
Z1, Z2, Z4, Z8, Y1, Y2 = range(1, 7)
CORE_MASK = 1


def halves(value):
    high = value.astype(BF16)
    low = (value - high.astype(F32)).astype(BF16)
    return high, low


def mm(left, right, dims):
    left_high, left_low = halves(left)
    right_high, right_low = halves(right)
    dot = functools.partial(lax.dot_general, dimension_numbers=dims, preferred_element_type=F32)
    return dot(left_high, right_high) + (dot(left_high, right_low) + dot(left_low, right_high))


def pick_left(spread, value, dims):
    high, low = halves(value)
    rest = (value - high.astype(F32) - low.astype(F32)).astype(BF16)
    dot = functools.partial(lax.dot_general, spread, dimension_numbers=dims, preferred_element_type=F32)
    return dot(high) + (dot(low) + dot(rest))


def pick_right(value, spread, dims):
    high, low = halves(value)
    rest = (value - high.astype(F32) - low.astype(F32)).astype(BF16)
    dot = functools.partial(lax.dot_general, dimension_numbers=dims, preferred_element_type=F32)
    return dot(high, spread) + (dot(low, spread) + dot(rest, spread))


def swap(value, axis, mask):
    return lax.ppermute(value, axis, [(i, i ^ mask) for i in range(lax.axis_size(axis))])


def across(value, mask):
    return swap(value, "leaf", mask)


def grow(value, mask):
    return jnp.concatenate([value, across(value, mask)], axis=1)


def pair_starts(blocks):
    starts, running = [], 0
    for column in range(blocks):
        starts.append(running)
        running += blocks - 1 - column
    return starts


def placement(rows, offset, count, start, width):
    row = lax.broadcasted_iota(jnp.int32, (rows, width), 0)
    column = lax.broadcasted_iota(jnp.int32, (rows, width), 1)
    inside = (row >= offset) & (row < offset + count)
    return jnp.where(inside & (row - offset == column - start), 1.0, 0.0).astype(BF16)


def forward_kernel(sizes, where, pattern, rhs, inverse, blocks, coupling, sep_rhs, y_out, t_out):
    count, size = inverse.shape[0], inverse.shape[1]
    starts = pair_starts(count)
    pending = [rhs[i * size : (i + 1) * size, :] for i in range(count)]
    for column in range(count):
        solved = mm(inverse[column], pending[column], NN)
        y_out[column * size : (column + 1) * size, :] = solved
        for later in range(column + 1, count):
            pair = starts[column] + later - column - 1
            weight = pattern[0, pair].astype(F32)
            pending[later] = pending[later] - weight * mm(blocks[pair], solved, NN)
    last = y_out[(count - 1) * size :, :]
    right = sep_rhs[...]
    width = coupling.shape[1]
    offset = 0
    for level, rows in enumerate(sizes):
        spread = placement(right.shape[0], offset, rows, where[level], width)
        offset += rows
        t_out[:, level * width : (level + 1) * width] = pick_right(right, spread, TN) - mm(
            last, coupling[level * size : (level + 1) * size, :], TN
        )


def backward_kernel(sizes, where, pattern, y, x, inverse, blocks, coupling, out, sep_out):
    count, size = inverse.shape[0], inverse.shape[1]
    starts = pair_starts(count)
    width = coupling.shape[1]
    place = where[LEVELS]
    quarter = x.shape[0]
    xs = jnp.concatenate([x[jnp.bitwise_xor(place, q)] for q in range(quarter)], axis=0)
    correction = jnp.zeros((size, y.shape[1]), F32)
    pieces = jnp.zeros((sep_out.shape[0], y.shape[1]), F32)
    offset = 0
    for level, rows in enumerate(sizes):
        part = xs[:, level * width : (level + 1) * width]
        correction = correction + mm(coupling[level * size : (level + 1) * size, :], part, NT)
        spread = placement(sep_out.shape[0], offset, rows, where[level], width)
        pieces = pieces + pick_left(spread, part, NT)
        offset += rows
    sep_out[...] = pieces
    pending = [y[i * size : (i + 1) * size, :] for i in range(count)]
    pending[-1] = pending[-1] - correction
    for column in reversed(range(count)):
        solved = mm(inverse[column], pending[column], TN)
        out[column * size : (column + 1) * size, :] = solved
        for earlier in reversed(range(column)):
            pair = starts[earlier] + column - earlier - 1
            weight = pattern[0, pair].astype(F32)
            pending[earlier] = pending[earlier] - weight * mm(blocks[pair], solved, TN)


def spots(start, count):
    return [slice(start + r * 128, start + (r + 1) * 128) for r in range(count)]


def times_rows(value, places, mats, index):
    result = []
    for half in mats:
        total = None
        for r, place in enumerate(places):
            term = mm(value[:, place], half[r, index], NT)
            total = term if total is None else total + term
        result.append(total)
    return result


def times_matrix(value, mats, index, r):
    total = None
    for piece, half in zip(value, mats):
        term = mm(piece, half[r, index], NN)
        total = term if total is None else total + term
    return total


def level_kernel(index, right, base, mine, other, z_out, v_out):
    mats = (mine, other)
    places = spots(0, mine.shape[0])
    z = times_rows(right, places, mats, index)
    z_out[...] = jnp.concatenate(z, axis=1)
    for r, place in enumerate(places):
        v_out[:, place] = base[:, place] - times_matrix(z, mats, index + 1, r)


def top_kernel(right, z1, z2, z3, m1, o1, m2, o2, m3, o3, x_out):
    width = right.shape[1]
    count = m3.shape[0]
    top = (m3, o3)
    z = times_rows(right, spots(0, count), top, 0)
    order = [(z3, top, 1), (z2, (m2, o2), 0), (z1, (m1, o1), 0)]
    mats, index = top, 0
    level = 3
    while True:
        for r, place in enumerate(spots(level * width, count)):
            x_out[:, place] = times_matrix(z, mats, index, r)
        if not order:
            break
        held, mats, index = order.pop(0)
        moved = times_rows(x_out, spots(level * width, count), mats, index + 1)
        half = held.shape[1] // 2
        z = [held[:, :half] - moved[0], held[:, half:] - moved[1]]
        level -= 1


SMEM = pl.BlockSpec(memory_space=pltpu.SMEM)
VMEM = pl.BlockSpec(memory_space=pltpu.VMEM)


def params():
    return pltpu.CompilerParams(vmem_limit_bytes=40 * 1024 * 1024)


def call(kernel, outs, *arrays):
    return pl.pallas_call(
        kernel,
        out_shape=[jax.ShapeDtypeStruct(s, F32) for s in outs],
        in_specs=[SMEM if v.dtype == jnp.int32 else VMEM for v in arrays],
        out_specs=[VMEM] * len(outs),
        compiler_params=params(),
    )(*arrays)


def shards(leaf_rhs, leaf_inverse, leaf_blocks, leaf_pattern, leaf_coupling, sep_rhs, sep_inverse, sep_coupling):
    position = lax.axis_index("leaf")
    columns = leaf_rhs.shape[1]
    width = leaf_coupling.shape[1]
    leaves = lax.axis_size("leaf")
    groups = [4, 16, 64, 128]
    sizes = [width // g for g in groups]
    offsets = [sum(sizes[:i]) for i in range(LEVELS)]
    where = jnp.stack([position % g * r for g, r in zip(groups, sizes)] + [position % 4]).astype(jnp.int32)

    def rows(array, level):
        return array[offsets[level] : offsets[level] + sizes[level]]

    def both(level):
        return jnp.stack([rows(sep_inverse, level), rows(sep_coupling, level)])

    def planes(value):
        count = lax.axis_size("col")
        return lax.all_to_all(jnp.broadcast_to(value[None], (count, *value.shape)), "col", 0, 0, tiled=True)

    tie = lax.optimization_barrier
    halves_z, wrap_z, wrap_y = 1 << Z4, (1 << Z8) | (1 << Z4) | (1 << Z2), (1 << Y2) | (1 << Y1)
    near = [[g * 4 + m for m in range(4)] for g in range(leaves // 4)]
    level = lambda kernel, *arrays: call(kernel, [(columns // 4, width)] * 2, *arrays)

    first = grow(both(0), 1 << Z1)
    far = grow(rows(sep_inverse, 3)[None], wrap_y)
    padded = jnp.pad(sep_rhs, ((0, 4), (0, 0)))
    y, t = call(
        functools.partial(forward_kernel, sizes),
        [leaf_rhs.shape, (columns, LEVELS * width)],
        where, leaf_pattern, leaf_rhs, leaf_inverse, leaf_blocks, leaf_coupling, padded,
    )
    t, first, far = tie((t, first, far))

    t = lax.all_to_all(t, "leaf", 0, 0, axis_index_groups=near, tiled=True)
    far = grow(jnp.concatenate([far, both(2)], 0), 1 << Y1)
    first = planes(first)
    t, far = tie((t, far))

    far = grow(far, wrap_z)
    t = t.reshape(4, columns // 4, LEVELS * width).sum(0)
    first, t, far = tie((first, t, far))

    far = grow(jnp.concatenate([far, both(1)], 0), halves_z)
    first = (first, across(first, CORE_MASK))
    z1, v = level(functools.partial(level_kernel, 0), t[:, :width], t[:, width : 2 * width], *first)
    v = jnp.concatenate([v, t[:, 2 * width :]], 1)
    v, far = tie((v, far))

    far = grow(far, 1 << Z2)
    v = v + across(v, 1 << Z2)
    v, far = tie((v, far))

    far = grow(far, 1 << Z1)
    v_far = across(v, halves_z)
    far, v = tie((far, v))

    third = lax.all_gather(far[:3], "col", axis=0)
    second = planes(far[3:])
    second, v, v_far = tie((second, v, v_far))
    second = (second, across(second, CORE_MASK))
    v = v + v_far
    z2, v3 = level(functools.partial(level_kernel, 0), v[:, :width], v[:, width : 2 * width], *second)
    v = jnp.concatenate([v3, v[:, 2 * width :]], 1)
    v = v + across(v, wrap_z)
    v, third = tie((v, third))

    third = (third, across(third, CORE_MASK))
    v = v + across(v, 1 << Y1)
    z3, v = level(functools.partial(level_kernel, 1), v[:, :width], v[:, width:], *third)
    v = v + across(v, wrap_y)
    (x,) = call(top_kernel, [(columns // 4, LEVELS * width)], v, z1, z2, z3, *first, *second, *third)
    x = jnp.stack([x, across(x, 1 << Z1)])
    other = across(x, CORE_MASK)
    x = jnp.stack([x[0], other[0], x[1], other[1]], 0)
    return call(
        functools.partial(backward_kernel, sizes),
        [leaf_rhs.shape, padded.shape],
        where, leaf_pattern, y, x, leaf_inverse, leaf_blocks, leaf_coupling,
    )


def program(*arrays):
    leaf, sep = shards(*arrays)
    return leaf, sep[: arrays[5].shape[0]]


def solution(mesh):
    return jax.shard_map(
        program,
        mesh=mesh,
        in_specs=(
            P("leaf", "col"),
            P("leaf", None, None),
            P("leaf", None, None),
            P("leaf", None),
            P("leaf", None),
            P("leaf", "col"),
            P("leaf", "col"),
            P("leaf", "col"),
        ),
        out_specs=(P("leaf", "col"), P("leaf", "col")),
        check_vma=False,
    )
```

```python
import functools

import jax
import jax.numpy as jnp
from jax import lax
from jax.experimental import pallas as pl
from jax.experimental.pallas import tpu as pltpu
from jax.sharding import PartitionSpec as P

F32 = jnp.float32
BF16 = jnp.bfloat16
NN = (((1,), (0,)), ((), ()))
NT = (((1,), (1,)), ((), ()))
TN = (((0,), (0,)), ((), ()))
LEVELS = 4
Z1, Z2, Z4, Z8, Y1, Y2 = range(1, 7)
CORE_MASK = 1


def halves(value):
    high = value.astype(BF16)
    low = (value - high.astype(F32)).astype(BF16)
    return high, low


def mm(left, right, dims):
    left_high, left_low = halves(left)
    right_high, right_low = halves(right)
    dot = functools.partial(lax.dot_general, dimension_numbers=dims, preferred_element_type=F32)
    return dot(left_high, right_high) + (dot(left_high, right_low) + dot(left_low, right_high))


def pick_left(spread, value, dims):
    high, low = halves(value)
    rest = (value - high.astype(F32) - low.astype(F32)).astype(BF16)
    dot = functools.partial(lax.dot_general, spread, dimension_numbers=dims, preferred_element_type=F32)
    return dot(high) + (dot(low) + dot(rest))


def pick_right(value, spread, dims):
    high, low = halves(value)
    rest = (value - high.astype(F32) - low.astype(F32)).astype(BF16)
    dot = functools.partial(lax.dot_general, dimension_numbers=dims, preferred_element_type=F32)
    return dot(high, spread) + (dot(low, spread) + dot(rest, spread))


def swap(value, axis, mask):
    return lax.ppermute(value, axis, [(i, i ^ mask) for i in range(lax.axis_size(axis))])


def across(value, mask):
    return swap(value, "leaf", mask)


def grow(value, mask):
    return jnp.concatenate([value, across(value, mask)], axis=1)


def pair_starts(blocks):
    starts, running = [], 0
    for column in range(blocks):
        starts.append(running)
        running += blocks - 1 - column
    return starts


def placement(rows, offset, count, start, width):
    row = lax.broadcasted_iota(jnp.int32, (rows, width), 0)
    column = lax.broadcasted_iota(jnp.int32, (rows, width), 1)
    inside = (row >= offset) & (row < offset + count)
    return jnp.where(inside & (row - offset == column - start), 1.0, 0.0).astype(BF16)


def forward_kernel(
    sizes, where, pattern, rhs_far, inverse_far, blocks_far, coupling_far, sep_rhs, y_out, t_out, rhs, inverse, blocks, coupling, sems
):
    count, size = inverse.shape[0], inverse.shape[1]
    starts = pair_starts(count)
    copies = [
        pltpu.make_async_copy(rhs_far, rhs, sems.at[0]),
        pltpu.make_async_copy(inverse_far, inverse, sems.at[1]),
        pltpu.make_async_copy(coupling_far, coupling, sems.at[2]),
    ]
    for column in range(count - 1):
        part = pl.ds(starts[column], count - 1 - column)
        copies.append(pltpu.make_async_copy(blocks_far.at[part], blocks.at[part], sems.at[3 + column]))
    for copy in copies[:2] + copies[3:] + copies[2:3]:
        copy.start()
    copies[0].wait()
    copies[1].wait()
    pending = [rhs[i * size : (i + 1) * size, :] for i in range(count)]
    for column in range(count):
        solved = mm(inverse[column], pending[column], NN)
        y_out[column * size : (column + 1) * size, :] = solved
        if column < count - 1:
            copies[3 + column].wait()
        for later in range(column + 1, count):
            pair = starts[column] + later - column - 1
            weight = pattern[0, pair].astype(F32)
            pending[later] = pending[later] - weight * mm(blocks[pair], solved, NN)
    last = y_out[(count - 1) * size :, :]
    right = sep_rhs[...]
    width = coupling.shape[1]
    copies[2].wait()
    offset = 0
    for level, rows in enumerate(sizes):
        spread = placement(right.shape[0], offset, rows, where[level], width)
        offset += rows
        t_out[:, level * width : (level + 1) * width] = pick_right(right, spread, TN) - mm(
            last, coupling[level * size : (level + 1) * size, :], TN
        )


def backward_kernel(sizes, where, pattern, y, x, inverse, blocks, coupling, out, sep_out):
    count, size = inverse.shape[0], inverse.shape[1]
    starts = pair_starts(count)
    width = coupling.shape[1]
    place = where[LEVELS]
    quarter = x.shape[0]
    xs = jnp.concatenate([x[jnp.bitwise_xor(place, q)] for q in range(quarter)], axis=0)
    correction = jnp.zeros((size, y.shape[1]), F32)
    padded = -(-sep_out.shape[0] // 8) * 8
    pieces = jnp.zeros((padded, y.shape[1]), F32)
    offset = 0
    for level, rows in enumerate(sizes):
        part = xs[:, level * width : (level + 1) * width]
        correction = correction + mm(coupling[level * size : (level + 1) * size, :], part, NT)
        spread = placement(padded, offset, rows, where[level], width)
        pieces = pieces + pick_left(spread, part, NT)
        offset += rows
    sep_out[...] = pieces[: sep_out.shape[0], :]
    pending = [y[i * size : (i + 1) * size, :] for i in range(count)]
    pending[-1] = pending[-1] - correction
    for column in reversed(range(count)):
        solved = mm(inverse[column], pending[column], TN)
        out[column * size : (column + 1) * size, :] = solved
        for earlier in reversed(range(column)):
            pair = starts[earlier] + column - earlier - 1
            weight = pattern[0, pair].astype(F32)
            pending[earlier] = pending[earlier] - weight * mm(blocks[pair], solved, TN)


def spots(start, count):
    return [slice(start + r * 128, start + (r + 1) * 128) for r in range(count)]


def times_rows(value, places, mats, index):
    result = []
    for half in mats:
        total = None
        for r, place in enumerate(places):
            term = mm(value[:, place], half[r, index], NT)
            total = term if total is None else total + term
        result.append(total)
    return result


def times_matrix(value, mats, index, r):
    total = None
    for piece, half in zip(value, mats):
        term = mm(piece, half[r, index], NN)
        total = term if total is None else total + term
    return total


def level_kernel(index, right, base, mine, other, z_out, v_out):
    mats = (mine, other)
    places = spots(0, mine.shape[0])
    z = times_rows(right, places, mats, index)
    z_out[...] = jnp.concatenate(z, axis=1)
    for r, place in enumerate(places):
        v_out[:, place] = base[:, place] - times_matrix(z, mats, index + 1, r)


def top_kernel(right, z1, z2, z3, m1, o1, m2, o2, m3, o3, x_out):
    width = right.shape[1]
    count = m3.shape[0]
    top = (m3, o3)
    z = times_rows(right, spots(0, count), top, 0)
    order = [(z3, top, 1), (z2, (m2, o2), 0), (z1, (m1, o1), 0)]
    mats, index = top, 0
    level = 3
    while True:
        for r, place in enumerate(spots(level * width, count)):
            x_out[:, place] = times_matrix(z, mats, index, r)
        if not order:
            break
        held, mats, index = order.pop(0)
        moved = times_rows(x_out, spots(level * width, count), mats, index + 1)
        half = held.shape[1] // 2
        z = [held[:, :half] - moved[0], held[:, half:] - moved[1]]
        level -= 1


SMEM = pl.BlockSpec(memory_space=pltpu.SMEM)
VMEM = pl.BlockSpec(memory_space=pltpu.VMEM)


def params():
    return pltpu.CompilerParams(vmem_limit_bytes=40 * 1024 * 1024)


def call(kernel, outs, *arrays):
    return pl.pallas_call(
        kernel,
        out_shape=[jax.ShapeDtypeStruct(s, F32) for s in outs],
        in_specs=[SMEM if v.dtype == jnp.int32 else VMEM for v in arrays],
        out_specs=[VMEM] * len(outs),
        compiler_params=params(),
    )(*arrays)


def shards(leaf_rhs, leaf_inverse, leaf_blocks, leaf_pattern, leaf_coupling, sep_rhs, sep_inverse, sep_coupling):
    position = lax.axis_index("leaf")
    columns = leaf_rhs.shape[1]
    width = leaf_coupling.shape[1]
    leaves = lax.axis_size("leaf")
    groups = [4, 16, 64, 128]
    sizes = [width // g for g in groups]
    offsets = [sum(sizes[:i]) for i in range(LEVELS)]
    where = jnp.stack([position % g * r for g, r in zip(groups, sizes)] + [position % 4]).astype(jnp.int32)

    def rows(array, level):
        return array[offsets[level] : offsets[level] + sizes[level]]

    def both(level):
        return jnp.stack([rows(sep_inverse, level), rows(sep_coupling, level)])

    def planes(value):
        count = lax.axis_size("col")
        return lax.all_to_all(jnp.broadcast_to(value[None], (count, *value.shape)), "col", 0, 0, tiled=True)

    tie = lax.optimization_barrier
    halves_z, wrap_z, wrap_y = 1 << Z4, (1 << Z8) | (1 << Z4) | (1 << Z2), (1 << Y2) | (1 << Y1)
    near = [[g * 4 + m for m in range(4)] for g in range(leaves // 4)]
    level = lambda kernel, *arrays: call(kernel, [(columns // 4, width)] * 2, *arrays)

    first = grow(both(0), 1 << Z1)
    far = grow(rows(sep_inverse, 3)[None], wrap_y)
    where, first = tie((where, first))
    first = planes(first)
    y, t = pl.pallas_call(
        functools.partial(forward_kernel, sizes),
        out_shape=[
            jax.ShapeDtypeStruct(leaf_rhs.shape, F32),
            jax.ShapeDtypeStruct((columns, LEVELS * width), F32),
        ],
        in_specs=[SMEM, SMEM] + [pl.BlockSpec(memory_space=pltpu.HBM)] * 4 + [VMEM],
        out_specs=[VMEM, VMEM],
        scratch_shapes=[pltpu.VMEM(v.shape, F32) for v in (leaf_rhs, leaf_inverse, leaf_blocks, leaf_coupling)]
        + [pltpu.SemaphoreType.DMA((2 + leaf_inverse.shape[0],))],
        compiler_params=params(),
    )(where, leaf_pattern, leaf_rhs, leaf_inverse, leaf_blocks, leaf_coupling, sep_rhs)
    second = both(1)
    t, far, second = tie((t, far, second))

    t = lax.all_to_all(t, "leaf", 0, 0, axis_index_groups=near, tiled=True)
    far = grow(jnp.concatenate([far, both(2)], 0), 1 << Y1)
    second = grow(second, halves_z)
    far, second = tie((far, second))

    line = [[m + 4 * k for k in range(8)] for m in range(leaves) if m % 32 < 4]
    far = lax.all_to_all(jnp.broadcast_to(far[None], (8, *far.shape)), "leaf", 0, 0, axis_index_groups=line, tiled=True)
    second = grow(second, 1 << Z2)
    first, t, second = tie((first, t, second))
    t = t.reshape(4, columns // 4, LEVELS * width).sum(0)

    upper = t[:, 2 * width :]
    upper_z2 = across(upper, 1 << Z2)
    first = (first, across(first, CORE_MASK))
    z1, v = level(functools.partial(level_kernel, 0), t[:, :width], t[:, width : 2 * width], *first)
    v, upper, upper_z2, second = tie((v, upper, upper_z2, second))

    upper = upper + upper_z2
    v_z2 = across(v, 1 << Z2)
    far = far.transpose(1, 0, 2, 3).reshape(3, -1, 128)
    far = grow(jnp.concatenate([far, second], 0), 1 << Z1)
    v = v + v_z2
    v, far, upper = tie((v, far, upper))

    second = planes(far[3:])
    third = lax.all_gather(far[:3], "col", axis=0)
    v = v + across(v, halves_z)
    v, second = tie((v, second))

    upper_z4 = across(upper, halves_z)
    second = (second, across(second, CORE_MASK))
    upper = upper + upper_z4
    z2, v3 = level(functools.partial(level_kernel, 0), v, upper[:, :width], *second)
    v = jnp.concatenate([v3, upper[:, width:]], 1)
    v = v + across(v, wrap_z)
    v, third = tie((v, third))

    third = (third, across(third, CORE_MASK))
    v = v + across(v, 1 << Y1)
    z3, v = level(functools.partial(level_kernel, 1), v[:, :width], v[:, width:], *third)
    v = v + across(v, wrap_y)
    (x,) = call(top_kernel, [(columns // 4, LEVELS * width)], v, z1, z2, z3, *first, *second, *third)
    x = jnp.stack([x, across(x, 1 << Z1)])
    other = across(x, CORE_MASK)
    x = jnp.stack([x[0], other[0], x[1], other[1]], 0)
    return call(
        functools.partial(backward_kernel, sizes),
        [leaf_rhs.shape, sep_rhs.shape],
        where, leaf_pattern, y, x, leaf_inverse, leaf_blocks, leaf_coupling,
    )


def solution(mesh):
    return jax.shard_map(
        shards,
        mesh=mesh,
        in_specs=(
            P("leaf", "col"),
            P("leaf", None, None),
            P("leaf", None, None),
            P("leaf", None),
            P("leaf", None),
            P("leaf", "col"),
            P("leaf", "col"),
            P("leaf", "col"),
        ),
        out_specs=(P("leaf", "col"), P("leaf", "col")),
        check_vma=False,
    )
```

```python
import functools

import jax
import jax.numpy as jnp
from jax import lax
from jax.experimental import pallas as pl
from jax.experimental.pallas import tpu as pltpu
from jax.sharding import PartitionSpec as P

F32 = jnp.float32
BF16 = jnp.bfloat16
NN = (((1,), (0,)), ((), ()))
NT = (((1,), (1,)), ((), ()))
TN = (((0,), (0,)), ((), ()))
LEVELS = 4
Z1, Z2, Z4, Z8, Y1, Y2 = range(1, 7)
CORE_MASK = 1


def halves(value):
    high = value.astype(BF16)
    low = (value - high.astype(F32)).astype(BF16)
    return high, low


def mm(left, right, dims):
    left_high, left_low = halves(left)
    right_high, right_low = halves(right)
    dot = functools.partial(lax.dot_general, dimension_numbers=dims, preferred_element_type=F32)
    return dot(left_high, right_high) + (dot(left_high, right_low) + dot(left_low, right_high))


def pick_left(spread, value, dims):
    high, low = halves(value)
    rest = (value - high.astype(F32) - low.astype(F32)).astype(BF16)
    dot = functools.partial(lax.dot_general, spread, dimension_numbers=dims, preferred_element_type=F32)
    return dot(high) + (dot(low) + dot(rest))


def pick_right(value, spread, dims):
    high, low = halves(value)
    rest = (value - high.astype(F32) - low.astype(F32)).astype(BF16)
    dot = functools.partial(lax.dot_general, dimension_numbers=dims, preferred_element_type=F32)
    return dot(high, spread) + (dot(low, spread) + dot(rest, spread))


def swap(value, axis, mask):
    return lax.ppermute(value, axis, [(i, i ^ mask) for i in range(lax.axis_size(axis))])


def across(value, mask):
    return swap(value, "leaf", mask)


def grow(value, mask):
    return jnp.concatenate([value, across(value, mask)], axis=1)


def pair_starts(blocks):
    starts, running = [], 0
    for column in range(blocks):
        starts.append(running)
        running += blocks - 1 - column
    return starts


def placement(rows, offset, count, start, width):
    row = lax.broadcasted_iota(jnp.int32, (rows, width), 0)
    column = lax.broadcasted_iota(jnp.int32, (rows, width), 1)
    inside = (row >= offset) & (row < offset + count)
    return jnp.where(inside & (row - offset == column - start), 1.0, 0.0).astype(BF16)


def forward_kernel(sizes, where, pattern, rhs, inverse, blocks, coupling, sep_rhs, y_out, t_out):
    count, size = inverse.shape[0], inverse.shape[1]
    starts = pair_starts(count)
    pending = [rhs[i * size : (i + 1) * size, :] for i in range(count)]
    for column in range(count):
        solved = mm(inverse[column], pending[column], NN)
        y_out[column * size : (column + 1) * size, :] = solved
        for later in range(column + 1, count):
            pair = starts[column] + later - column - 1
            weight = pattern[0, pair].astype(F32)
            pending[later] = pending[later] - weight * mm(blocks[pair], solved, NN)
    last = y_out[(count - 1) * size :, :]
    right = sep_rhs[...]
    width = coupling.shape[1]
    offset = 0
    for level, rows in enumerate(sizes):
        spread = placement(right.shape[0], offset, rows, where[level], width)
        offset += rows
        t_out[:, level * width : (level + 1) * width] = pick_right(right, spread, TN) - mm(
            last, coupling[level * size : (level + 1) * size, :], TN
        )


def backward_kernel(sizes, where, pattern, y, near, across_core, inverse, blocks, coupling, out, sep_out):
    count, size = inverse.shape[0], inverse.shape[1]
    starts = pair_starts(count)
    width = coupling.shape[1]
    place = where[LEVELS]
    chunks = []
    for member in range(2 * near.shape[0]):
        apart = place ^ member
        chunks.append(jnp.where(apart % 2 == 1, across_core[apart // 2], near[apart // 2]))
    xs = jnp.concatenate(chunks, axis=0)
    correction = jnp.zeros((size, y.shape[1]), F32)
    padded = -(-sep_out.shape[0] // 8) * 8
    pieces = jnp.zeros((padded, y.shape[1]), F32)
    offset = 0
    for level, rows in enumerate(sizes):
        part = xs[:, level * width : (level + 1) * width]
        correction = correction + mm(coupling[level * size : (level + 1) * size, :], part, NT)
        spread = placement(padded, offset, rows, where[level], width)
        pieces = pieces + pick_left(spread, part, NT)
        offset += rows
    sep_out[...] = pieces[: sep_out.shape[0], :]
    pending = [y[i * size : (i + 1) * size, :] for i in range(count)]
    pending[-1] = pending[-1] - correction
    for column in reversed(range(count)):
        solved = mm(inverse[column], pending[column], TN)
        out[column * size : (column + 1) * size, :] = solved
        for earlier in reversed(range(column)):
            pair = starts[earlier] + column - earlier - 1
            weight = pattern[0, pair].astype(F32)
            pending[earlier] = pending[earlier] - weight * mm(blocks[pair], solved, TN)


def spots(start, count, turn=None):
    if turn is None:
        return [slice(start + r * 128, start + (r + 1) * 128) for r in range(count)]
    return [pl.ds(pl.multiple_of(start + (turn ^ r) * 128, 128), 128) for r in range(count)]


def times_rows(value, places, mats, index):
    result = []
    for half in mats:
        total = None
        for r, place in enumerate(places):
            term = mm(value[:, place], half[r, index], NT)
            total = term if total is None else total + term
        result.append(total)
    return result


def times_matrix(value, mats, index, r):
    total = None
    for piece, half in zip(value, mats):
        term = mm(piece, half[r, index], NN)
        total = term if total is None else total + term
    return total


def summed(parts, rows):
    total = None
    for part in parts:
        for start in range(0, part.shape[0], rows):
            term = part[start : start + rows, :]
            total = term if total is None else total + term
    return total


def level_kernel(index, turned, plane, *refs):
    mine, other, z_out, v_out = refs[-4:]
    mats = (mine, other)
    total = summed(refs[:-4], z_out.shape[0])
    places = spots(0, mine.shape[0], plane[0] if turned else None)
    width = z_out.shape[1]
    z_out[...] = total[:, :width]
    v_out[...] = total[:, width:]
    z = times_rows(z_out, places, mats, index)
    z_out[...] = jnp.concatenate(z, axis=1)
    for r, place in enumerate(places):
        v_out[:, place] = v_out[:, place] - times_matrix(z, mats, index + 1, r)


def top_kernel(plane, right, right_far, z1, z2, z3, m1, o1, m2, o2, m3, o3, x_out):
    width = right.shape[1]
    count = m3.shape[0]
    top = (m3, o3)
    z = times_rows(right[...] + right_far[...], spots(0, count), top, 0)
    order = [(z3, top, 1, None), (z2, (m2, o2), 0, None), (z1, (m1, o1), 0, plane[0])]
    mats, index, turn = top, 0, None
    level = 3
    while True:
        for r, place in enumerate(spots(level * width, count, turn)):
            x_out[:, place] = times_matrix(z, mats, index, r)
        if not order:
            break
        held, mats, index, turn = order.pop(0)
        moved = times_rows(x_out, spots(level * width, count, turn), mats, index + 1)
        half = held.shape[1] // 2
        z = [held[:, :half] - moved[0], held[:, half:] - moved[1]]
        level -= 1


SMEM = pl.BlockSpec(memory_space=pltpu.SMEM)
VMEM = pl.BlockSpec(memory_space=pltpu.VMEM)


def params():
    return pltpu.CompilerParams(vmem_limit_bytes=40 * 1024 * 1024)


def call(kernel, outs, *arrays):
    return pl.pallas_call(
        kernel,
        out_shape=[jax.ShapeDtypeStruct(s, F32) for s in outs],
        in_specs=[SMEM if v.dtype == jnp.int32 else VMEM for v in arrays],
        out_specs=[VMEM] * len(outs),
        compiler_params=params(),
    )(*arrays)


def shards(leaf_rhs, leaf_inverse, leaf_blocks, leaf_pattern, leaf_coupling, sep_rhs, sep_inverse, sep_coupling):
    position = lax.axis_index("leaf")
    columns = leaf_rhs.shape[1]
    width = leaf_coupling.shape[1]
    leaves = lax.axis_size("leaf")
    groups = [4, 16, 64, 128]
    sizes = [width // g for g in groups]
    offsets = [sum(sizes[:i]) for i in range(LEVELS)]
    where = jnp.stack([position % g * r for g, r in zip(groups, sizes)] + [position % 4]).astype(jnp.int32)

    def rows(array, level):
        return array[offsets[level] : offsets[level] + sizes[level]]

    def both(level):
        return jnp.stack([rows(sep_inverse, level), rows(sep_coupling, level)])

    def planes(value):
        count = lax.axis_size("col")
        return lax.all_to_all(jnp.broadcast_to(value[None], (count, *value.shape)), "col", 0, 0, tiled=True)

    tie = lax.optimization_barrier
    halves_z, wrap_z, wrap_y = 1 << Z4, (1 << Z8) | (1 << Z4) | (1 << Z2), (1 << Y2) | (1 << Y1)
    near = [[g * 4 + m for m in range(4)] for g in range(leaves // 4)]
    plane = lax.axis_index("col").astype(jnp.int32)[None]

    def turned_planes(value):
        return jnp.stack([value] + [swap(value, "col", r) for r in range(1, lax.axis_size("col"))])

    def solve(index, turned, depth, *arrays):
        outs = [(columns // 4, width), (columns // 4, depth * width)]
        return call(functools.partial(level_kernel, index, turned), outs, plane, *arrays)

    first = grow(both(0), 1 << Z1)
    far = grow(rows(sep_inverse, 3)[None], wrap_y)
    y, t = call(
        functools.partial(forward_kernel, sizes),
        [leaf_rhs.shape, (columns, LEVELS * width)],
        where, leaf_pattern, leaf_rhs, leaf_inverse, leaf_blocks, leaf_coupling, sep_rhs,
    )
    t, first, far = tie((t, first, far))

    t = lax.all_to_all(t, "leaf", 0, 0, axis_index_groups=near, tiled=True)
    first = turned_planes(first)
    far = grow(jnp.concatenate([far, both(2)], 0), 1 << Y1)
    far = grow(far, wrap_z)
    t, first, far = tie((t, first, far))

    first = (first, across(first, CORE_MASK))
    far = grow(jnp.concatenate([far, both(1)], 0), halves_z)
    z1, v = solve(0, True, 3, t, *first)
    v, far = tie((v, far))
    v_far = across(v, 1 << Z2)

    far = grow(far, 1 << Z2)
    v = v + v_far
    v_far = across(v, halves_z)
    far = grow(far, 1 << Z1)
    far, v = tie((far, v))

    second = planes(far[3:])
    third = lax.all_gather(far[:3], "col", axis=0)
    second, v, v_far = tie((second, v, v_far))

    second = (second, across(second, CORE_MASK))
    z2, v = solve(0, False, 2, v, v_far, *second)
    v = v + across(v, wrap_z)
    v, third = tie((v, third))

    third = (third, across(third, CORE_MASK))
    z3, v = solve(1, False, 1, v, across(v, 1 << Y1), *third)
    (x,) = call(
        top_kernel, [(columns // 4, LEVELS * width)], plane, v, across(v, wrap_y), z1, z2, z3, *first, *second, *third
    )
    x = jnp.stack([x, across(x, 1 << Z1)])
    return call(
        functools.partial(backward_kernel, sizes),
        [leaf_rhs.shape, sep_rhs.shape],
        where, leaf_pattern, y, x, across(x, CORE_MASK), leaf_inverse, leaf_blocks, leaf_coupling,
    )


def solution(mesh):
    return jax.shard_map(
        shards,
        mesh=mesh,
        in_specs=(
            P("leaf", "col"),
            P("leaf", None, None),
            P("leaf", None, None),
            P("leaf", None),
            P("leaf", None),
            P("leaf", "col"),
            P("leaf", "col"),
            P("leaf", "col"),
        ),
        out_specs=(P("leaf", "col"), P("leaf", "col")),
        check_vma=False,
    )
```

```python
import functools

import jax
import jax.numpy as jnp
from jax import lax
from jax.experimental import pallas as pl
from jax.experimental.pallas import tpu as pltpu
from jax.sharding import PartitionSpec as P

F32 = jnp.float32
BF16 = jnp.bfloat16
NN = (((1,), (0,)), ((), ()))
NT = (((1,), (1,)), ((), ()))
TN = (((0,), (0,)), ((), ()))
LEVELS = 4
Z1, Z2, Z4, Z8, Y1, Y2 = range(1, 7)
CORE_MASK = 1


def halves(value):
    high = value.astype(BF16)
    low = (value - high.astype(F32)).astype(BF16)
    return high, low


def mm(left, right, dims):
    left_high, left_low = halves(left)
    right_high, right_low = halves(right)
    dot = functools.partial(lax.dot_general, dimension_numbers=dims, preferred_element_type=F32)
    return dot(left_high, right_high) + (dot(left_high, right_low) + dot(left_low, right_high))


def pick_left(spread, value, dims):
    high, low = halves(value)
    rest = (value - high.astype(F32) - low.astype(F32)).astype(BF16)
    dot = functools.partial(lax.dot_general, spread, dimension_numbers=dims, preferred_element_type=F32)
    return dot(high) + (dot(low) + dot(rest))


def pick_right(value, spread, dims):
    high, low = halves(value)
    rest = (value - high.astype(F32) - low.astype(F32)).astype(BF16)
    dot = functools.partial(lax.dot_general, dimension_numbers=dims, preferred_element_type=F32)
    return dot(high, spread) + (dot(low, spread) + dot(rest, spread))


def swap(value, axis, mask):
    return lax.ppermute(value, axis, [(i, i ^ mask) for i in range(lax.axis_size(axis))])


def across(value, mask):
    return swap(value, "leaf", mask)


def grow(value, mask):
    return jnp.concatenate([value, across(value, mask)], axis=1)


def pair_starts(blocks):
    starts, running = [], 0
    for column in range(blocks):
        starts.append(running)
        running += blocks - 1 - column
    return starts


def placement(rows, offset, count, start, width):
    row = lax.broadcasted_iota(jnp.int32, (rows, width), 0)
    column = lax.broadcasted_iota(jnp.int32, (rows, width), 1)
    inside = (row >= offset) & (row < offset + count)
    return jnp.where(inside & (row - offset == column - start), 1.0, 0.0).astype(BF16)


def forward_kernel(sizes, where, pattern, rhs, inverse, blocks, coupling, sep_rhs, y_out, t_out):
    count, size = inverse.shape[0], inverse.shape[1]
    starts = pair_starts(count)
    pending = [rhs[i * size : (i + 1) * size, :] for i in range(count)]
    for column in range(count):
        solved = mm(inverse[column], pending[column], NN)
        y_out[column * size : (column + 1) * size, :] = solved
        for later in range(column + 1, count):
            pair = starts[column] + later - column - 1
            weight = pattern[0, pair].astype(F32)
            pending[later] = pending[later] - weight * mm(blocks[pair], solved, NN)
    last = y_out[(count - 1) * size :, :]
    right = sep_rhs[...]
    width = coupling.shape[1]
    offset = 0
    for level, rows in enumerate(sizes):
        spread = placement(right.shape[0], offset, rows, where[level], width)
        offset += rows
        t_out[:, level * width : (level + 1) * width] = pick_right(right, spread, TN) - mm(
            last, coupling[level * size : (level + 1) * size, :], TN
        )


def backward_kernel(sizes, where, pattern, y, near, across_core, inverse, blocks, coupling, out, sep_out):
    count, size = inverse.shape[0], inverse.shape[1]
    starts = pair_starts(count)
    width = coupling.shape[1]
    place = where[LEVELS]
    chunks = []
    for member in range(2 * near.shape[0]):
        apart = place ^ member
        chunks.append(jnp.where(apart % 2 == 1, across_core[apart // 2], near[apart // 2]))
    xs = jnp.concatenate(chunks, axis=0)
    correction = jnp.zeros((size, y.shape[1]), F32)
    padded = -(-sep_out.shape[0] // 8) * 8
    pieces = jnp.zeros((padded, y.shape[1]), F32)
    offset = 0
    for level, rows in enumerate(sizes):
        part = xs[:, level * width : (level + 1) * width]
        correction = correction + mm(coupling[level * size : (level + 1) * size, :], part, NT)
        spread = placement(padded, offset, rows, where[level], width)
        pieces = pieces + pick_left(spread, part, NT)
        offset += rows
    sep_out[...] = pieces[: sep_out.shape[0], :]
    pending = [y[i * size : (i + 1) * size, :] for i in range(count)]
    pending[-1] = pending[-1] - correction
    for column in reversed(range(count)):
        solved = mm(inverse[column], pending[column], TN)
        out[column * size : (column + 1) * size, :] = solved
        for earlier in reversed(range(column)):
            pair = starts[earlier] + column - earlier - 1
            weight = pattern[0, pair].astype(F32)
            pending[earlier] = pending[earlier] - weight * mm(blocks[pair], solved, TN)


def spots(start, count, turn=None):
    if turn is None:
        return [slice(start + r * 128, start + (r + 1) * 128) for r in range(count)]
    return [pl.ds(pl.multiple_of(start + (turn ^ r) * 128, 128), 128) for r in range(count)]


def times_rows(value, places, mats, index):
    result = []
    for half in mats:
        total = None
        for r, place in enumerate(places):
            term = mm(value[:, place], half[r, index], NT)
            total = term if total is None else total + term
        result.append(total)
    return result


def times_matrix(value, mats, index, r):
    total = None
    for piece, half in zip(value, mats):
        term = mm(piece, half[r, index], NN)
        total = term if total is None else total + term
    return total


def summed(parts, rows):
    total = None
    for part in parts:
        for start in range(0, part.shape[0], rows):
            term = part[start : start + rows, :]
            total = term if total is None else total + term
    return total


def level_kernel(index, turned, plane, *refs):
    mine, other, z_out, v_out = refs[-4:]
    mats = (mine, other)
    total = summed(refs[:-4], z_out.shape[0])
    places = spots(0, mine.shape[0], plane[0] if turned else None)
    width = z_out.shape[1]
    z_out[...] = total[:, :width]
    v_out[...] = total[:, width:]
    z = times_rows(z_out, places, mats, index)
    z_out[...] = jnp.concatenate(z, axis=1)
    for r, place in enumerate(places):
        v_out[:, place] = v_out[:, place] - times_matrix(z, mats, index + 1, r)


def top_kernel(plane, right, right_far, z1, z2, z3, m1, o1, m2, o2, m3, o3, x_out):
    width = right.shape[1]
    count = m3.shape[0]
    top = (m3, o3)
    z = times_rows(right[...] + right_far[...], spots(0, count), top, 0)
    order = [(z3, top, 1, None), (z2, (m2, o2), 0, None), (z1, (m1, o1), 0, plane[0])]
    mats, index, turn = top, 0, None
    level = 3
    while True:
        for r, place in enumerate(spots(level * width, count, turn)):
            x_out[:, place] = times_matrix(z, mats, index, r)
        if not order:
            break
        held, mats, index, turn = order.pop(0)
        moved = times_rows(x_out, spots(level * width, count, turn), mats, index + 1)
        half = held.shape[1] // 2
        z = [held[:, :half] - moved[0], held[:, half:] - moved[1]]
        level -= 1


SMEM = pl.BlockSpec(memory_space=pltpu.SMEM)
VMEM = pl.BlockSpec(memory_space=pltpu.VMEM)


def params():
    return pltpu.CompilerParams(vmem_limit_bytes=40 * 1024 * 1024)


def call(kernel, outs, *arrays):
    return pl.pallas_call(
        kernel,
        out_shape=[jax.ShapeDtypeStruct(s, F32) for s in outs],
        in_specs=[SMEM if v.dtype == jnp.int32 else VMEM for v in arrays],
        out_specs=[VMEM] * len(outs),
        compiler_params=params(),
    )(*arrays)


def shards(leaf_rhs, leaf_inverse, leaf_blocks, leaf_pattern, leaf_coupling, sep_rhs, sep_inverse, sep_coupling):
    position = lax.axis_index("leaf")
    columns = leaf_rhs.shape[1]
    width = leaf_coupling.shape[1]
    leaves = lax.axis_size("leaf")
    groups = [4, 16, 64, 128]
    sizes = [width // g for g in groups]
    offsets = [sum(sizes[:i]) for i in range(LEVELS)]
    where = jnp.stack([position % g * r for g, r in zip(groups, sizes)] + [position % 4]).astype(jnp.int32)

    def rows(array, level):
        return array[offsets[level] : offsets[level] + sizes[level]]

    def both(level):
        return jnp.stack([rows(sep_inverse, level), rows(sep_coupling, level)])

    def planes(value):
        count = lax.axis_size("col")
        return lax.all_to_all(jnp.broadcast_to(value[None], (count, *value.shape)), "col", 0, 0, tiled=True)

    tie = lax.optimization_barrier
    halves_z, wrap_z, wrap_y = 1 << Z4, (1 << Z8) | (1 << Z4), (1 << Y2) | (1 << Y1)
    near = [[g * 4 + m for m in range(4)] for g in range(leaves // 4)]
    plane = lax.axis_index("col").astype(jnp.int32)[None]

    def turned_planes(value):
        return jnp.stack([value] + [swap(value, "col", r) for r in range(1, lax.axis_size("col"))])

    def solve(index, turned, depth, *arrays):
        outs = [(columns // 4, width), (columns // 4, depth * width)]
        return call(functools.partial(level_kernel, index, turned), outs, plane, *arrays)

    first = grow(both(0), 1 << Z1)
    far = grow(rows(sep_inverse, 3)[None], wrap_y)
    y, t = call(
        functools.partial(forward_kernel, sizes),
        [leaf_rhs.shape, (columns, LEVELS * width)],
        where, leaf_pattern, leaf_rhs, leaf_inverse, leaf_blocks, leaf_coupling, sep_rhs,
    )
    t, first, far, second = tie((t, first, far, both(1)))

    t = lax.all_to_all(t, "leaf", 0, 0, axis_index_groups=near, tiled=True)
    far = grow(jnp.concatenate([far, both(2)], 0), 1 << Y1)
    second = grow(second, halves_z)
    first = turned_planes(first)
    far = grow(far, wrap_z)
    second = grow(second, 1 << Z2)
    t, first, far, second = tie((t, first, far, second))

    first = (first, across(first, CORE_MASK))
    second = grow(second, 1 << Z1)
    far = grow(far, halves_z)
    z1, v = solve(0, True, 3, t, *first)
    v_far = across(v, 1 << Z2)
    v, v_far, second, far = tie((v, v_far, second, far))

    second = planes(second)
    v = v + v_far
    v_far = across(v, halves_z)
    far = grow(grow(far, 1 << Z2), 1 << Z1)
    far, second, v, v_far = tie((far, second, v, v_far))

    third = lax.all_gather(far, "col", axis=0)
    second = (second, across(second, CORE_MASK))
    z2, v = solve(0, False, 2, v, v_far, *second)
    v = v + across(v, wrap_z)
    v, third = tie((v, third))

    third = (third, across(third, CORE_MASK))
    z3, v = solve(1, False, 1, v, across(v, 1 << Y1), *third)
    (x,) = call(
        top_kernel, [(columns // 4, LEVELS * width)], plane, v, across(v, wrap_y), z1, z2, z3, *first, *second, *third
    )
    x = jnp.stack([x, across(x, 1 << Z1)])
    return call(
        functools.partial(backward_kernel, sizes),
        [leaf_rhs.shape, sep_rhs.shape],
        where, leaf_pattern, y, x, across(x, CORE_MASK), leaf_inverse, leaf_blocks, leaf_coupling,
    )


def solution(mesh):
    return jax.shard_map(
        shards,
        mesh=mesh,
        in_specs=(
            P("leaf", "col"),
            P("leaf", None, None),
            P("leaf", None, None),
            P("leaf", None),
            P("leaf", None),
            P("leaf", "col"),
            P("leaf", "col"),
            P("leaf", "col"),
        ),
        out_specs=(P("leaf", "col"), P("leaf", "col")),
        check_vma=False,
    )
```

```python
import functools

import jax
import jax.numpy as jnp
from jax import lax
from jax.experimental import pallas as pl
from jax.experimental.pallas import tpu as pltpu
from jax.sharding import PartitionSpec as P

F32 = jnp.float32
BF16 = jnp.bfloat16
NN = (((1,), (0,)), ((), ()))
NT = (((1,), (1,)), ((), ()))
TN = (((0,), (0,)), ((), ()))
LEVELS = 4
Z1, Z2, Z4, Z8, Y1, Y2 = range(1, 7)
CORE_MASK = 1


def halves(value):
    high = value.astype(BF16)
    low = (value - high.astype(F32)).astype(BF16)
    return high, low


def mm(left, right, dims):
    left_high, left_low = halves(left)
    right_high, right_low = halves(right)
    dot = functools.partial(lax.dot_general, dimension_numbers=dims, preferred_element_type=F32)
    return dot(left_high, right_high) + (dot(left_high, right_low) + dot(left_low, right_high))


def pick_left(spread, value, dims):
    high, low = halves(value)
    rest = (value - high.astype(F32) - low.astype(F32)).astype(BF16)
    dot = functools.partial(lax.dot_general, spread, dimension_numbers=dims, preferred_element_type=F32)
    return dot(high) + (dot(low) + dot(rest))


def pick_right(value, spread, dims):
    high, low = halves(value)
    rest = (value - high.astype(F32) - low.astype(F32)).astype(BF16)
    dot = functools.partial(lax.dot_general, dimension_numbers=dims, preferred_element_type=F32)
    return dot(high, spread) + (dot(low, spread) + dot(rest, spread))


def swap(value, axis, mask):
    return lax.ppermute(value, axis, [(i, i ^ mask) for i in range(lax.axis_size(axis))])


def across(value, mask):
    return swap(value, "leaf", mask)


def grow(value, mask):
    return jnp.concatenate([value, across(value, mask)], axis=1)


def pair_starts(blocks):
    starts, running = [], 0
    for column in range(blocks):
        starts.append(running)
        running += blocks - 1 - column
    return starts


def placement(rows, offset, count, start, width):
    row = lax.broadcasted_iota(jnp.int32, (rows, width), 0)
    column = lax.broadcasted_iota(jnp.int32, (rows, width), 1)
    inside = (row >= offset) & (row < offset + count)
    return jnp.where(inside & (row - offset == column - start), 1.0, 0.0).astype(BF16)


def forward_kernel(sizes, where, pattern, rhs, inverse, blocks, coupling, sep_rhs, y_out, t_out):
    count, size = inverse.shape[0], inverse.shape[1]
    starts = pair_starts(count)
    pending = [rhs[i * size : (i + 1) * size, :] for i in range(count)]
    for column in range(count):
        solved = mm(inverse[column], pending[column], NN)
        y_out[column * size : (column + 1) * size, :] = solved
        for later in range(column + 1, count):
            pair = starts[column] + later - column - 1
            weight = pattern[0, pair].astype(F32)
            pending[later] = pending[later] - weight * mm(blocks[pair], solved, NN)
    last = y_out[(count - 1) * size :, :]
    right = sep_rhs[...]
    width = coupling.shape[1]
    offset = 0
    for level, rows in enumerate(sizes):
        spread = placement(right.shape[0], offset, rows, where[level], width)
        offset += rows
        t_out[:, level * width : (level + 1) * width] = pick_right(right, spread, TN) - mm(
            last, coupling[level * size : (level + 1) * size, :], TN
        )


def backward_kernel(sizes, where, pattern, y, near, across_core, inverse, blocks, coupling, out, sep_out):
    count, size = inverse.shape[0], inverse.shape[1]
    starts = pair_starts(count)
    width = coupling.shape[1]
    place = where[LEVELS]
    chunks = []
    for member in range(2 * near.shape[0]):
        apart = place ^ member
        chunks.append(jnp.where(apart % 2 == 1, across_core[apart // 2], near[apart // 2]))
    xs = jnp.concatenate(chunks, axis=0)
    correction = jnp.zeros((size, y.shape[1]), F32)
    padded = -(-sep_out.shape[0] // 8) * 8
    pieces = jnp.zeros((padded, y.shape[1]), F32)
    offset = 0
    for level, rows in enumerate(sizes):
        part = xs[:, level * width : (level + 1) * width]
        correction = correction + mm(coupling[level * size : (level + 1) * size, :], part, NT)
        spread = placement(padded, offset, rows, where[level], width)
        pieces = pieces + pick_left(spread, part, NT)
        offset += rows
    sep_out[...] = pieces[: sep_out.shape[0], :]
    pending = [y[i * size : (i + 1) * size, :] for i in range(count)]
    pending[-1] = pending[-1] - correction
    for column in reversed(range(count)):
        solved = mm(inverse[column], pending[column], TN)
        out[column * size : (column + 1) * size, :] = solved
        for earlier in reversed(range(column)):
            pair = starts[earlier] + column - earlier - 1
            weight = pattern[0, pair].astype(F32)
            pending[earlier] = pending[earlier] - weight * mm(blocks[pair], solved, TN)


def spots(start, count, turn=None):
    if turn is None:
        return [slice(start + r * 128, start + (r + 1) * 128) for r in range(count)]
    return [pl.ds(pl.multiple_of(start + (turn ^ r) * 128, 128), 128) for r in range(count)]


def times_rows(value, places, mats, index):
    result = []
    for half in mats:
        total = None
        for r, place in enumerate(places):
            term = mm(value[:, place], half[r, index], NT)
            total = term if total is None else total + term
        result.append(total)
    return result


def times_matrix(value, mats, index, r):
    total = None
    for piece, half in zip(value, mats):
        term = mm(piece, half[r, index], NN)
        total = term if total is None else total + term
    return total


def summed(parts, rows):
    total = None
    for part in parts:
        for start in range(0, part.shape[0], rows):
            term = part[start : start + rows, :]
            total = term if total is None else total + term
    return total


def level_kernel(index, turned, plane, *refs):
    mine, other, z_out, v_out = refs[-4:]
    mats = (mine, other)
    count, width = z_out.shape
    more = v_out.shape[1]
    heads = [ref for ref in refs[:-4] if ref.shape[1] in (width, width + more)]
    rests = [ref for ref in refs[:-4] if ref.shape[1] >= more and ref.shape[1] != width]
    places = spots(0, mine.shape[0], plane[0] if turned else None)
    z_out[...] = summed(heads, count)[:, :width]
    v_out[...] = summed(rests, count)[:, -more:]
    z = times_rows(z_out, places, mats, index)
    z_out[...] = jnp.concatenate(z, axis=1)
    for r, place in enumerate(places):
        v_out[:, place] = v_out[:, place] - times_matrix(z, mats, index + 1, r)


def top_kernel(plane, right, right_far, z1, z2, z3, m1, o1, m2, o2, m3, o3, x_out):
    width = right.shape[1]
    count = m3.shape[0]
    top = (m3, o3)
    z = times_rows(right[...] + right_far[...], spots(0, count), top, 0)
    order = [(z3, top, 1, None), (z2, (m2, o2), 0, None), (z1, (m1, o1), 0, plane[0])]
    mats, index, turn = top, 0, None
    level = 3
    while True:
        for r, place in enumerate(spots(level * width, count, turn)):
            x_out[:, place] = times_matrix(z, mats, index, r)
        if not order:
            break
        held, mats, index, turn = order.pop(0)
        moved = times_rows(x_out, spots(level * width, count, turn), mats, index + 1)
        half = held.shape[1] // 2
        z = [held[:, :half] - moved[0], held[:, half:] - moved[1]]
        level -= 1


SMEM = pl.BlockSpec(memory_space=pltpu.SMEM)
VMEM = pl.BlockSpec(memory_space=pltpu.VMEM)


def params():
    return pltpu.CompilerParams(vmem_limit_bytes=40 * 1024 * 1024)


def call(kernel, outs, *arrays):
    return pl.pallas_call(
        kernel,
        out_shape=[jax.ShapeDtypeStruct(s, F32) for s in outs],
        in_specs=[SMEM if v.dtype == jnp.int32 else VMEM for v in arrays],
        out_specs=[VMEM] * len(outs),
        compiler_params=params(),
    )(*arrays)


def shards(leaf_rhs, leaf_inverse, leaf_blocks, leaf_pattern, leaf_coupling, sep_rhs, sep_inverse, sep_coupling):
    position = lax.axis_index("leaf")
    columns = leaf_rhs.shape[1]
    width = leaf_coupling.shape[1]
    leaves = lax.axis_size("leaf")
    groups = [4, 16, 64, 128]
    sizes = [width // g for g in groups]
    offsets = [sum(sizes[:i]) for i in range(LEVELS)]
    where = jnp.stack([position % g * r for g, r in zip(groups, sizes)] + [position % 4]).astype(jnp.int32)

    def rows(array, level):
        return array[offsets[level] : offsets[level] + sizes[level]]

    def both(level):
        return jnp.stack([rows(sep_inverse, level), rows(sep_coupling, level)])

    def planes(value):
        count = lax.axis_size("col")
        return lax.all_to_all(jnp.broadcast_to(value[None], (count, *value.shape)), "col", 0, 0, tiled=True)

    tie = lax.optimization_barrier
    halves_z, wrap_z, wrap_y = 1 << Z4, (1 << Z8) | (1 << Z4), (1 << Y2) | (1 << Y1)
    near = [[g * 4 + m for m in range(4)] for g in range(leaves // 4)]
    plane = lax.axis_index("col").astype(jnp.int32)[None]

    def turned_planes(value):
        return jnp.stack([value] + [swap(value, "col", r) for r in range(1, lax.axis_size("col"))])

    def solve(index, turned, depth, *arrays):
        outs = [(columns // 4, width), (columns // 4, depth * width)]
        return call(functools.partial(level_kernel, index, turned), outs, plane, *arrays)

    first = grow(both(0), 1 << Z1)
    far = grow(rows(sep_inverse, 3)[None], wrap_y)
    y, t = call(
        functools.partial(forward_kernel, sizes),
        [leaf_rhs.shape, (columns, LEVELS * width)],
        where, leaf_pattern, leaf_rhs, leaf_inverse, leaf_blocks, leaf_coupling, sep_rhs,
    )
    t, first, far, second = tie((t, first, far, both(1)))

    t = lax.all_to_all(t, "leaf", 0, 0, axis_index_groups=near, tiled=True)
    far = grow(jnp.concatenate([far, both(2)], 0), 1 << Y1)
    second = grow(second, halves_z)
    first = turned_planes(first)
    far = grow(far, wrap_z)
    second = grow(second, 1 << Z2)
    t, first, far, second = tie((t, first, far, second))

    first = (first, across(first, CORE_MASK))
    second = grow(second, 1 << Z1)
    far = grow(far, halves_z)
    z1, v = solve(0, True, 3, t, *first)
    v_far = across(v, 1 << Z2)
    v, v_far, second, far = tie((v, v_far, second, far))

    second = planes(second)
    v = v + v_far
    v, upper = v[:, :width], v[:, width:]
    v_far = across(v, halves_z)
    far = grow(far, 1 << Z2)
    far, upper, v_far = tie((far, upper, v_far))

    upper_far = across(upper, halves_z)
    far = grow(far, 1 << Z1)
    far, second = tie((far, second))

    third = lax.all_gather(far, "col", axis=0)
    second = (second, across(second, CORE_MASK))
    z2, v = solve(0, False, 2, v, v_far, upper, upper_far, *second)
    v = v + across(v, wrap_z)
    v, third = tie((v, third))

    third = (third, across(third, CORE_MASK))
    z3, v = solve(1, False, 1, v, across(v, 1 << Y1), *third)
    (x,) = call(
        top_kernel, [(columns // 4, LEVELS * width)], plane, v, across(v, wrap_y), z1, z2, z3, *first, *second, *third
    )
    x = jnp.stack([x, across(x, 1 << Z1)])
    return call(
        functools.partial(backward_kernel, sizes),
        [leaf_rhs.shape, sep_rhs.shape],
        where, leaf_pattern, y, x, across(x, CORE_MASK), leaf_inverse, leaf_blocks, leaf_coupling,
    )


def solution(mesh):
    return jax.shard_map(
        shards,
        mesh=mesh,
        in_specs=(
            P("leaf", "col"),
            P("leaf", None, None),
            P("leaf", None, None),
            P("leaf", None),
            P("leaf", None),
            P("leaf", "col"),
            P("leaf", "col"),
            P("leaf", "col"),
        ),
        out_specs=(P("leaf", "col"), P("leaf", "col")),
        check_vma=False,
    )
```

```python
import functools

import jax
import jax.numpy as jnp
from jax import lax
from jax.experimental import pallas as pl
from jax.experimental.pallas import tpu as pltpu
from jax.sharding import PartitionSpec as P

F32 = jnp.float32
BF16 = jnp.bfloat16
NN = (((1,), (0,)), ((), ()))
NT = (((1,), (1,)), ((), ()))
TN = (((0,), (0,)), ((), ()))
LEVELS = 4
Z1, Z2, Z4, Z8, Y1, Y2 = range(1, 7)
CORE_MASK = 1


def halves(value):
    high = value.astype(BF16)
    low = (value - high.astype(F32)).astype(BF16)
    return high, low


def mm(left, right, dims):
    left_high, left_low = halves(left)
    right_high, right_low = halves(right)
    dot = functools.partial(lax.dot_general, dimension_numbers=dims, preferred_element_type=F32)
    return dot(left_high, right_high) + (dot(left_high, right_low) + dot(left_low, right_high))


def pick_left(spread, value, dims):
    high, low = halves(value)
    rest = (value - high.astype(F32) - low.astype(F32)).astype(BF16)
    dot = functools.partial(lax.dot_general, spread, dimension_numbers=dims, preferred_element_type=F32)
    return dot(high) + (dot(low) + dot(rest))


def pick_right(value, spread, dims):
    high, low = halves(value)
    rest = (value - high.astype(F32) - low.astype(F32)).astype(BF16)
    dot = functools.partial(lax.dot_general, dimension_numbers=dims, preferred_element_type=F32)
    return dot(high, spread) + (dot(low, spread) + dot(rest, spread))


def swap(value, axis, mask):
    return lax.ppermute(value, axis, [(i, i ^ mask) for i in range(lax.axis_size(axis))])


def across(value, mask):
    return swap(value, "leaf", mask)


def grow(value, mask):
    return jnp.concatenate([value, across(value, mask)], axis=1)


def pair_starts(blocks):
    starts, running = [], 0
    for column in range(blocks):
        starts.append(running)
        running += blocks - 1 - column
    return starts


def placement(rows, offset, count, start, width):
    row = lax.broadcasted_iota(jnp.int32, (rows, width), 0)
    column = lax.broadcasted_iota(jnp.int32, (rows, width), 1)
    inside = (row >= offset) & (row < offset + count)
    return jnp.where(inside & (row - offset == column - start), 1.0, 0.0).astype(BF16)


def forward_kernel(sizes, where, pattern, rhs, inverse, blocks, coupling, sep_rhs, y_out, t_out):
    count, size = inverse.shape[0], inverse.shape[1]
    starts = pair_starts(count)
    pending = [rhs[i * size : (i + 1) * size, :] for i in range(count)]
    for column in range(count):
        solved = mm(inverse[column], pending[column], NN)
        y_out[column * size : (column + 1) * size, :] = solved
        for later in range(column + 1, count):
            pair = starts[column] + later - column - 1
            weight = pattern[0, pair].astype(F32)
            pending[later] = pending[later] - weight * mm(blocks[pair], solved, NN)
    last = y_out[(count - 1) * size :, :]
    right = sep_rhs[...]
    width = coupling.shape[1]
    offset = 0
    for level, rows in enumerate(sizes):
        spread = placement(right.shape[0], offset, rows, where[level], width)
        offset += rows
        t_out[:, level * width : (level + 1) * width] = pick_right(right, spread, TN) - mm(
            last, coupling[level * size : (level + 1) * size, :], TN
        )


def backward_kernel(sizes, where, pattern, y, near, across_core, inverse, blocks, coupling, out, sep_out):
    count, size = inverse.shape[0], inverse.shape[1]
    starts = pair_starts(count)
    width = coupling.shape[1]
    place = where[LEVELS]
    chunks = []
    for member in range(2 * near.shape[0]):
        apart = place ^ member
        chunks.append(jnp.where(apart % 2 == 1, across_core[apart // 2], near[apart // 2]))
    xs = jnp.concatenate(chunks, axis=0)
    correction = jnp.zeros((size, y.shape[1]), F32)
    padded = -(-sep_out.shape[0] // 8) * 8
    pieces = jnp.zeros((padded, y.shape[1]), F32)
    offset = 0
    for level, rows in enumerate(sizes):
        part = xs[:, level * width : (level + 1) * width]
        correction = correction + mm(coupling[level * size : (level + 1) * size, :], part, NT)
        spread = placement(padded, offset, rows, where[level], width)
        pieces = pieces + pick_left(spread, part, NT)
        offset += rows
    sep_out[...] = pieces[: sep_out.shape[0], :]
    pending = [y[i * size : (i + 1) * size, :] for i in range(count)]
    pending[-1] = pending[-1] - correction
    for column in reversed(range(count)):
        solved = mm(inverse[column], pending[column], TN)
        out[column * size : (column + 1) * size, :] = solved
        for earlier in reversed(range(column)):
            pair = starts[earlier] + column - earlier - 1
            weight = pattern[0, pair].astype(F32)
            pending[earlier] = pending[earlier] - weight * mm(blocks[pair], solved, TN)


def spots(start, count, turn=None):
    if turn is None:
        return [slice(start + r * 128, start + (r + 1) * 128) for r in range(count)]
    return [pl.ds(pl.multiple_of(start + (turn ^ r) * 128, 128), 128) for r in range(count)]


def times_rows(value, places, mats, index):
    result = []
    for half in mats:
        total = None
        for r, place in enumerate(places):
            term = mm(value[:, place], half[r, index], NT)
            total = term if total is None else total + term
        result.append(total)
    return result


def times_matrix(value, mats, index, r):
    total = None
    for piece, half in zip(value, mats):
        term = mm(piece, half[r, index], NN)
        total = term if total is None else total + term
    return total


def summed(parts, rows):
    total = None
    for part in parts:
        for start in range(0, part.shape[0], rows):
            term = part[start : start + rows, :]
            total = term if total is None else total + term
    return total


def level_kernel(index, turned, plane, *refs):
    mine, other, z_out, v_out = refs[-4:]
    mats = (mine, other)
    count, width = z_out.shape
    more = v_out.shape[1]
    both = [ref for ref in refs[:-4] if ref.shape[1] >= width + more]
    heads = [ref for ref in refs[:-4] if ref.shape[1] == width]
    rests = [ref for ref in refs[:-4] if width < ref.shape[1] < width + more]
    places = spots(0, mine.shape[0], plane[0] if turned else None)
    z_out[...] = summed([ref[:, :width] for ref in both] + heads, count)
    v_out[...] = summed([ref[:, width : width + more] for ref in both] + rests, count)
    z = times_rows(z_out, places, mats, index)
    z_out[...] = jnp.concatenate(z, axis=1)
    for r, place in enumerate(places):
        v_out[:, place] = v_out[:, place] - times_matrix(z, mats, index + 1, r)


def top_kernel(plane, right, right_far, z1, z2, z3, m1, o1, m2, o2, m3, o3, x_out):
    width = right.shape[1]
    count = m3.shape[0]
    top = (m3, o3)
    z = times_rows(right[...] + right_far[...], spots(0, count), top, 0)
    order = [(z3, top, 1, None), (z2, (m2, o2), 0, None), (z1, (m1, o1), 0, plane[0])]
    mats, index, turn = top, 0, None
    level = 3
    while True:
        for r, place in enumerate(spots(level * width, count, turn)):
            x_out[:, place] = times_matrix(z, mats, index, r)
        if not order:
            break
        held, mats, index, turn = order.pop(0)
        moved = times_rows(x_out, spots(level * width, count, turn), mats, index + 1)
        half = held.shape[1] // 2
        z = [held[:, :half] - moved[0], held[:, half:] - moved[1]]
        level -= 1


SMEM = pl.BlockSpec(memory_space=pltpu.SMEM)
VMEM = pl.BlockSpec(memory_space=pltpu.VMEM)


def params():
    return pltpu.CompilerParams(vmem_limit_bytes=40 * 1024 * 1024)


def call(kernel, outs, *arrays):
    return pl.pallas_call(
        kernel,
        out_shape=[jax.ShapeDtypeStruct(s, F32) for s in outs],
        in_specs=[SMEM if v.dtype == jnp.int32 else VMEM for v in arrays],
        out_specs=[VMEM] * len(outs),
        compiler_params=params(),
    )(*arrays)


def shards(leaf_rhs, leaf_inverse, leaf_blocks, leaf_pattern, leaf_coupling, sep_rhs, sep_inverse, sep_coupling):
    position = lax.axis_index("leaf")
    columns = leaf_rhs.shape[1]
    width = leaf_coupling.shape[1]
    leaves = lax.axis_size("leaf")
    groups = [4, 16, 64, 128]
    sizes = [width // g for g in groups]
    offsets = [sum(sizes[:i]) for i in range(LEVELS)]
    where = jnp.stack([position % g * r for g, r in zip(groups, sizes)] + [position % 4]).astype(jnp.int32)

    def rows(array, level):
        return array[offsets[level] : offsets[level] + sizes[level]]

    def both(level):
        return jnp.stack([rows(sep_inverse, level), rows(sep_coupling, level)])

    def planes(value):
        count = lax.axis_size("col")
        return lax.all_to_all(jnp.broadcast_to(value[None], (count, *value.shape)), "col", 0, 0, tiled=True)

    tie = lax.optimization_barrier
    halves_z, wrap_z, wrap_y = 1 << Z4, (1 << Z8) | (1 << Z4), (1 << Y2) | (1 << Y1)
    near = [[g * 4 + m for m in range(4)] for g in range(leaves // 4)]
    plane = lax.axis_index("col").astype(jnp.int32)[None]

    def turned_planes(value):
        return jnp.stack([value] + [swap(value, "col", r) for r in range(1, lax.axis_size("col"))])

    def solve(index, turned, depth, *arrays):
        outs = [(columns // 4, width), (columns // 4, depth * width)]
        return call(functools.partial(level_kernel, index, turned), outs, plane, *arrays)

    first = grow(both(0), 1 << Z1)
    far = grow(rows(sep_inverse, 3)[None], wrap_y)
    y, t = call(
        functools.partial(forward_kernel, sizes),
        [leaf_rhs.shape, (columns, LEVELS * width)],
        where, leaf_pattern, leaf_rhs, leaf_inverse, leaf_blocks, leaf_coupling, sep_rhs,
    )
    t, first, far, second = tie((t, first, far, both(1)))

    t = lax.all_to_all(t, "leaf", 0, 0, axis_index_groups=near, tiled=True)
    far = grow(jnp.concatenate([far, both(2)], 0), 1 << Y1)
    second = grow(second, halves_z)
    first = turned_planes(first)
    far = grow(far, wrap_z)
    second = grow(second, 1 << Z2)
    t, first, far, second = tie((t, first, far, second))

    upper = t[:, 2 * width :].reshape(4, columns // 4, 2 * width).sum(0)
    upper_far = across(upper, 1 << Z2)
    first = (first, across(first, CORE_MASK))
    second = grow(second, 1 << Z1)
    far = grow(far, halves_z)
    upper, upper_far, far = tie((upper, upper_far, far))
    upper = upper + upper_far
    upper_far = across(upper, halves_z)
    z1, v = solve(0, True, 1, t, *first)
    v_far = across(v, 1 << Z2)
    v, v_far, second, far, upper, upper_far = tie((v, v_far, second, far, upper, upper_far))

    second = planes(second)
    v = v + v_far
    v_far = across(v, halves_z)
    far = grow(far, 1 << Z2)
    far, v_far = tie((far, v_far))

    far = grow(far, 1 << Z1)
    far, second = tie((far, second))

    third = lax.all_gather(far, "col", axis=0)
    second = (second, across(second, CORE_MASK))
    z2, v = solve(0, False, 2, v, v_far, upper, upper_far, *second)
    v = v + across(v, wrap_z)
    v, third = tie((v, third))

    third = (third, across(third, CORE_MASK))
    z3, v = solve(1, False, 1, v, across(v, 1 << Y1), *third)
    (x,) = call(
        top_kernel, [(columns // 4, LEVELS * width)], plane, v, across(v, wrap_y), z1, z2, z3, *first, *second, *third
    )
    x = jnp.stack([x, across(x, 1 << Z1)])
    return call(
        functools.partial(backward_kernel, sizes),
        [leaf_rhs.shape, sep_rhs.shape],
        where, leaf_pattern, y, x, across(x, CORE_MASK), leaf_inverse, leaf_blocks, leaf_coupling,
    )


def solution(mesh):
    return jax.shard_map(
        shards,
        mesh=mesh,
        in_specs=(
            P("leaf", "col"),
            P("leaf", None, None),
            P("leaf", None, None),
            P("leaf", None),
            P("leaf", None),
            P("leaf", "col"),
            P("leaf", "col"),
            P("leaf", "col"),
        ),
        out_specs=(P("leaf", "col"), P("leaf", "col")),
        check_vma=False,
    )
```

```python
import functools

import jax
import jax.numpy as jnp
from jax import lax
from jax.experimental import pallas as pl
from jax.experimental.pallas import tpu as pltpu
from jax.sharding import PartitionSpec as P

F32 = jnp.float32
BF16 = jnp.bfloat16
NN = (((1,), (0,)), ((), ()))
NT = (((1,), (1,)), ((), ()))
TN = (((0,), (0,)), ((), ()))
LEVELS = 4
Z1, Z2, Z4, Z8, Y1, Y2 = range(1, 7)
CORE_MASK = 1


def halves(value):
    high = value.astype(BF16)
    low = (value - high.astype(F32)).astype(BF16)
    return high, low


def mm(left, right, dims):
    left_high, left_low = halves(left)
    right_high, right_low = halves(right)
    dot = functools.partial(lax.dot_general, dimension_numbers=dims, preferred_element_type=F32)
    return dot(left_high, right_high) + (dot(left_high, right_low) + dot(left_low, right_high))


def pick_left(spread, value, dims):
    high, low = halves(value)
    rest = (value - high.astype(F32) - low.astype(F32)).astype(BF16)
    dot = functools.partial(lax.dot_general, spread, dimension_numbers=dims, preferred_element_type=F32)
    return dot(high) + (dot(low) + dot(rest))


def pick_right(value, spread, dims):
    high, low = halves(value)
    rest = (value - high.astype(F32) - low.astype(F32)).astype(BF16)
    dot = functools.partial(lax.dot_general, dimension_numbers=dims, preferred_element_type=F32)
    return dot(high, spread) + (dot(low, spread) + dot(rest, spread))


def swap(value, axis, mask):
    return lax.ppermute(value, axis, [(i, i ^ mask) for i in range(lax.axis_size(axis))])


def across(value, mask):
    return swap(value, "leaf", mask)


def grow(value, mask):
    return jnp.concatenate([value, across(value, mask)], axis=1)


def pair_starts(blocks):
    starts, running = [], 0
    for column in range(blocks):
        starts.append(running)
        running += blocks - 1 - column
    return starts


def placement(rows, offset, count, start, width):
    row = lax.broadcasted_iota(jnp.int32, (rows, width), 0)
    column = lax.broadcasted_iota(jnp.int32, (rows, width), 1)
    inside = (row >= offset) & (row < offset + count)
    return jnp.where(inside & (row - offset == column - start), 1.0, 0.0).astype(BF16)


def forward_kernel(sizes, where, pattern, rhs, inverse, blocks, coupling, sep_rhs, y_out, t_out):
    count, size = inverse.shape[0], inverse.shape[1]
    starts = pair_starts(count)
    pending = [rhs[i * size : (i + 1) * size, :] for i in range(count)]
    for column in range(count):
        solved = mm(inverse[column], pending[column], NN)
        y_out[column * size : (column + 1) * size, :] = solved
        for later in range(column + 1, count):
            pair = starts[column] + later - column - 1
            weight = pattern[0, pair].astype(F32)
            pending[later] = pending[later] - weight * mm(blocks[pair], solved, NN)
    last = y_out[(count - 1) * size :, :]
    right = sep_rhs[...]
    width = coupling.shape[1]
    offset = 0
    for level, rows in enumerate(sizes):
        spread = placement(right.shape[0], offset, rows, where[level], width)
        offset += rows
        t_out[:, level * width : (level + 1) * width] = pick_right(right, spread, TN) - mm(
            last, coupling[level * size : (level + 1) * size, :], TN
        )


def backward_kernel(sizes, where, pattern, y, near, across_core, inverse, blocks, coupling, out, sep_out):
    count, size = inverse.shape[0], inverse.shape[1]
    starts = pair_starts(count)
    width = coupling.shape[1]
    place = where[LEVELS]
    chunks = []
    for member in range(2 * near.shape[0]):
        apart = place ^ member
        chunks.append(jnp.where(apart % 2 == 1, across_core[apart // 2], near[apart // 2]))
    xs = jnp.concatenate(chunks, axis=0)
    correction = jnp.zeros((size, y.shape[1]), F32)
    padded = -(-sep_out.shape[0] // 8) * 8
    pieces = jnp.zeros((padded, y.shape[1]), F32)
    offset = 0
    for level, rows in enumerate(sizes):
        part = xs[:, level * width : (level + 1) * width]
        correction = correction + mm(coupling[level * size : (level + 1) * size, :], part, NT)
        spread = placement(padded, offset, rows, where[level], width)
        pieces = pieces + pick_left(spread, part, NT)
        offset += rows
    sep_out[...] = pieces[: sep_out.shape[0], :]
    pending = [y[i * size : (i + 1) * size, :] for i in range(count)]
    pending[-1] = pending[-1] - correction
    for column in reversed(range(count)):
        solved = mm(inverse[column], pending[column], TN)
        out[column * size : (column + 1) * size, :] = solved
        for earlier in reversed(range(column)):
            pair = starts[earlier] + column - earlier - 1
            weight = pattern[0, pair].astype(F32)
            pending[earlier] = pending[earlier] - weight * mm(blocks[pair], solved, TN)


def spots(start, count):
    return [slice(start + r * 128, start + (r + 1) * 128) for r in range(count)]


def times_rows(value, places, mats, index):
    result = []
    for half in mats:
        total = None
        for r, place in enumerate(places):
            term = mm(value[:, place], half[r, index], NT)
            total = term if total is None else total + term
        result.append(total)
    return result


def times_matrix(value, mats, index, r):
    total = None
    for piece, half in zip(value, mats):
        term = mm(piece, half[r, index], NN)
        total = term if total is None else total + term
    return total


def summed(parts, rows):
    total = None
    for part in parts:
        for start in range(0, part.shape[0], rows):
            term = part[start : start + rows, :]
            total = term if total is None else total + term
    return total


def level_kernel(index, *refs):
    mine, other, z_out, v_out = refs[-4:]
    mats = (mine, other)
    count, width = z_out.shape
    more = v_out.shape[1]
    both = [ref for ref in refs[:-4] if ref.shape[1] >= width + more]
    heads = [ref for ref in refs[:-4] if ref.shape[1] == width]
    rests = [ref for ref in refs[:-4] if width < ref.shape[1] < width + more]
    places = spots(0, mine.shape[0])
    z_out[...] = summed([ref[:, :width] for ref in both] + heads, count)
    v_out[...] = summed([ref[:, width : width + more] for ref in both] + rests, count)
    z = times_rows(z_out, places, mats, index)
    z_out[...] = jnp.concatenate(z, axis=1)
    for r, place in enumerate(places):
        v_out[:, place] = v_out[:, place] - times_matrix(z, mats, index + 1, r)


def top_kernel(right, right_far, z1, z2, z3, m1, o1, m2, o2, m3, o3, x_out):
    width = right.shape[1]
    count = m3.shape[0]
    top = (m3, o3)
    z = times_rows(right[...] + right_far[...], spots(0, count), top, 0)
    order = [(z3, top, 1), (z2, (m2, o2), 0), (z1, (m1, o1), 0)]
    mats, index = top, 0
    level = 3
    while True:
        for r, place in enumerate(spots(level * width, count)):
            x_out[:, place] = times_matrix(z, mats, index, r)
        if not order:
            break
        held, mats, index = order.pop(0)
        moved = times_rows(x_out, spots(level * width, count), mats, index + 1)
        half = held.shape[1] // 2
        z = [held[:, :half] - moved[0], held[:, half:] - moved[1]]
        level -= 1


SMEM = pl.BlockSpec(memory_space=pltpu.SMEM)
VMEM = pl.BlockSpec(memory_space=pltpu.VMEM)


def params():
    return pltpu.CompilerParams(vmem_limit_bytes=40 * 1024 * 1024)


def call(kernel, outs, *arrays):
    return pl.pallas_call(
        kernel,
        out_shape=[jax.ShapeDtypeStruct(s, F32) for s in outs],
        in_specs=[SMEM if v.dtype == jnp.int32 else VMEM for v in arrays],
        out_specs=[VMEM] * len(outs),
        compiler_params=params(),
    )(*arrays)


def shards(leaf_rhs, leaf_inverse, leaf_blocks, leaf_pattern, leaf_coupling, sep_rhs, sep_inverse, sep_coupling):
    position = lax.axis_index("leaf")
    columns = leaf_rhs.shape[1]
    width = leaf_coupling.shape[1]
    leaves = lax.axis_size("leaf")
    groups = [4, 16, 64, 128]
    sizes = [width // g for g in groups]
    offsets = [sum(sizes[:i]) for i in range(LEVELS)]
    where = jnp.stack([position % g * r for g, r in zip(groups, sizes)] + [position % 4]).astype(jnp.int32)

    def rows(array, level):
        return array[offsets[level] : offsets[level] + sizes[level]]

    def both(level):
        return jnp.stack([rows(sep_inverse, level), rows(sep_coupling, level)])

    def planes(value):
        count = lax.axis_size("col")
        return lax.all_to_all(jnp.broadcast_to(value[None], (count, *value.shape)), "col", 0, 0, tiled=True)

    tie = lax.optimization_barrier
    halves_z, wrap_z, wrap_y = 1 << Z4, (1 << Z8) | (1 << Z4), (1 << Y2) | (1 << Y1)
    near = [[g * 4 + m for m in range(4)] for g in range(leaves // 4)]
    def solve(index, depth, *arrays):
        outs = [(columns // 4, width), (columns // 4, depth * width)]
        return call(functools.partial(level_kernel, index), outs, *arrays)

    first = grow(both(0), 1 << Z1)
    far = grow(rows(sep_inverse, 3)[None], wrap_y)
    first = lax.all_gather(first, "col", axis=0)
    y, t = call(
        functools.partial(forward_kernel, sizes),
        [leaf_rhs.shape, (columns, LEVELS * width)],
        where, leaf_pattern, leaf_rhs, leaf_inverse, leaf_blocks, leaf_coupling, sep_rhs,
    )
    t, far, second = tie((t, far, both(1)))

    t = lax.all_to_all(t, "leaf", 0, 0, axis_index_groups=near, tiled=True)
    far = grow(jnp.concatenate([far, both(2)], 0), 1 << Y1)
    second = grow(second, halves_z)
    far = grow(far, wrap_z)
    second = grow(second, 1 << Z2)
    t, first, far, second = tie((t, first, far, second))

    first = (first, across(first, CORE_MASK))
    second = grow(second, 1 << Z1)
    far = grow(grow(far, halves_z), 1 << Z2)
    z1, v = solve(0, 3, t, *first)
    v_far = across(v, 1 << Z2)
    v, v_far, second, far = tie((v, v_far, second, far))

    second = planes(second)
    v = v + v_far
    v_far = across(v, halves_z)
    far = grow(far, 1 << Z1)
    far, v_far, second = tie((far, v_far, second))

    third = lax.all_gather(far, "col", axis=0)
    second = (second, across(second, CORE_MASK))
    z2, v = solve(0, 2, v, v_far, *second)
    v = v + across(v, wrap_z)
    v, third = tie((v, third))

    third = (third, across(third, CORE_MASK))
    z3, v = solve(1, 1, v, across(v, 1 << Y1), *third)
    (x,) = call(
        top_kernel, [(columns // 4, LEVELS * width)], v, across(v, wrap_y), z1, z2, z3, *first, *second, *third
    )
    x = jnp.stack([x, across(x, 1 << Z1)])
    return call(
        functools.partial(backward_kernel, sizes),
        [leaf_rhs.shape, sep_rhs.shape],
        where, leaf_pattern, y, x, across(x, CORE_MASK), leaf_inverse, leaf_blocks, leaf_coupling,
    )


def solution(mesh):
    return jax.shard_map(
        shards,
        mesh=mesh,
        in_specs=(
            P("leaf", "col"),
            P("leaf", None, None),
            P("leaf", None, None),
            P("leaf", None),
            P("leaf", None),
            P("leaf", "col"),
            P("leaf", "col"),
            P("leaf", "col"),
        ),
        out_specs=(P("leaf", "col"), P("leaf", "col")),
        check_vma=False,
    )
```

```python
import functools

import jax
import jax.numpy as jnp
from jax import lax
from jax.experimental import pallas as pl
from jax.experimental.pallas import tpu as pltpu
from jax.sharding import PartitionSpec as P

F32 = jnp.float32
BF16 = jnp.bfloat16
NN = (((1,), (0,)), ((), ()))
NT = (((1,), (1,)), ((), ()))
TN = (((0,), (0,)), ((), ()))
LEVELS = 4
Z1, Z2, Z4, Z8, Y1, Y2 = range(1, 7)
CORE_MASK = 1


def halves(value):
    high = value.astype(BF16)
    low = (value - high.astype(F32)).astype(BF16)
    return high, low


def mm(left, right, dims):
    left_high, left_low = halves(left)
    right_high, right_low = halves(right)
    dot = functools.partial(lax.dot_general, dimension_numbers=dims, preferred_element_type=F32)
    return dot(left_high, right_high) + (dot(left_high, right_low) + dot(left_low, right_high))


def pick_left(spread, value, dims):
    high, low = halves(value)
    rest = (value - high.astype(F32) - low.astype(F32)).astype(BF16)
    dot = functools.partial(lax.dot_general, spread, dimension_numbers=dims, preferred_element_type=F32)
    return dot(high) + (dot(low) + dot(rest))


def pick_right(value, spread, dims):
    high, low = halves(value)
    rest = (value - high.astype(F32) - low.astype(F32)).astype(BF16)
    dot = functools.partial(lax.dot_general, dimension_numbers=dims, preferred_element_type=F32)
    return dot(high, spread) + (dot(low, spread) + dot(rest, spread))


def swap(value, axis, mask):
    return lax.ppermute(value, axis, [(i, i ^ mask) for i in range(lax.axis_size(axis))])


def across(value, mask):
    return swap(value, "leaf", mask)


def grow(value, mask):
    return jnp.concatenate([value, across(value, mask)], axis=1)


def pair_starts(blocks):
    starts, running = [], 0
    for column in range(blocks):
        starts.append(running)
        running += blocks - 1 - column
    return starts


def placement(rows, offset, count, start, width):
    row = lax.broadcasted_iota(jnp.int32, (rows, width), 0)
    column = lax.broadcasted_iota(jnp.int32, (rows, width), 1)
    inside = (row >= offset) & (row < offset + count)
    return jnp.where(inside & (row - offset == column - start), 1.0, 0.0).astype(BF16)


def forward_kernel(sizes, where, pattern, rhs, inverse, blocks, coupling, sep_rhs, y_out, t_out):
    count, size = inverse.shape[0], inverse.shape[1]
    starts = pair_starts(count)
    pending = [rhs[i * size : (i + 1) * size, :] for i in range(count)]
    for column in range(count):
        solved = mm(inverse[column], pending[column], NN)
        y_out[column * size : (column + 1) * size, :] = solved
        for later in range(column + 1, count):
            pair = starts[column] + later - column - 1
            weight = pattern[0, pair].astype(F32)
            pending[later] = pending[later] - weight * mm(blocks[pair], solved, NN)
    last = y_out[(count - 1) * size :, :]
    right = sep_rhs[...]
    width = coupling.shape[1]
    offset = 0
    for level, rows in enumerate(sizes):
        spread = placement(right.shape[0], offset, rows, where[level], width)
        offset += rows
        t_out[:, level * width : (level + 1) * width] = pick_right(right, spread, TN) - mm(
            last, coupling[level * size : (level + 1) * size, :], TN
        )


def backward_kernel(sizes, where, pattern, y, near, across_core, inverse, blocks, coupling, out, sep_out):
    count, size = inverse.shape[0], inverse.shape[1]
    starts = pair_starts(count)
    width = coupling.shape[1]
    place = where[LEVELS]
    chunks = []
    for member in range(2 * near.shape[0]):
        apart = place ^ member
        chunks.append(jnp.where(apart % 2 == 1, across_core[apart // 2], near[apart // 2]))
    xs = jnp.concatenate(chunks, axis=0)
    correction = jnp.zeros((size, y.shape[1]), F32)
    padded = -(-sep_out.shape[0] // 8) * 8
    pieces = jnp.zeros((padded, y.shape[1]), F32)
    offset = 0
    for level, rows in enumerate(sizes):
        part = xs[:, level * width : (level + 1) * width]
        correction = correction + mm(coupling[level * size : (level + 1) * size, :], part, NT)
        spread = placement(padded, offset, rows, where[level], width)
        pieces = pieces + pick_left(spread, part, NT)
        offset += rows
    sep_out[...] = pieces[: sep_out.shape[0], :]
    pending = [y[i * size : (i + 1) * size, :] for i in range(count)]
    pending[-1] = pending[-1] - correction
    for column in reversed(range(count)):
        solved = mm(inverse[column], pending[column], TN)
        out[column * size : (column + 1) * size, :] = solved
        for earlier in reversed(range(column)):
            pair = starts[earlier] + column - earlier - 1
            weight = pattern[0, pair].astype(F32)
            pending[earlier] = pending[earlier] - weight * mm(blocks[pair], solved, TN)


def spots(start, count, turn=None):
    if turn is None:
        return [slice(start + r * 128, start + (r + 1) * 128) for r in range(count)]
    return [pl.ds(pl.multiple_of(start + (turn ^ r) * 128, 128), 128) for r in range(count)]


def times_rows(value, places, mats, index):
    result = []
    for half in mats:
        total = None
        for r, place in enumerate(places):
            term = mm(value[:, place], half[r, index], NT)
            total = term if total is None else total + term
        result.append(total)
    return result


def times_matrix(value, mats, index, r):
    total = None
    for piece, half in zip(value, mats):
        term = mm(piece, half[r, index], NN)
        total = term if total is None else total + term
    return total


def summed(parts, rows):
    total = None
    for part in parts:
        for start in range(0, part.shape[0], rows):
            term = part[start : start + rows, :]
            total = term if total is None else total + term
    return total


def level_kernel(index, turned, plane, *refs):
    mine, other, z_out, v_out = refs[-4:]
    mats = (mine, other)
    count, width = z_out.shape
    more = v_out.shape[1]
    both = [ref for ref in refs[:-4] if ref.shape[1] >= width + more]
    heads = [ref for ref in refs[:-4] if ref.shape[1] == width]
    rests = [ref for ref in refs[:-4] if width < ref.shape[1] < width + more]
    places = spots(0, mine.shape[0], plane[0] if turned else None)
    z_out[...] = summed([ref[:, :width] for ref in both] + heads, count)
    v_out[...] = summed([ref[:, width : width + more] for ref in both] + rests, count)
    z = times_rows(z_out, places, mats, index)
    z_out[...] = jnp.concatenate(z, axis=1)
    for r, place in enumerate(places):
        v_out[:, place] = v_out[:, place] - times_matrix(z, mats, index + 1, r)


def top_kernel(plane, right, right_far, z1, z2, z3, m1, o1, m2, o2, m3, o3, x_out):
    width = right.shape[1]
    count = m3.shape[0]
    top = (m3, o3)
    z = times_rows(right[...] + right_far[...], spots(0, count), top, 0)
    order = [(z3, top, 1, None), (z2, (m2, o2), 0, None), (z1, (m1, o1), 0, plane[0])]
    mats, index, turn = top, 0, None
    level = 3
    while True:
        for r, place in enumerate(spots(level * width, count, turn)):
            x_out[:, place] = times_matrix(z, mats, index, r)
        if not order:
            break
        held, mats, index, turn = order.pop(0)
        moved = times_rows(x_out, spots(level * width, count, turn), mats, index + 1)
        half = held.shape[1] // 2
        z = [held[:, :half] - moved[0], held[:, half:] - moved[1]]
        level -= 1


SMEM = pl.BlockSpec(memory_space=pltpu.SMEM)
VMEM = pl.BlockSpec(memory_space=pltpu.VMEM)


def params():
    return pltpu.CompilerParams(vmem_limit_bytes=40 * 1024 * 1024)


def call(kernel, outs, *arrays):
    return pl.pallas_call(
        kernel,
        out_shape=[jax.ShapeDtypeStruct(s, F32) for s in outs],
        in_specs=[SMEM if v.dtype == jnp.int32 else VMEM for v in arrays],
        out_specs=[VMEM] * len(outs),
        compiler_params=params(),
    )(*arrays)


def shards(leaf_rhs, leaf_inverse, leaf_blocks, leaf_pattern, leaf_coupling, sep_rhs, sep_inverse, sep_coupling):
    position = lax.axis_index("leaf")
    columns = leaf_rhs.shape[1]
    width = leaf_coupling.shape[1]
    leaves = lax.axis_size("leaf")
    groups = [4, 16, 64, 128]
    sizes = [width // g for g in groups]
    offsets = [sum(sizes[:i]) for i in range(LEVELS)]
    where = jnp.stack([position % g * r for g, r in zip(groups, sizes)] + [position % 4]).astype(jnp.int32)

    def rows(array, level):
        return array[offsets[level] : offsets[level] + sizes[level]]

    def both(level):
        return jnp.stack([rows(sep_inverse, level), rows(sep_coupling, level)])

    def planes(value):
        count = lax.axis_size("col")
        return lax.all_to_all(jnp.broadcast_to(value[None], (count, *value.shape)), "col", 0, 0, tiled=True)

    tie = lax.optimization_barrier
    halves_z, wrap_z, wrap_y = 1 << Z4, (1 << Z8) | (1 << Z4), (1 << Y2) | (1 << Y1)
    near = [[g * 4 + m for m in range(4)] for g in range(leaves // 4)]
    plane = lax.axis_index("col").astype(jnp.int32)[None]

    def turned_planes(value):
        return jnp.stack([value] + [swap(value, "col", r) for r in range(1, lax.axis_size("col"))])

    def solve(index, turned, depth, *arrays):
        outs = [(columns // 4, width), (columns // 4, depth * width)]
        return call(functools.partial(level_kernel, index, turned), outs, plane, *arrays)

    first = grow(both(0), 1 << Z1)
    far = grow(rows(sep_inverse, 3)[None], wrap_y)
    y, t = call(
        functools.partial(forward_kernel, sizes),
        [leaf_rhs.shape, (columns, LEVELS * width)],
        where, leaf_pattern, leaf_rhs, leaf_inverse, leaf_blocks, leaf_coupling, sep_rhs,
    )
    t, first, far = tie((t, first, far))

    t = lax.all_to_all(t, "leaf", 0, 0, axis_index_groups=near, tiled=True)
    first = turned_planes(first)
    far = grow(jnp.concatenate([far, both(2)], 0), 1 << Y1)
    far = grow(far, wrap_z)
    t, first, far = tie((t, first, far))

    first = (first, across(first, CORE_MASK))
    upper = t[:, 2 * width :].reshape(4, columns // 4, 2 * width).sum(0)
    upper_far = across(upper, 1 << Z2)
    far = grow(jnp.concatenate([far, both(1)], 0), halves_z)
    z1, v = solve(0, True, 1, t, *first)
    v, far, upper, upper_far = tie((v, far, upper, upper_far))

    upper = upper + upper_far
    v_far = across(v, 1 << Z2)
    upper_far = across(upper, halves_z)
    far = grow(grow(far, 1 << Z2), 1 << Z1)
    v = v + v_far
    far, v, upper, upper_far = tie((far, v, upper, upper_far))

    second, third = far[3:], far[:3]
    second = planes(second)
    v_far = across(v, halves_z)
    second, third, v_far = tie((second, third, v_far))

    third = lax.all_gather(third, "col", axis=0)
    second = (second, across(second, CORE_MASK))
    z2, v = solve(0, False, 2, v, v_far, upper, upper_far, *second)
    v = v + across(v, wrap_z)
    v, third = tie((v, third))

    third = (third, across(third, CORE_MASK))
    z3, v = solve(1, False, 1, v, across(v, 1 << Y1), *third)
    (x,) = call(
        top_kernel, [(columns // 4, LEVELS * width)], plane, v, across(v, wrap_y), z1, z2, z3, *first, *second, *third
    )
    x = jnp.stack([x, across(x, 1 << Z1)])
    return call(
        functools.partial(backward_kernel, sizes),
        [leaf_rhs.shape, sep_rhs.shape],
        where, leaf_pattern, y, x, across(x, CORE_MASK), leaf_inverse, leaf_blocks, leaf_coupling,
    )


def solution(mesh):
    return jax.shard_map(
        shards,
        mesh=mesh,
        in_specs=(
            P("leaf", "col"),
            P("leaf", None, None),
            P("leaf", None, None),
            P("leaf", None),
            P("leaf", None),
            P("leaf", "col"),
            P("leaf", "col"),
            P("leaf", "col"),
        ),
        out_specs=(P("leaf", "col"), P("leaf", "col")),
        check_vma=False,
    )
```

```python
import functools

import jax
import jax.numpy as jnp
from jax import lax
from jax.experimental import pallas as pl
from jax.experimental.pallas import tpu as pltpu
from jax.sharding import PartitionSpec as P

F32 = jnp.float32
BF16 = jnp.bfloat16
NN = (((1,), (0,)), ((), ()))
NT = (((1,), (1,)), ((), ()))
TN = (((0,), (0,)), ((), ()))
LEVELS = 4
Z1, Z2, Z4, Z8, Y1, Y2 = range(1, 7)
CORE_MASK = 1


def halves(value):
    high = value.astype(BF16)
    low = (value - high.astype(F32)).astype(BF16)
    return high, low


def mm(left, right, dims):
    left_high, left_low = halves(left)
    right_high, right_low = halves(right)
    dot = functools.partial(lax.dot_general, dimension_numbers=dims, preferred_element_type=F32)
    return dot(left_high, right_high) + (dot(left_high, right_low) + dot(left_low, right_high))


def pick_left(spread, value, dims):
    high, low = halves(value)
    rest = (value - high.astype(F32) - low.astype(F32)).astype(BF16)
    dot = functools.partial(lax.dot_general, spread, dimension_numbers=dims, preferred_element_type=F32)
    return dot(high) + (dot(low) + dot(rest))


def pick_right(value, spread, dims):
    high, low = halves(value)
    rest = (value - high.astype(F32) - low.astype(F32)).astype(BF16)
    dot = functools.partial(lax.dot_general, dimension_numbers=dims, preferred_element_type=F32)
    return dot(high, spread) + (dot(low, spread) + dot(rest, spread))


def swap(value, axis, mask):
    return lax.ppermute(value, axis, [(i, i ^ mask) for i in range(lax.axis_size(axis))])


def across(value, mask):
    return swap(value, "leaf", mask)


def grow(value, mask):
    return jnp.concatenate([value, across(value, mask)], axis=1)


def pair_starts(blocks):
    starts, running = [], 0
    for column in range(blocks):
        starts.append(running)
        running += blocks - 1 - column
    return starts


def placement(rows, offset, count, start, width):
    row = lax.broadcasted_iota(jnp.int32, (rows, width), 0)
    column = lax.broadcasted_iota(jnp.int32, (rows, width), 1)
    inside = (row >= offset) & (row < offset + count)
    return jnp.where(inside & (row - offset == column - start), 1.0, 0.0).astype(BF16)


def forward_kernel(sizes, where, pattern, rhs, inverse, blocks, coupling, sep_rhs, y_out, t_out):
    count, size = inverse.shape[0], inverse.shape[1]
    starts = pair_starts(count)
    pending = [rhs[i * size : (i + 1) * size, :] for i in range(count)]
    for column in range(count):
        solved = mm(inverse[column], pending[column], NN)
        y_out[column * size : (column + 1) * size, :] = solved
        for later in range(column + 1, count):
            pair = starts[column] + later - column - 1
            weight = pattern[0, pair].astype(F32)
            pending[later] = pending[later] - weight * mm(blocks[pair], solved, NN)
    last = y_out[(count - 1) * size :, :]
    right = sep_rhs[...]
    width = coupling.shape[1]
    offset = 0
    for level, rows in enumerate(sizes):
        spread = placement(right.shape[0], offset, rows, where[level], width)
        offset += rows
        t_out[:, level * width : (level + 1) * width] = pick_right(right, spread, TN) - mm(
            last, coupling[level * size : (level + 1) * size, :], TN
        )


def backward_kernel(sizes, where, pattern, y, near, across_core, inverse, blocks, coupling, out, sep_out):
    count, size = inverse.shape[0], inverse.shape[1]
    starts = pair_starts(count)
    width = coupling.shape[1]
    place = where[LEVELS]
    chunks = []
    for member in range(2 * near.shape[0]):
        apart = place ^ member
        chunks.append(jnp.where(apart % 2 == 1, across_core[apart // 2], near[apart // 2]))
    xs = jnp.concatenate(chunks, axis=0)
    correction = jnp.zeros((size, y.shape[1]), F32)
    padded = -(-sep_out.shape[0] // 8) * 8
    pieces = jnp.zeros((padded, y.shape[1]), F32)
    offset = 0
    for level, rows in enumerate(sizes):
        part = xs[:, level * width : (level + 1) * width]
        correction = correction + mm(coupling[level * size : (level + 1) * size, :], part, NT)
        spread = placement(padded, offset, rows, where[level], width)
        pieces = pieces + pick_left(spread, part, NT)
        offset += rows
    sep_out[...] = pieces[: sep_out.shape[0], :]
    pending = [y[i * size : (i + 1) * size, :] for i in range(count)]
    pending[-1] = pending[-1] - correction
    for column in reversed(range(count)):
        solved = mm(inverse[column], pending[column], TN)
        out[column * size : (column + 1) * size, :] = solved
        for earlier in reversed(range(column)):
            pair = starts[earlier] + column - earlier - 1
            weight = pattern[0, pair].astype(F32)
            pending[earlier] = pending[earlier] - weight * mm(blocks[pair], solved, TN)


def spots(start, count, turn=None):
    if turn is None:
        return [slice(start + r * 128, start + (r + 1) * 128) for r in range(count)]
    return [pl.ds(pl.multiple_of(start + (turn ^ r) * 128, 128), 128) for r in range(count)]


def times_rows(value, places, mats, index):
    result = []
    for half in mats:
        total = None
        for r, place in enumerate(places):
            term = mm(value[:, place], half[r, index], NT)
            total = term if total is None else total + term
        result.append(total)
    return result


def times_matrix(value, mats, index, r):
    total = None
    for piece, half in zip(value, mats):
        term = mm(piece, half[r, index], NN)
        total = term if total is None else total + term
    return total


def summed(parts, rows):
    total = None
    for part in parts:
        for start in range(0, part.shape[0], rows):
            term = part[start : start + rows, :]
            total = term if total is None else total + term
    return total


def level_kernel(index, turned, plane, *refs):
    mine, other, z_out, v_out = refs[-4:]
    mats = (mine, other)
    total = summed(refs[:-4], z_out.shape[0])
    places = spots(0, mine.shape[0], plane[0] if turned else None)
    width = z_out.shape[1]
    z_out[...] = total[:, :width]
    v_out[...] = total[:, width:]
    z = times_rows(z_out, places, mats, index)
    z_out[...] = jnp.concatenate(z, axis=1)
    for r, place in enumerate(places):
        v_out[:, place] = v_out[:, place] - times_matrix(z, mats, index + 1, r)


def top_kernel(plane, right, right_far, z1, z2, z3, m1, o1, m2, o2, m3, o3, x_out):
    width = right.shape[1]
    count = m3.shape[0]
    top = (m3, o3)
    z = times_rows(right[...] + right_far[...], spots(0, count), top, 0)
    order = [(z3, top, 1, None), (z2, (m2, o2), 0, None), (z1, (m1, o1), 0, plane[0])]
    mats, index, turn = top, 0, None
    level = 3
    while True:
        for r, place in enumerate(spots(level * width, count, turn)):
            x_out[:, place] = times_matrix(z, mats, index, r)
        if not order:
            break
        held, mats, index, turn = order.pop(0)
        moved = times_rows(x_out, spots(level * width, count, turn), mats, index + 1)
        half = held.shape[1] // 2
        z = [held[:, :half] - moved[0], held[:, half:] - moved[1]]
        level -= 1


SMEM = pl.BlockSpec(memory_space=pltpu.SMEM)
VMEM = pl.BlockSpec(memory_space=pltpu.VMEM)


def params():
    return pltpu.CompilerParams(vmem_limit_bytes=40 * 1024 * 1024)


def call(kernel, outs, *arrays):
    return pl.pallas_call(
        kernel,
        out_shape=[jax.ShapeDtypeStruct(s, F32) for s in outs],
        in_specs=[SMEM if v.dtype == jnp.int32 else VMEM for v in arrays],
        out_specs=[VMEM] * len(outs),
        compiler_params=params(),
    )(*arrays)


def shards(leaf_rhs, leaf_inverse, leaf_blocks, leaf_pattern, leaf_coupling, sep_rhs, sep_inverse, sep_coupling):
    position = lax.axis_index("leaf")
    columns = leaf_rhs.shape[1]
    width = leaf_coupling.shape[1]
    leaves = lax.axis_size("leaf")
    groups = [4, 16, 64, 128]
    sizes = [width // g for g in groups]
    offsets = [sum(sizes[:i]) for i in range(LEVELS)]
    where = jnp.stack([position % g * r for g, r in zip(groups, sizes)] + [position % 4]).astype(jnp.int32)

    def rows(array, level):
        return array[offsets[level] : offsets[level] + sizes[level]]

    def both(level):
        return jnp.stack([rows(sep_inverse, level), rows(sep_coupling, level)])

    def planes(value):
        count = lax.axis_size("col")
        return lax.all_to_all(jnp.broadcast_to(value[None], (count, *value.shape)), "col", 0, 0, tiled=True)

    tie = lax.optimization_barrier
    halves_z, wrap_z, wrap_y = 1 << Z4, (1 << Z8) | (1 << Z4), (1 << Y2) | (1 << Y1)
    near = [[g * 4 + m for m in range(4)] for g in range(leaves // 4)]
    plane = lax.axis_index("col").astype(jnp.int32)[None]

    def turned_planes(value):
        return jnp.stack([value] + [swap(value, "col", r) for r in range(1, lax.axis_size("col"))])

    def solve(index, turned, depth, *arrays):
        outs = [(columns // 4, width), (columns // 4, depth * width)]
        return call(functools.partial(level_kernel, index, turned), outs, plane, *arrays)

    first = grow(both(0), 1 << Z1)
    far = grow(rows(sep_inverse, 3)[None], wrap_y)
    y, t = call(
        functools.partial(forward_kernel, sizes),
        [leaf_rhs.shape, (columns, LEVELS * width)],
        where, leaf_pattern, leaf_rhs, leaf_inverse, leaf_blocks, leaf_coupling, sep_rhs,
    )
    t, first, far = tie((t, first, far))

    t = lax.all_to_all(t, "leaf", 0, 0, axis_index_groups=near, tiled=True)
    first = turned_planes(first)
    far = grow(jnp.concatenate([far, both(2)], 0), 1 << Y1)
    far = grow(far, wrap_z)
    t, first, far = tie((t, first, far))

    first = (first, across(first, CORE_MASK))
    far = grow(jnp.concatenate([far, both(1)], 0), halves_z)
    z1, v = solve(0, True, 3, t, *first)
    v, far = tie((v, far))
    v_far = across(v, 1 << Z2)

    far = grow(far, 1 << Z2)
    v = v + v_far
    v_far = across(v, halves_z)
    far = grow(far, 1 << Z1)
    far, v = tie((far, v))

    second = planes(far[3:])
    third = lax.all_gather(far[:3], "col", axis=0)
    second, v, v_far = tie((second, v, v_far))

    second = (second, across(second, CORE_MASK))
    z2, v = solve(0, False, 2, v, v_far, *second)
    v, third = tie((v, third))

    v = v + across(v, wrap_z)
    third = (third, across(third, CORE_MASK))
    z3, v = solve(1, False, 1, v, across(v, 1 << Y1), *third)
    (x,) = call(
        top_kernel, [(columns // 4, LEVELS * width)], plane, v, across(v, wrap_y), z1, z2, z3, *first, *second, *third
    )
    x = jnp.stack([x, across(x, 1 << Z1)])
    return call(
        functools.partial(backward_kernel, sizes),
        [leaf_rhs.shape, sep_rhs.shape],
        where, leaf_pattern, y, x, across(x, CORE_MASK), leaf_inverse, leaf_blocks, leaf_coupling,
    )


def solution(mesh):
    return jax.shard_map(
        shards,
        mesh=mesh,
        in_specs=(
            P("leaf", "col"),
            P("leaf", None, None),
            P("leaf", None, None),
            P("leaf", None),
            P("leaf", None),
            P("leaf", "col"),
            P("leaf", "col"),
            P("leaf", "col"),
        ),
        out_specs=(P("leaf", "col"), P("leaf", "col")),
        check_vma=False,
    )
```

```python
import functools

import jax
import jax.numpy as jnp
from jax import lax
from jax.experimental import pallas as pl
from jax.experimental.pallas import tpu as pltpu
from jax.sharding import PartitionSpec as P

F32 = jnp.float32
BF16 = jnp.bfloat16
NN = (((1,), (0,)), ((), ()))
NT = (((1,), (1,)), ((), ()))
TN = (((0,), (0,)), ((), ()))
LEVELS = 4
Z1, Z2, Z4, Z8, Y1, Y2 = range(1, 7)
CORE_MASK = 1


def halves(value):
    high = value.astype(BF16)
    low = (value - high.astype(F32)).astype(BF16)
    return high, low


def mm(left, right, dims):
    left_high, left_low = halves(left)
    right_high, right_low = halves(right)
    dot = functools.partial(lax.dot_general, dimension_numbers=dims, preferred_element_type=F32)
    return dot(left_high, right_high) + (dot(left_high, right_low) + dot(left_low, right_high))


def pick_left(spread, value, dims):
    high, low = halves(value)
    rest = (value - high.astype(F32) - low.astype(F32)).astype(BF16)
    dot = functools.partial(lax.dot_general, spread, dimension_numbers=dims, preferred_element_type=F32)
    return dot(high) + (dot(low) + dot(rest))


def pick_right(value, spread, dims):
    high, low = halves(value)
    rest = (value - high.astype(F32) - low.astype(F32)).astype(BF16)
    dot = functools.partial(lax.dot_general, dimension_numbers=dims, preferred_element_type=F32)
    return dot(high, spread) + (dot(low, spread) + dot(rest, spread))


def swap(value, axis, mask):
    return lax.ppermute(value, axis, [(i, i ^ mask) for i in range(lax.axis_size(axis))])


def across(value, mask):
    return swap(value, "leaf", mask)


def grow(value, mask):
    return jnp.concatenate([value, across(value, mask)], axis=1)


def pair_starts(blocks):
    starts, running = [], 0
    for column in range(blocks):
        starts.append(running)
        running += blocks - 1 - column
    return starts


def placement(rows, offset, count, start, width):
    row = lax.broadcasted_iota(jnp.int32, (rows, width), 0)
    column = lax.broadcasted_iota(jnp.int32, (rows, width), 1)
    inside = (row >= offset) & (row < offset + count)
    return jnp.where(inside & (row - offset == column - start), 1.0, 0.0).astype(BF16)


def forward_kernel(
    sizes, where, pattern, rhs_far, inverse_far, blocks_far, coupling_far, sep_rhs, y_out, t_out, rhs, inverse, blocks, coupling, sems
):
    count, size = inverse.shape[0], inverse.shape[1]
    starts = pair_starts(count)
    copies = [
        pltpu.make_async_copy(rhs_far, rhs, sems.at[0]),
        pltpu.make_async_copy(inverse_far, inverse, sems.at[1]),
        pltpu.make_async_copy(coupling_far, coupling, sems.at[2]),
    ]
    for column in range(count - 1):
        part = pl.ds(starts[column], count - 1 - column)
        copies.append(pltpu.make_async_copy(blocks_far.at[part], blocks.at[part], sems.at[3 + column]))
    for copy in copies[:2] + copies[3:] + copies[2:3]:
        copy.start()
    copies[0].wait()
    copies[1].wait()
    pending = [rhs[i * size : (i + 1) * size, :] for i in range(count)]
    for column in range(count):
        solved = mm(inverse[column], pending[column], NN)
        y_out[column * size : (column + 1) * size, :] = solved
        if column < count - 1:
            copies[3 + column].wait()
        for later in range(column + 1, count):
            pair = starts[column] + later - column - 1
            weight = pattern[0, pair].astype(F32)
            pending[later] = pending[later] - weight * mm(blocks[pair], solved, NN)
    last = y_out[(count - 1) * size :, :]
    right = sep_rhs[...]
    width = coupling.shape[1]
    copies[2].wait()
    offset = 0
    for level, rows in enumerate(sizes):
        spread = placement(right.shape[0], offset, rows, where[level], width)
        offset += rows
        t_out[:, level * width : (level + 1) * width] = pick_right(right, spread, TN) - mm(
            last, coupling[level * size : (level + 1) * size, :], TN
        )


def backward_kernel(sizes, where, pattern, y, near, across_core, inverse, blocks, coupling, out, sep_out):
    count, size = inverse.shape[0], inverse.shape[1]
    starts = pair_starts(count)
    width = coupling.shape[1]
    place = where[LEVELS]
    chunks = []
    for member in range(2 * near.shape[0]):
        apart = place ^ member
        chunks.append(jnp.where(apart % 2 == 1, across_core[apart // 2], near[apart // 2]))
    xs = jnp.concatenate(chunks, axis=0)
    correction = jnp.zeros((size, y.shape[1]), F32)
    padded = -(-sep_out.shape[0] // 8) * 8
    pieces = jnp.zeros((padded, y.shape[1]), F32)
    offset = 0
    for level, rows in enumerate(sizes):
        part = xs[:, level * width : (level + 1) * width]
        correction = correction + mm(coupling[level * size : (level + 1) * size, :], part, NT)
        spread = placement(padded, offset, rows, where[level], width)
        pieces = pieces + pick_left(spread, part, NT)
        offset += rows
    sep_out[...] = pieces[: sep_out.shape[0], :]
    pending = [y[i * size : (i + 1) * size, :] for i in range(count)]
    pending[-1] = pending[-1] - correction
    for column in reversed(range(count)):
        solved = mm(inverse[column], pending[column], TN)
        out[column * size : (column + 1) * size, :] = solved
        for earlier in reversed(range(column)):
            pair = starts[earlier] + column - earlier - 1
            weight = pattern[0, pair].astype(F32)
            pending[earlier] = pending[earlier] - weight * mm(blocks[pair], solved, TN)


def spots(start, count, turn=None):
    if turn is None:
        return [slice(start + r * 128, start + (r + 1) * 128) for r in range(count)]
    return [pl.ds(pl.multiple_of(start + (turn ^ r) * 128, 128), 128) for r in range(count)]


def times_rows(value, places, mats, index):
    result = []
    for half in mats:
        total = None
        for r, place in enumerate(places):
            term = mm(value[:, place], half[r, index], NT)
            total = term if total is None else total + term
        result.append(total)
    return result


def times_matrix(value, mats, index, r):
    total = None
    for piece, half in zip(value, mats):
        term = mm(piece, half[r, index], NN)
        total = term if total is None else total + term
    return total


def summed(parts, rows):
    total = None
    for part in parts:
        for start in range(0, part.shape[0], rows):
            term = part[start : start + rows, :]
            total = term if total is None else total + term
    return total


def level_kernel(index, turned, plane, *refs):
    mine, other, z_out, v_out = refs[-4:]
    mats = (mine, other)
    total = summed(refs[:-4], z_out.shape[0])
    places = spots(0, mine.shape[0], plane[0] if turned else None)
    width = z_out.shape[1]
    z_out[...] = total[:, :width]
    v_out[...] = total[:, width:]
    z = times_rows(z_out, places, mats, index)
    z_out[...] = jnp.concatenate(z, axis=1)
    for r, place in enumerate(places):
        v_out[:, place] = v_out[:, place] - times_matrix(z, mats, index + 1, r)


def top_kernel(plane, right, right_far, z1, z2, z3, m1, o1, m2, o2, m3, o3, x_out):
    width = right.shape[1]
    count = m3.shape[0]
    top = (m3, o3)
    z = times_rows(right[...] + right_far[...], spots(0, count), top, 0)
    order = [(z3, top, 1, None), (z2, (m2, o2), 0, None), (z1, (m1, o1), 0, plane[0])]
    mats, index, turn = top, 0, None
    level = 3
    while True:
        for r, place in enumerate(spots(level * width, count, turn)):
            x_out[:, place] = times_matrix(z, mats, index, r)
        if not order:
            break
        held, mats, index, turn = order.pop(0)
        moved = times_rows(x_out, spots(level * width, count, turn), mats, index + 1)
        half = held.shape[1] // 2
        z = [held[:, :half] - moved[0], held[:, half:] - moved[1]]
        level -= 1


SMEM = pl.BlockSpec(memory_space=pltpu.SMEM)
VMEM = pl.BlockSpec(memory_space=pltpu.VMEM)


def params():
    return pltpu.CompilerParams(vmem_limit_bytes=40 * 1024 * 1024)


def call(kernel, outs, *arrays):
    return pl.pallas_call(
        kernel,
        out_shape=[jax.ShapeDtypeStruct(s, F32) for s in outs],
        in_specs=[SMEM if v.dtype == jnp.int32 else VMEM for v in arrays],
        out_specs=[VMEM] * len(outs),
        compiler_params=params(),
    )(*arrays)


def shards(leaf_rhs, leaf_inverse, leaf_blocks, leaf_pattern, leaf_coupling, sep_rhs, sep_inverse, sep_coupling):
    position = lax.axis_index("leaf")
    columns = leaf_rhs.shape[1]
    width = leaf_coupling.shape[1]
    leaves = lax.axis_size("leaf")
    groups = [4, 16, 64, 128]
    sizes = [width // g for g in groups]
    offsets = [sum(sizes[:i]) for i in range(LEVELS)]
    where = jnp.stack([position % g * r for g, r in zip(groups, sizes)] + [position % 4]).astype(jnp.int32)

    def rows(array, level):
        return array[offsets[level] : offsets[level] + sizes[level]]

    def both(level):
        return jnp.stack([rows(sep_inverse, level), rows(sep_coupling, level)])

    def planes(value):
        count = lax.axis_size("col")
        return lax.all_to_all(jnp.broadcast_to(value[None], (count, *value.shape)), "col", 0, 0, tiled=True)

    tie = lax.optimization_barrier
    halves_z, wrap_z, wrap_y = 1 << Z4, (1 << Z8) | (1 << Z4), (1 << Y2) | (1 << Y1)
    near = [[g * 4 + m for m in range(4)] for g in range(leaves // 4)]
    plane = lax.axis_index("col").astype(jnp.int32)[None]

    def turned_planes(value):
        return jnp.stack([value] + [swap(value, "col", r) for r in range(1, lax.axis_size("col"))])

    def solve(index, turned, depth, *arrays):
        outs = [(columns // 4, width), (columns // 4, depth * width)]
        return call(functools.partial(level_kernel, index, turned), outs, plane, *arrays)

    first = grow(both(0), 1 << Z1)
    far = grow(rows(sep_inverse, 3)[None], wrap_y)
    y, t = pl.pallas_call(
        functools.partial(forward_kernel, sizes),
        out_shape=[
            jax.ShapeDtypeStruct(leaf_rhs.shape, F32),
            jax.ShapeDtypeStruct((columns, LEVELS * width), F32),
        ],
        in_specs=[SMEM, SMEM] + [pl.BlockSpec(memory_space=pl.ANY)] * 4 + [VMEM],
        out_specs=[VMEM, VMEM],
        scratch_shapes=[pltpu.VMEM(v.shape, F32) for v in (leaf_rhs, leaf_inverse, leaf_blocks, leaf_coupling)]
        + [pltpu.SemaphoreType.DMA((2 + leaf_inverse.shape[0],))],
        compiler_params=pltpu.CompilerParams(vmem_limit_bytes=58 * 1024 * 1024),
    )(where, leaf_pattern, leaf_rhs, leaf_inverse, leaf_blocks, leaf_coupling, sep_rhs)
    t, first, far = tie((t, first, far))

    t = lax.all_to_all(t, "leaf", 0, 0, axis_index_groups=near, tiled=True)
    first = turned_planes(first)
    far = grow(jnp.concatenate([far, both(2)], 0), 1 << Y1)
    far = grow(far, wrap_z)
    t, first, far = tie((t, first, far))

    first = (first, across(first, CORE_MASK))
    far = grow(jnp.concatenate([far, both(1)], 0), halves_z)
    z1, v = solve(0, True, 3, t, *first)
    v, far = tie((v, far))
    v_far = across(v, 1 << Z2)

    far = grow(far, 1 << Z2)
    v = v + v_far
    v_far = across(v, halves_z)
    far = grow(far, 1 << Z1)
    far, v = tie((far, v))

    second = planes(far[3:])
    third = lax.all_gather(far[:3], "col", axis=0)
    second, v, v_far = tie((second, v, v_far))

    second = (second, across(second, CORE_MASK))
    z2, v = solve(0, False, 2, v, v_far, *second)
    v = v + across(v, wrap_z)
    v, third = tie((v, third))

    third = (third, across(third, CORE_MASK))
    z3, v = solve(1, False, 1, v, across(v, 1 << Y1), *third)
    (x,) = call(
        top_kernel, [(columns // 4, LEVELS * width)], plane, v, across(v, wrap_y), z1, z2, z3, *first, *second, *third
    )
    x = jnp.stack([x, across(x, 1 << Z1)])
    return call(
        functools.partial(backward_kernel, sizes),
        [leaf_rhs.shape, sep_rhs.shape],
        where, leaf_pattern, y, x, across(x, CORE_MASK), leaf_inverse, leaf_blocks, leaf_coupling,
    )


def solution(mesh):
    return jax.shard_map(
        shards,
        mesh=mesh,
        in_specs=(
            P("leaf", "col"),
            P("leaf", None, None),
            P("leaf", None, None),
            P("leaf", None),
            P("leaf", None),
            P("leaf", "col"),
            P("leaf", "col"),
            P("leaf", "col"),
        ),
        out_specs=(P("leaf", "col"), P("leaf", "col")),
        check_vma=False,
    )
```

```python
import functools

import jax
import jax.numpy as jnp
from jax import lax
from jax.experimental import pallas as pl
from jax.experimental.pallas import tpu as pltpu
from jax.sharding import PartitionSpec as P

F32 = jnp.float32
BF16 = jnp.bfloat16
NN = (((1,), (0,)), ((), ()))
NT = (((1,), (1,)), ((), ()))
TN = (((0,), (0,)), ((), ()))
LEVELS = 4
Z1, Z2, Z4, Z8, Y1, Y2 = range(1, 7)
CORE_MASK = 1


def halves(value):
    high = value.astype(BF16)
    low = (value - high.astype(F32)).astype(BF16)
    return high, low


def mm(left, right, dims):
    left_high, left_low = halves(left)
    right_high, right_low = halves(right)
    dot = functools.partial(lax.dot_general, dimension_numbers=dims, preferred_element_type=F32)
    return dot(left_high, right_high) + (dot(left_high, right_low) + dot(left_low, right_high))


def pick_left(spread, value, dims):
    high, low = halves(value)
    rest = (value - high.astype(F32) - low.astype(F32)).astype(BF16)
    dot = functools.partial(lax.dot_general, spread, dimension_numbers=dims, preferred_element_type=F32)
    return dot(high) + (dot(low) + dot(rest))


def pick_right(value, spread, dims):
    high, low = halves(value)
    rest = (value - high.astype(F32) - low.astype(F32)).astype(BF16)
    dot = functools.partial(lax.dot_general, dimension_numbers=dims, preferred_element_type=F32)
    return dot(high, spread) + (dot(low, spread) + dot(rest, spread))


def swap(value, axis, mask):
    return lax.ppermute(value, axis, [(i, i ^ mask) for i in range(lax.axis_size(axis))])


def across(value, mask):
    return swap(value, "leaf", mask)


def grow(value, mask):
    return jnp.concatenate([value, across(value, mask)], axis=1)


def pair_starts(blocks):
    starts, running = [], 0
    for column in range(blocks):
        starts.append(running)
        running += blocks - 1 - column
    return starts


def placement(rows, offset, count, start, width):
    row = lax.broadcasted_iota(jnp.int32, (rows, width), 0)
    column = lax.broadcasted_iota(jnp.int32, (rows, width), 1)
    inside = (row >= offset) & (row < offset + count)
    return jnp.where(inside & (row - offset == column - start), 1.0, 0.0).astype(BF16)


def forward_kernel(
    sizes, where, pattern, rhs_far, inverse_far, blocks_far, coupling_far, sep_rhs, y_out, t_out, rhs, inverse, blocks, coupling, sems
):
    count, size = inverse.shape[0], inverse.shape[1]
    starts = pair_starts(count)
    copies = [
        pltpu.make_async_copy(rhs_far, rhs, sems.at[0]),
        pltpu.make_async_copy(inverse_far, inverse, sems.at[1]),
        pltpu.make_async_copy(coupling_far, coupling, sems.at[2]),
    ]
    for column in range(count - 1):
        part = pl.ds(starts[column], count - 1 - column)
        copies.append(pltpu.make_async_copy(blocks_far.at[part], blocks.at[part], sems.at[3 + column]))
    for copy in copies[:2] + copies[3:] + copies[2:3]:
        copy.start()
    copies[0].wait()
    copies[1].wait()
    pending = [rhs[i * size : (i + 1) * size, :] for i in range(count)]
    for column in range(count):
        solved = mm(inverse[column], pending[column], NN)
        y_out[column * size : (column + 1) * size, :] = solved
        if column < count - 1:
            copies[3 + column].wait()
        for later in range(column + 1, count):
            pair = starts[column] + later - column - 1
            weight = pattern[0, pair].astype(F32)
            pending[later] = pending[later] - weight * mm(blocks[pair], solved, NN)
    last = y_out[(count - 1) * size :, :]
    right = sep_rhs[...]
    width = coupling.shape[1]
    copies[2].wait()
    offset = 0
    for level, rows in enumerate(sizes):
        spread = placement(right.shape[0], offset, rows, where[level], width)
        offset += rows
        t_out[:, level * width : (level + 1) * width] = pick_right(right, spread, TN) - mm(
            last, coupling[level * size : (level + 1) * size, :], TN
        )


def backward_kernel(sizes, where, pattern, y, near, across_core, inverse, blocks, coupling, out, sep_out):
    count, size = inverse.shape[0], inverse.shape[1]
    starts = pair_starts(count)
    width = coupling.shape[1]
    place = where[LEVELS]
    chunks = []
    for member in range(2 * near.shape[0]):
        apart = place ^ member
        chunks.append(jnp.where(apart % 2 == 1, across_core[apart // 2], near[apart // 2]))
    xs = jnp.concatenate(chunks, axis=0)
    correction = jnp.zeros((size, y.shape[1]), F32)
    padded = -(-sep_out.shape[0] // 8) * 8
    pieces = jnp.zeros((padded, y.shape[1]), F32)
    offset = 0
    for level, rows in enumerate(sizes):
        part = xs[:, level * width : (level + 1) * width]
        correction = correction + mm(coupling[level * size : (level + 1) * size, :], part, NT)
        spread = placement(padded, offset, rows, where[level], width)
        pieces = pieces + pick_left(spread, part, NT)
        offset += rows
    sep_out[...] = pieces[: sep_out.shape[0], :]
    pending = [y[i * size : (i + 1) * size, :] for i in range(count)]
    pending[-1] = pending[-1] - correction
    for column in reversed(range(count)):
        solved = mm(inverse[column], pending[column], TN)
        out[column * size : (column + 1) * size, :] = solved
        for earlier in reversed(range(column)):
            pair = starts[earlier] + column - earlier - 1
            weight = pattern[0, pair].astype(F32)
            pending[earlier] = pending[earlier] - weight * mm(blocks[pair], solved, TN)


def spots(start, count, turn=None):
    if turn is None:
        return [slice(start + r * 128, start + (r + 1) * 128) for r in range(count)]
    return [pl.ds(pl.multiple_of(start + (turn ^ r) * 128, 128), 128) for r in range(count)]


def times_rows(value, places, mats, index):
    result = []
    for half in mats:
        total = None
        for r, place in enumerate(places):
            term = mm(value[:, place], half[r, index], NT)
            total = term if total is None else total + term
        result.append(total)
    return result


def times_matrix(value, mats, index, r):
    total = None
    for piece, half in zip(value, mats):
        term = mm(piece, half[r, index], NN)
        total = term if total is None else total + term
    return total


def summed(parts, rows):
    total = None
    for part in parts:
        for start in range(0, part.shape[0], rows):
            term = part[start : start + rows, :]
            total = term if total is None else total + term
    return total


def level_kernel(index, turned, plane, *refs):
    mine, other, z_out, v_out = refs[-4:]
    mats = (mine, other)
    total = summed(refs[:-4], z_out.shape[0])
    places = spots(0, mine.shape[0], plane[0] if turned else None)
    width = z_out.shape[1]
    z_out[...] = total[:, :width]
    v_out[...] = total[:, width:]
    z = times_rows(z_out, places, mats, index)
    z_out[...] = jnp.concatenate(z, axis=1)
    for r, place in enumerate(places):
        v_out[:, place] = v_out[:, place] - times_matrix(z, mats, index + 1, r)


def top_kernel(plane, right, right_far, z1, z2, z3, m1, o1, m2, o2, m3, o3, x_out):
    width = right.shape[1]
    count = m3.shape[0]
    top = (m3, o3)
    z = times_rows(right[...] + right_far[...], spots(0, count), top, 0)
    order = [(z3, top, 1, None), (z2, (m2, o2), 0, None), (z1, (m1, o1), 0, plane[0])]
    mats, index, turn = top, 0, None
    level = 3
    while True:
        for r, place in enumerate(spots(level * width, count, turn)):
            x_out[:, place] = times_matrix(z, mats, index, r)
        if not order:
            break
        held, mats, index, turn = order.pop(0)
        moved = times_rows(x_out, spots(level * width, count, turn), mats, index + 1)
        half = held.shape[1] // 2
        z = [held[:, :half] - moved[0], held[:, half:] - moved[1]]
        level -= 1


SMEM = pl.BlockSpec(memory_space=pltpu.SMEM)
VMEM = pl.BlockSpec(memory_space=pltpu.VMEM)


def params():
    return pltpu.CompilerParams(vmem_limit_bytes=40 * 1024 * 1024)


def call(kernel, outs, *arrays):
    return pl.pallas_call(
        kernel,
        out_shape=[jax.ShapeDtypeStruct(s, F32) for s in outs],
        in_specs=[SMEM if v.dtype == jnp.int32 else VMEM for v in arrays],
        out_specs=[VMEM] * len(outs),
        compiler_params=params(),
    )(*arrays)


def shards(leaf_rhs, leaf_inverse, leaf_blocks, leaf_pattern, leaf_coupling, sep_rhs, sep_inverse, sep_coupling):
    position = lax.axis_index("leaf")
    columns = leaf_rhs.shape[1]
    width = leaf_coupling.shape[1]
    leaves = lax.axis_size("leaf")
    groups = [4, 16, 64, 128]
    sizes = [width // g for g in groups]
    offsets = [sum(sizes[:i]) for i in range(LEVELS)]
    where = jnp.stack([position % g * r for g, r in zip(groups, sizes)] + [position % 4]).astype(jnp.int32)

    def rows(array, level):
        return array[offsets[level] : offsets[level] + sizes[level]]

    def both(level):
        return jnp.stack([rows(sep_inverse, level), rows(sep_coupling, level)])

    def planes(value):
        count = lax.axis_size("col")
        return lax.all_to_all(jnp.broadcast_to(value[None], (count, *value.shape)), "col", 0, 0, tiled=True)

    tie = lax.optimization_barrier
    halves_z, wrap_z, wrap_y = 1 << Z4, (1 << Z8) | (1 << Z4), (1 << Y2) | (1 << Y1)
    near = [[g * 4 + m for m in range(4)] for g in range(leaves // 4)]
    plane = lax.axis_index("col").astype(jnp.int32)[None]

    def turned_planes(value):
        return jnp.stack([value] + [swap(value, "col", r) for r in range(1, lax.axis_size("col"))])

    def solve(index, turned, depth, *arrays):
        outs = [(columns // 4, width), (columns // 4, depth * width)]
        return call(functools.partial(level_kernel, index, turned), outs, plane, *arrays)

    first = grow(both(0), 1 << Z1)
    far = grow(rows(sep_inverse, 3)[None], wrap_y)
    y, t = pl.pallas_call(
        functools.partial(forward_kernel, sizes),
        out_shape=[
            jax.ShapeDtypeStruct(leaf_rhs.shape, F32),
            jax.ShapeDtypeStruct((columns, LEVELS * width), F32),
        ],
        in_specs=[SMEM, SMEM] + [pl.BlockSpec(memory_space=pl.ANY)] * 4 + [VMEM],
        out_specs=[VMEM, VMEM],
        scratch_shapes=[pltpu.VMEM(v.shape, F32) for v in (leaf_rhs, leaf_inverse, leaf_blocks, leaf_coupling)]
        + [pltpu.SemaphoreType.DMA((2 + leaf_inverse.shape[0],))],
        compiler_params=pltpu.CompilerParams(vmem_limit_bytes=58 * 1024 * 1024),
    )(where, leaf_pattern, leaf_rhs, leaf_inverse, leaf_blocks, leaf_coupling, sep_rhs)
    t, first, far = tie((t, first, far))

    t = lax.all_to_all(t, "leaf", 0, 0, axis_index_groups=near, tiled=True)
    first = turned_planes(first)
    far = grow(jnp.concatenate([far, both(2)], 0), 1 << Y1)
    far = grow(far, wrap_z)
    t, first, far = tie((t, first, far))

    first = (first, across(first, CORE_MASK))
    far = grow(jnp.concatenate([far, both(1)], 0), halves_z)
    z1, v = solve(0, True, 3, t, *first)
    v_far = across(v, 1 << Z2)
    v, v_far, far = tie((v, v_far, far))

    v = v + v_far
    v_far = across(v, halves_z)
    far = grow(grow(far, 1 << Z2), 1 << Z1)
    far, v = tie((far, v))

    second = planes(far[3:])
    third = lax.all_gather(far[:3], "col", axis=0)
    second, v, v_far = tie((second, v, v_far))

    second = (second, across(second, CORE_MASK))
    z2, v = solve(0, False, 2, v, v_far, *second)
    v = v + across(v, wrap_z)
    v, third = tie((v, third))

    third = (third, across(third, CORE_MASK))
    z3, v = solve(1, False, 1, v, across(v, 1 << Y1), *third)
    (x,) = call(
        top_kernel, [(columns // 4, LEVELS * width)], plane, v, across(v, wrap_y), z1, z2, z3, *first, *second, *third
    )
    x = jnp.stack([x, across(x, 1 << Z1)])
    return call(
        functools.partial(backward_kernel, sizes),
        [leaf_rhs.shape, sep_rhs.shape],
        where, leaf_pattern, y, x, across(x, CORE_MASK), leaf_inverse, leaf_blocks, leaf_coupling,
    )


def solution(mesh):
    return jax.shard_map(
        shards,
        mesh=mesh,
        in_specs=(
            P("leaf", "col"),
            P("leaf", None, None),
            P("leaf", None, None),
            P("leaf", None),
            P("leaf", None),
            P("leaf", "col"),
            P("leaf", "col"),
            P("leaf", "col"),
        ),
        out_specs=(P("leaf", "col"), P("leaf", "col")),
        check_vma=False,
    )
```

```python
import functools

import jax
import jax.numpy as jnp
from jax import lax
from jax.experimental import pallas as pl
from jax.experimental.pallas import tpu as pltpu
from jax.sharding import PartitionSpec as P

F32 = jnp.float32
BF16 = jnp.bfloat16
NN = (((1,), (0,)), ((), ()))
NT = (((1,), (1,)), ((), ()))
TN = (((0,), (0,)), ((), ()))
LEVELS = 4
Z1, Z2, Z4, Z8, Y1, Y2 = range(1, 7)
CORE_MASK = 1


def halves(value):
    high = value.astype(BF16)
    low = (value - high.astype(F32)).astype(BF16)
    return high, low


def mm(left, right, dims):
    left_high, left_low = halves(left)
    right_high, right_low = halves(right)
    dot = functools.partial(lax.dot_general, dimension_numbers=dims, preferred_element_type=F32)
    return dot(left_high, right_high) + (dot(left_high, right_low) + dot(left_low, right_high))


def pick_left(spread, value, dims):
    high, low = halves(value)
    rest = (value - high.astype(F32) - low.astype(F32)).astype(BF16)
    dot = functools.partial(lax.dot_general, spread, dimension_numbers=dims, preferred_element_type=F32)
    return dot(high) + (dot(low) + dot(rest))


def pick_right(value, spread, dims):
    high, low = halves(value)
    rest = (value - high.astype(F32) - low.astype(F32)).astype(BF16)
    dot = functools.partial(lax.dot_general, dimension_numbers=dims, preferred_element_type=F32)
    return dot(high, spread) + (dot(low, spread) + dot(rest, spread))


def swap(value, axis, mask):
    return lax.ppermute(value, axis, [(i, i ^ mask) for i in range(lax.axis_size(axis))])


def across(value, mask):
    return swap(value, "leaf", mask)


def grow(value, mask):
    return jnp.concatenate([value, across(value, mask)], axis=1)


def pair_starts(blocks):
    starts, running = [], 0
    for column in range(blocks):
        starts.append(running)
        running += blocks - 1 - column
    return starts


def placement(rows, offset, count, start, width):
    row = lax.broadcasted_iota(jnp.int32, (rows, width), 0)
    column = lax.broadcasted_iota(jnp.int32, (rows, width), 1)
    inside = (row >= offset) & (row < offset + count)
    return jnp.where(inside & (row - offset == column - start), 1.0, 0.0).astype(BF16)


def forward_kernel(
    sizes, where, pattern, rhs_far, inverse_far, blocks_far, coupling_far, sep_rhs, sep_inverse, sep_coupling,
    y_out, t_out, second_out, third_out, rhs, inverse, blocks, coupling, sems,
):
    count, size = inverse.shape[0], inverse.shape[1]
    starts = pair_starts(count)
    copies = [
        pltpu.make_async_copy(rhs_far, rhs, sems.at[0]),
        pltpu.make_async_copy(inverse_far, inverse, sems.at[1]),
        pltpu.make_async_copy(coupling_far, coupling, sems.at[2]),
    ]
    for column in range(count - 1):
        part = pl.ds(starts[column], count - 1 - column)
        copies.append(pltpu.make_async_copy(blocks_far.at[part], blocks.at[part], sems.at[3 + column]))
    for copy in copies[:2] + copies[3:] + copies[2:3]:
        copy.start()
    offset = sizes[0]
    for pack in (second_out, third_out):
        for place, source in enumerate((sep_inverse, sep_coupling)):
            pack[place] = source[offset : offset + pack.shape[1], :]
        offset += pack.shape[1]
    copies[0].wait()
    copies[1].wait()
    pending = [rhs[i * size : (i + 1) * size, :] for i in range(count)]
    for column in range(count):
        solved = mm(inverse[column], pending[column], NN)
        y_out[column * size : (column + 1) * size, :] = solved
        if column < count - 1:
            copies[3 + column].wait()
        for later in range(column + 1, count):
            pair = starts[column] + later - column - 1
            weight = pattern[0, pair].astype(F32)
            pending[later] = pending[later] - weight * mm(blocks[pair], solved, NN)
    last = y_out[(count - 1) * size :, :]
    right = sep_rhs[...]
    width = coupling.shape[1]
    copies[2].wait()
    offset = 0
    for level, rows in enumerate(sizes):
        spread = placement(right.shape[0], offset, rows, where[level], width)
        offset += rows
        t_out[:, level * width : (level + 1) * width] = pick_right(right, spread, TN) - mm(
            last, coupling[level * size : (level + 1) * size, :], TN
        )


def backward_kernel(sizes, where, pattern, y, near, across_core, inverse, blocks, coupling, out, sep_out):
    count, size = inverse.shape[0], inverse.shape[1]
    starts = pair_starts(count)
    width = coupling.shape[1]
    place = where[LEVELS]
    chunks = []
    for member in range(2 * near.shape[0]):
        apart = place ^ member
        chunks.append(jnp.where(apart % 2 == 1, across_core[apart // 2], near[apart // 2]))
    xs = jnp.concatenate(chunks, axis=0)
    correction = jnp.zeros((size, y.shape[1]), F32)
    padded = -(-sep_out.shape[0] // 8) * 8
    pieces = jnp.zeros((padded, y.shape[1]), F32)
    offset = 0
    for level, rows in enumerate(sizes):
        part = xs[:, level * width : (level + 1) * width]
        correction = correction + mm(coupling[level * size : (level + 1) * size, :], part, NT)
        spread = placement(padded, offset, rows, where[level], width)
        pieces = pieces + pick_left(spread, part, NT)
        offset += rows
    sep_out[...] = pieces[: sep_out.shape[0], :]
    pending = [y[i * size : (i + 1) * size, :] for i in range(count)]
    pending[-1] = pending[-1] - correction
    for column in reversed(range(count)):
        solved = mm(inverse[column], pending[column], TN)
        out[column * size : (column + 1) * size, :] = solved
        for earlier in reversed(range(column)):
            pair = starts[earlier] + column - earlier - 1
            weight = pattern[0, pair].astype(F32)
            pending[earlier] = pending[earlier] - weight * mm(blocks[pair], solved, TN)


def spots(start, count, turn=None):
    if turn is None:
        return [slice(start + r * 128, start + (r + 1) * 128) for r in range(count)]
    return [pl.ds(pl.multiple_of(start + (turn ^ r) * 128, 128), 128) for r in range(count)]


def times_rows(value, places, mats, index):
    result = []
    for half in mats:
        total = None
        for r, place in enumerate(places):
            term = mm(value[:, place], half[r, index], NT)
            total = term if total is None else total + term
        result.append(total)
    return result


def times_matrix(value, mats, index, r):
    total = None
    for piece, half in zip(value, mats):
        term = mm(piece, half[r, index], NN)
        total = term if total is None else total + term
    return total


def summed(parts, rows):
    total = None
    for part in parts:
        for start in range(0, part.shape[0], rows):
            term = part[start : start + rows, :]
            total = term if total is None else total + term
    return total


def level_kernel(index, turned, plane, *refs):
    mine, other, z_out, v_out = refs[-4:]
    mats = (mine, other)
    total = summed(refs[:-4], z_out.shape[0])
    places = spots(0, mine.shape[0], plane[0] if turned else None)
    width = z_out.shape[1]
    z_out[...] = total[:, :width]
    v_out[...] = total[:, width:]
    z = times_rows(z_out, places, mats, index)
    z_out[...] = jnp.concatenate(z, axis=1)
    for r, place in enumerate(places):
        v_out[:, place] = v_out[:, place] - times_matrix(z, mats, index + 1, r)


def top_kernel(plane, right, right_far, z1, z2, z3, m1, o1, m2, o2, m3, o3, x_out):
    width = right.shape[1]
    count = m3.shape[0]
    top = (m3, o3)
    z = times_rows(right[...] + right_far[...], spots(0, count), top, 0)
    order = [(z3, top, 1, None), (z2, (m2, o2), 0, None), (z1, (m1, o1), 0, plane[0])]
    mats, index, turn = top, 0, None
    level = 3
    while True:
        for r, place in enumerate(spots(level * width, count, turn)):
            x_out[:, place] = times_matrix(z, mats, index, r)
        if not order:
            break
        held, mats, index, turn = order.pop(0)
        moved = times_rows(x_out, spots(level * width, count, turn), mats, index + 1)
        half = held.shape[1] // 2
        z = [held[:, :half] - moved[0], held[:, half:] - moved[1]]
        level -= 1


SMEM = pl.BlockSpec(memory_space=pltpu.SMEM)
VMEM = pl.BlockSpec(memory_space=pltpu.VMEM)


def params():
    return pltpu.CompilerParams(vmem_limit_bytes=20 * 1024 * 1024)


def call(kernel, outs, *arrays):
    return pl.pallas_call(
        kernel,
        out_shape=[jax.ShapeDtypeStruct(s, F32) for s in outs],
        in_specs=[SMEM if v.dtype == jnp.int32 else VMEM for v in arrays],
        out_specs=[VMEM] * len(outs),
        compiler_params=params(),
    )(*arrays)


def shards(leaf_rhs, leaf_inverse, leaf_blocks, leaf_pattern, leaf_coupling, sep_rhs, sep_inverse, sep_coupling):
    position = lax.axis_index("leaf")
    columns = leaf_rhs.shape[1]
    width = leaf_coupling.shape[1]
    leaves = lax.axis_size("leaf")
    groups = [4, 16, 64, 128]
    sizes = [width // g for g in groups]
    offsets = [sum(sizes[:i]) for i in range(LEVELS)]
    where = jnp.stack([position % g * r for g, r in zip(groups, sizes)] + [position % 4]).astype(jnp.int32)

    def rows(array, level):
        return array[offsets[level] : offsets[level] + sizes[level]]

    def both(level):
        return jnp.stack([rows(sep_inverse, level), rows(sep_coupling, level)])

    def planes(value):
        count = lax.axis_size("col")
        return lax.all_to_all(jnp.broadcast_to(value[None], (count, *value.shape)), "col", 0, 0, tiled=True)

    tie = lax.optimization_barrier
    halves_z, wrap_z, wrap_y = 1 << Z4, (1 << Z8) | (1 << Z4), (1 << Y2) | (1 << Y1)
    near = [[g * 4 + m for m in range(4)] for g in range(leaves // 4)]
    plane = lax.axis_index("col").astype(jnp.int32)[None]

    def turned_planes(value):
        return jnp.stack([value] + [swap(value, "col", r) for r in range(1, lax.axis_size("col"))])

    def solve(index, turned, depth, *arrays):
        outs = [(columns // 4, width), (columns // 4, depth * width)]
        return call(functools.partial(level_kernel, index, turned), outs, plane, *arrays)

    first = grow(both(0), 1 << Z1)
    far = grow(rows(sep_inverse, 3)[None], wrap_y)
    y, t, second, third = pl.pallas_call(
        functools.partial(forward_kernel, sizes),
        out_shape=[
            jax.ShapeDtypeStruct(leaf_rhs.shape, F32),
            jax.ShapeDtypeStruct((columns, LEVELS * width), F32),
            jax.ShapeDtypeStruct((2, sizes[1], 128), F32),
            jax.ShapeDtypeStruct((2, sizes[2], 128), F32),
        ],
        in_specs=[SMEM, SMEM] + [pl.BlockSpec(memory_space=pl.ANY)] * 4 + [VMEM] * 3,
        out_specs=[VMEM] * 4,
        scratch_shapes=[pltpu.VMEM(v.shape, F32) for v in (leaf_rhs, leaf_inverse, leaf_blocks, leaf_coupling)]
        + [pltpu.SemaphoreType.DMA((2 + leaf_inverse.shape[0],))],
        compiler_params=pltpu.CompilerParams(vmem_limit_bytes=58 * 1024 * 1024),
    )(where, leaf_pattern, leaf_rhs, leaf_inverse, leaf_blocks, leaf_coupling, sep_rhs, sep_inverse, sep_coupling)
    t, first, far = tie((t, first, far))

    t = lax.all_to_all(t, "leaf", 0, 0, axis_index_groups=near, tiled=True)
    first = turned_planes(first)
    far = grow(jnp.concatenate([far, third], 0), 1 << Y1)
    far = grow(far, wrap_z)
    t, first, far = tie((t, first, far))

    first = (first, across(first, CORE_MASK))
    far = grow(jnp.concatenate([far, second], 0), halves_z)
    z1, v = solve(0, True, 3, t, *first)
    v_far = across(v, 1 << Z2)
    v, v_far, far = tie((v, v_far, far))

    v = v + v_far
    v_far = across(v, halves_z)
    far = grow(grow(far, 1 << Z2), 1 << Z1)
    far, v = tie((far, v))

    second = planes(far[3:])
    third = lax.all_gather(far[:3], "col", axis=0)
    second, v, v_far = tie((second, v, v_far))

    second = (second, across(second, CORE_MASK))
    z2, v = solve(0, False, 2, v, v_far, *second)
    v = v + across(v, wrap_z)
    v, third = tie((v, third))

    third = (third, across(third, CORE_MASK))
    z3, v = solve(1, False, 1, v, across(v, 1 << Y1), *third)
    (x,) = call(
        top_kernel, [(columns // 4, LEVELS * width)], plane, v, across(v, wrap_y), z1, z2, z3, *first, *second, *third
    )
    x = jnp.stack([x, across(x, 1 << Z1)])
    return call(
        functools.partial(backward_kernel, sizes),
        [leaf_rhs.shape, sep_rhs.shape],
        where, leaf_pattern, y, x, across(x, CORE_MASK), leaf_inverse, leaf_blocks, leaf_coupling,
    )


def solution(mesh):
    return jax.shard_map(
        shards,
        mesh=mesh,
        in_specs=(
            P("leaf", "col"),
            P("leaf", None, None),
            P("leaf", None, None),
            P("leaf", None),
            P("leaf", None),
            P("leaf", "col"),
            P("leaf", "col"),
            P("leaf", "col"),
        ),
        out_specs=(P("leaf", "col"), P("leaf", "col")),
        check_vma=False,
    )
```

```python
import functools

import jax
import jax.numpy as jnp
from jax import lax
from jax.experimental import pallas as pl
from jax.experimental.pallas import tpu as pltpu
from jax.sharding import PartitionSpec as P

F32 = jnp.float32
BF16 = jnp.bfloat16
NN = (((1,), (0,)), ((), ()))
NT = (((1,), (1,)), ((), ()))
TN = (((0,), (0,)), ((), ()))
LEVELS = 4
Z1, Z2, Z4, Z8, Y1, Y2 = range(1, 7)
CORE_MASK = 1


def halves(value):
    high = value.astype(BF16)
    low = (value - high.astype(F32)).astype(BF16)
    return high, low


def mm(left, right, dims):
    left_high, left_low = halves(left)
    right_high, right_low = halves(right)
    dot = functools.partial(lax.dot_general, dimension_numbers=dims, preferred_element_type=F32)
    return dot(left_high, right_high) + (dot(left_high, right_low) + dot(left_low, right_high))


def pick_left(spread, value, dims):
    high, low = halves(value)
    rest = (value - high.astype(F32) - low.astype(F32)).astype(BF16)
    dot = functools.partial(lax.dot_general, spread, dimension_numbers=dims, preferred_element_type=F32)
    return dot(high) + (dot(low) + dot(rest))


def pick_right(value, spread, dims):
    high, low = halves(value)
    rest = (value - high.astype(F32) - low.astype(F32)).astype(BF16)
    dot = functools.partial(lax.dot_general, dimension_numbers=dims, preferred_element_type=F32)
    return dot(high, spread) + (dot(low, spread) + dot(rest, spread))


def swap(value, axis, mask):
    return lax.ppermute(value, axis, [(i, i ^ mask) for i in range(lax.axis_size(axis))])


def across(value, mask):
    return swap(value, "leaf", mask)


def grow(value, mask):
    return jnp.concatenate([value, across(value, mask)], axis=1)


def pair_starts(blocks):
    starts, running = [], 0
    for column in range(blocks):
        starts.append(running)
        running += blocks - 1 - column
    return starts


def placement(rows, offset, count, start, width):
    row = lax.broadcasted_iota(jnp.int32, (rows, width), 0)
    column = lax.broadcasted_iota(jnp.int32, (rows, width), 1)
    inside = (row >= offset) & (row < offset + count)
    return jnp.where(inside & (row - offset == column - start), 1.0, 0.0).astype(BF16)


def forward_kernel(
    sizes, where, pattern, rhs_far, inverse_far, blocks_far, coupling_far, sep_rhs, sep_inverse, sep_coupling,
    y_out, t_out, second_out, third_out, rhs, inverse, blocks, coupling, sems,
):
    count, size = inverse.shape[0], inverse.shape[1]
    starts = pair_starts(count)
    copies = [
        pltpu.make_async_copy(rhs_far, rhs, sems.at[0]),
        pltpu.make_async_copy(inverse_far, inverse, sems.at[1]),
        pltpu.make_async_copy(coupling_far, coupling, sems.at[2]),
    ]
    for column in range(count - 1):
        part = pl.ds(starts[column], count - 1 - column)
        copies.append(pltpu.make_async_copy(blocks_far.at[part], blocks.at[part], sems.at[3 + column]))
    for copy in copies[:2] + copies[3:] + copies[2:3]:
        copy.start()
    offset = sizes[0]
    for pack in (second_out, third_out):
        for place, source in enumerate((sep_inverse, sep_coupling)):
            pack[place] = source[offset : offset + pack.shape[1], :]
        offset += pack.shape[1]
    copies[0].wait()
    copies[1].wait()
    pending = [rhs[i * size : (i + 1) * size, :] for i in range(count)]
    for column in range(count):
        solved = mm(inverse[column], pending[column], NN)
        y_out[column * size : (column + 1) * size, :] = solved
        if column < count - 1:
            copies[3 + column].wait()
        for later in range(column + 1, count):
            pair = starts[column] + later - column - 1
            weight = pattern[0, pair].astype(F32)
            pending[later] = pending[later] - weight * mm(blocks[pair], solved, NN)
    last = y_out[(count - 1) * size :, :]
    right = sep_rhs[...]
    width = coupling.shape[1]
    copies[2].wait()
    offset = 0
    for level, rows in enumerate(sizes):
        spread = placement(right.shape[0], offset, rows, where[level], width)
        offset += rows
        t_out[:, level * width : (level + 1) * width] = pick_right(right, spread, TN) - mm(
            last, coupling[level * size : (level + 1) * size, :], TN
        )


def backward_kernel(sizes, where, pattern, y, near, across_core, inverse, blocks, coupling, out, sep_out):
    count, size = inverse.shape[0], inverse.shape[1]
    starts = pair_starts(count)
    width = coupling.shape[1]
    place = where[LEVELS]
    chunks = []
    for member in range(2 * near.shape[0]):
        apart = place ^ member
        chunks.append(jnp.where(apart % 2 == 1, across_core[apart // 2], near[apart // 2]))
    xs = jnp.concatenate(chunks, axis=0)
    correction = jnp.zeros((size, y.shape[1]), F32)
    padded = -(-sep_out.shape[0] // 8) * 8
    pieces = jnp.zeros((padded, y.shape[1]), F32)
    offset = 0
    for level, rows in enumerate(sizes):
        part = xs[:, level * width : (level + 1) * width]
        correction = correction + mm(coupling[level * size : (level + 1) * size, :], part, NT)
        spread = placement(padded, offset, rows, where[level], width)
        pieces = pieces + pick_left(spread, part, NT)
        offset += rows
    sep_out[...] = pieces[: sep_out.shape[0], :]
    pending = [y[i * size : (i + 1) * size, :] for i in range(count)]
    pending[-1] = pending[-1] - correction
    for column in reversed(range(count)):
        solved = mm(inverse[column], pending[column], TN)
        out[column * size : (column + 1) * size, :] = solved
        for earlier in reversed(range(column)):
            pair = starts[earlier] + column - earlier - 1
            weight = pattern[0, pair].astype(F32)
            pending[earlier] = pending[earlier] - weight * mm(blocks[pair], solved, TN)


def spots(start, count, turn=None):
    if turn is None:
        return [slice(start + r * 128, start + (r + 1) * 128) for r in range(count)]
    return [pl.ds(pl.multiple_of(start + (turn ^ r) * 128, 128), 128) for r in range(count)]


def times_rows(value, places, mats, index):
    result = []
    for half in mats:
        total = None
        for r, place in enumerate(places):
            term = mm(value[:, place], half[r, index], NT)
            total = term if total is None else total + term
        result.append(total)
    return result


def times_matrix(value, mats, index, r):
    total = None
    for piece, half in zip(value, mats):
        term = mm(piece, half[r, index], NN)
        total = term if total is None else total + term
    return total


def summed(parts, rows):
    total = None
    for part in parts:
        for start in range(0, part.shape[0], rows):
            term = part[start : start + rows, :]
            total = term if total is None else total + term
    return total


def level_kernel(index, turned, plane, *refs):
    mine, other, z_out, v_out = refs[-4:]
    mats = (mine, other)
    total = summed(refs[:-4], z_out.shape[0])
    places = spots(0, mine.shape[0], plane[0] if turned else None)
    width = z_out.shape[1]
    z_out[...] = total[:, :width]
    v_out[...] = total[:, width:]
    z = times_rows(z_out, places, mats, index)
    z_out[...] = jnp.concatenate(z, axis=1)
    for r, place in enumerate(places):
        v_out[:, place] = v_out[:, place] - times_matrix(z, mats, index + 1, r)


def top_kernel(plane, right, right_far, z1, z2, z3, m1, o1, m2, o2, m3, o3, x_out):
    width = right.shape[1]
    count = m3.shape[0]
    top = (m3, o3)
    z = times_rows(right[...] + right_far[...], spots(0, count), top, 0)
    order = [(z3, top, 1, None), (z2, (m2, o2), 0, None), (z1, (m1, o1), 0, plane[0])]
    mats, index, turn = top, 0, None
    level = 3
    while True:
        for r, place in enumerate(spots(level * width, count, turn)):
            x_out[:, place] = times_matrix(z, mats, index, r)
        if not order:
            break
        held, mats, index, turn = order.pop(0)
        moved = times_rows(x_out, spots(level * width, count, turn), mats, index + 1)
        half = held.shape[1] // 2
        z = [held[:, :half] - moved[0], held[:, half:] - moved[1]]
        level -= 1


SMEM = pl.BlockSpec(memory_space=pltpu.SMEM)
VMEM = pl.BlockSpec(memory_space=pltpu.VMEM)


def params():
    return pltpu.CompilerParams(vmem_limit_bytes=20 * 1024 * 1024)


def call(kernel, outs, *arrays):
    return pl.pallas_call(
        kernel,
        out_shape=[jax.ShapeDtypeStruct(s, F32) for s in outs],
        in_specs=[SMEM if v.dtype == jnp.int32 else VMEM for v in arrays],
        out_specs=[VMEM] * len(outs),
        compiler_params=params(),
    )(*arrays)


def shards(leaf_rhs, leaf_inverse, leaf_blocks, leaf_pattern, leaf_coupling, sep_rhs, sep_inverse, sep_coupling):
    position = lax.axis_index("leaf")
    columns = leaf_rhs.shape[1]
    width = leaf_coupling.shape[1]
    leaves = lax.axis_size("leaf")
    groups = [4, 16, 64, 128]
    sizes = [width // g for g in groups]
    offsets = [sum(sizes[:i]) for i in range(LEVELS)]
    where = jnp.stack([position % g * r for g, r in zip(groups, sizes)] + [position % 4]).astype(jnp.int32)

    def rows(array, level):
        return array[offsets[level] : offsets[level] + sizes[level]]

    def both(level):
        return jnp.stack([rows(sep_inverse, level), rows(sep_coupling, level)])

    def planes(value):
        count = lax.axis_size("col")
        return lax.all_to_all(jnp.broadcast_to(value[None], (count, *value.shape)), "col", 0, 0, tiled=True)

    tie = lax.optimization_barrier
    halves_z, wrap_z, wrap_y = 1 << Z4, (1 << Z8) | (1 << Z4), (1 << Y2) | (1 << Y1)
    near = [[g * 4 + m for m in range(4)] for g in range(leaves // 4)]
    plane = lax.axis_index("col").astype(jnp.int32)[None]

    def turned_planes(value):
        return jnp.stack([value] + [swap(value, "col", r) for r in range(1, lax.axis_size("col"))])

    def solve(index, turned, depth, *arrays):
        outs = [(columns // 4, width), (columns // 4, depth * width)]
        return call(functools.partial(level_kernel, index, turned), outs, plane, *arrays)

    first = grow(both(0), 1 << Z1)
    own = jnp.concatenate([rows(sep_inverse, 2), rows(sep_coupling, 2), rows(sep_inverse, 3)], 0)
    far = (own, across(own, wrap_z))
    y, t, second, third = pl.pallas_call(
        functools.partial(forward_kernel, sizes),
        out_shape=[
            jax.ShapeDtypeStruct(leaf_rhs.shape, F32),
            jax.ShapeDtypeStruct((columns, LEVELS * width), F32),
            jax.ShapeDtypeStruct((2, sizes[1], 128), F32),
            jax.ShapeDtypeStruct((2, sizes[2], 128), F32),
        ],
        in_specs=[SMEM, SMEM] + [pl.BlockSpec(memory_space=pl.ANY)] * 4 + [VMEM] * 3,
        out_specs=[VMEM] * 4,
        scratch_shapes=[pltpu.VMEM(v.shape, F32) for v in (leaf_rhs, leaf_inverse, leaf_blocks, leaf_coupling)]
        + [pltpu.SemaphoreType.DMA((2 + leaf_inverse.shape[0],))],
        compiler_params=pltpu.CompilerParams(vmem_limit_bytes=58 * 1024 * 1024),
    )(where, leaf_pattern, leaf_rhs, leaf_inverse, leaf_blocks, leaf_coupling, sep_rhs, sep_inverse, sep_coupling)
    t, first, far = tie((t, first, far))

    t = lax.all_to_all(t, "leaf", 0, 0, axis_index_groups=near, tiled=True)
    first = turned_planes(first)
    top = jnp.concatenate([part[2 * sizes[2] :] for part in far], 0)[None]
    third = jnp.stack([part[: 2 * sizes[2]].reshape(2, sizes[2], 128) for part in far], 1).reshape(2, -1, 128)
    far = grow(jnp.concatenate([grow(top, wrap_y), third], 0), 1 << Y1)
    t, first, far = tie((t, first, far))

    first = (first, across(first, CORE_MASK))
    far = grow(jnp.concatenate([far, second], 0), halves_z)
    z1, v = solve(0, True, 3, t, *first)
    v_far = across(v, 1 << Z2)
    v, v_far, far = tie((v, v_far, far))

    v = v + v_far
    v_far = across(v, halves_z)
    far = grow(grow(far, 1 << Z2), 1 << Z1)
    far, v = tie((far, v))

    second = planes(far[3:])
    third = lax.all_gather(far[:3], "col", axis=0)
    second, v, v_far = tie((second, v, v_far))

    second = (second, across(second, CORE_MASK))
    z2, v = solve(0, False, 2, v, v_far, *second)
    v = v + across(v, wrap_z)
    v, third = tie((v, third))

    third = (third, across(third, CORE_MASK))
    z3, v = solve(1, False, 1, v, across(v, 1 << Y1), *third)
    (x,) = call(
        top_kernel, [(columns // 4, LEVELS * width)], plane, v, across(v, wrap_y), z1, z2, z3, *first, *second, *third
    )
    x = jnp.stack([x, across(x, 1 << Z1)])
    return call(
        functools.partial(backward_kernel, sizes),
        [leaf_rhs.shape, sep_rhs.shape],
        where, leaf_pattern, y, x, across(x, CORE_MASK), leaf_inverse, leaf_blocks, leaf_coupling,
    )


def solution(mesh):
    return jax.shard_map(
        shards,
        mesh=mesh,
        in_specs=(
            P("leaf", "col"),
            P("leaf", None, None),
            P("leaf", None, None),
            P("leaf", None),
            P("leaf", None),
            P("leaf", "col"),
            P("leaf", "col"),
            P("leaf", "col"),
        ),
        out_specs=(P("leaf", "col"), P("leaf", "col")),
        check_vma=False,
    )
```
